32 devices in a mesh: dp: 8 (over y, x, core), seq: 4 (over z).
Axes of the slice: x: 2, y: 2, z: 4, core: 2. Of those that a mesh axis runs over, the one named last changes fastest.
Arguments:
- tokens: float32 [8, 1024, 1152], P('dp', 'seq'), may hold values from -6 to 6
- cotangent: float32 [8, 1024, 1152], P('dp', 'seq'), may hold values from -6 to 6
- counts: int32 [8, 4], P('dp'), may hold values from 1 to 256, 729 in all within a row
- owner_table: int32 [6], replicated, may hold values from 0 to 7, as said below
- owned_weights: float32 [8, 1152, 4, 1076], P('dp', None, 'seq'), as said below
- owned_moments: float32 [8, 1152, 4, 1076], P('dp', None, 'seq'), as said below
- vectors: float32 [13520], P('seq')
- vector_moments: float32 [2, 13520], P(None, 'seq')
Outputs:
- block_out: float32 [8, 1024, 1152], P('dp', 'seq')
- grad_tokens: float32 [8, 1024, 1152], P('dp', 'seq')
- owned_first: float32 [8, 1152, 4, 1076], P('dp', None, 'seq')
- owned_new: float32 [8, 1152, 4, 1076], P('dp', None, 'seq')
- vector_first: float32 [13520], P('seq')
- vector_second: float32 [13520], P('seq')
- vector_new: float32 [13520], P('seq')
The draws below stay inside these ranges and needn't reach their ends.
Inputs may be any that keep to these rules, and one draw needn't show every extreme that they name: A seq index holds counts[i, s] tokens of image i in its first slots; each row sums to 729 and reaches 256. `owner_table`: six different owners, for query, key, value, output, up and down matrices in that order. `owned_weights`: slot owner_table[m] holds matrix m as in the statement; other entries are zero. `owned_moments`: laid out as owned_weights, zero in the same entries.
All inputs are finite; a program needn't handle non-finite values.
Results may differ from the reference program's by a relative error of at most 0.025.
Values may be sent and summed in bfloat16 or wider, within the bound.
No kernel may reach another device: no remote copies, remote signals or barrier semaphores. Data moves between devices by JAX's collectives and lax.ppermute only.
A program may use at most 256 MiB of HBM per device.

```python
import math
import jax
import jax.numpy as jnp
import numpy as np
from jax import lax

D = 1152
HEADS = 16
FF = 4304
LEN = 729
SLOT_TOTAL = 1024
CAP = 256
IMAGES = 8
NVEC = 13520
NS_ITERS = 5
STEP = 10
N_DP = 8
N_SEQ = 4


def owner_draw(key):
    middle = jax.random.permutation(jax.random.fold_in(key, 101), N_DP - 2)[:4] + 1
    chosen = jnp.concatenate([jnp.array([0, N_DP - 1], jnp.int32), middle.astype(jnp.int32)])
    shuffle = jax.random.permutation(jax.random.fold_in(key, 102), 6)
    return chosen[shuffle]


def place_slots(owners, key, scales):
    slot_width = FF // N_SEQ
    filled = jnp.zeros((N_DP, D, N_SEQ, slot_width), jnp.float32)
    for matrix in range(6):
        columns = (D if matrix < 4 else FF) // N_SEQ
        entries = jax.random.normal(jax.random.fold_in(key, matrix), (D, N_SEQ, columns), jnp.float32)
        entries = jnp.clip(entries, -6.0, 6.0) * scales[matrix]
        entries = jnp.pad(entries, ((0, 0), (0, 0), (0, slot_width - columns)))
        filled = filled.at[owners[matrix]].set(entries)
    return filled


def draw_owner_table(key, part):
    return owner_draw(key)


def draw_owned_weights(key, part):
    owners = owner_draw(key)
    key = jax.random.fold_in(key, 3)
    scales = [D ** (-0.5), D ** (-0.5), D ** (-0.5), (LEN / (32.0 * D)) ** 0.5, D ** (-0.5), FF ** (-0.5)]
    return place_slots(owners, key, scales)


def draw_owned_moments(key, part):
    owners = owner_draw(key)
    key = jax.random.fold_in(key, 5)
    summed = math.sqrt(IMAGES * LEN)
    scales = [summed, summed, 0.5 * summed, math.sqrt(2.7 / LEN) * summed, 0.5 * summed, 0.5 * summed]
    return place_slots(owners, key, scales)


def draw_vectors(key, part):
    key = jax.random.fold_in(key, 7)
    biases = jnp.clip(jax.random.normal(key, (8, D), jnp.float32), -6.0, 6.0) * 0.3
    gains = jax.random.uniform(jax.random.fold_in(key, 1), (8, D), jnp.float32, 0.6, 1.4)
    is_gain = jnp.array([1.0, 0.0, 0.0, 0.0, 0.0, 1.0, 0.0, 0.0], jnp.float32)[:, None]
    row_values = is_gain * gains + (1.0 - is_gain) * biases
    up_bias = jnp.clip(jax.random.normal(jax.random.fold_in(key, 2), (FF,), jnp.float32), -6.0, 6.0) * 0.3
    return jnp.concatenate([row_values.reshape(8 * D), up_bias])


def draw_vector_moments(key, part):
    key = jax.random.fold_in(key, 9)
    summed = math.sqrt(IMAGES * LEN)
    row_scale = jnp.array([2.5, 2.5, 1.0, 0.5, 1.0, 0.6, 0.6, 1.0], jnp.float32)
    scale_all = jnp.concatenate([jnp.repeat(row_scale, D), jnp.full((FF,), 0.5, jnp.float32)]) * summed
    first = jnp.clip(jax.random.normal(key, (NVEC,), jnp.float32), -6.0, 6.0) * 0.11 * scale_all
    factor = jnp.exp(jax.random.uniform(jax.random.fold_in(key, 1), (NVEC,), jnp.float32, math.log(0.5), math.log(2.0)))
    second = 0.002 * scale_all * scale_all * factor
    return jnp.stack([first, second])


def steps_of(rng, extent, split, least, largest):
    def one(position, parts):
        draws = jax.random.uniform(jax.random.fold_in(jax.random.fold_in(rng, 6), position), (parts,), jnp.float32, least / len(split), largest / len(split))
        return jnp.repeat(jnp.exp(draws), extent[position] // parts).reshape((-1,) + (1,) * (len(extent) - position - 1))

    gain = one(*split[0])
    for cut in split[1:]:
        gain = gain * one(*cut)
    return gain


def length_profile(amount, total, reach, skew):
    loads = [(1 << 20) // math.isqrt(rank ** skew) + 1 for rank in range(2, amount + 1)]
    spare, given = total - reach - (amount - 1), [1] * (amount - 1)
    while spare > 0:
        free = [i for i in range(amount - 1) if given[i] < reach]
        mass, budget = sum([loads[i] for i in free]), spare
        for i in free:
            addition = min(reach - given[i], max(1, budget * loads[i] // mass), spare)
            given[i] = given[i] + addition
            spare = spare - addition
    return np.array([reach] + given)


def uneven(rng, amount, total, most, lean):
    if amount == 2:
        one = jax.random.randint(rng, (), max(1, total - most), min(most, total - 1) + 1)
        return jnp.stack([one, total - one])
    sizes = jnp.asarray(length_profile(amount, total, most, lean), jnp.int32)
    twos = (amount - 1) // 2
    giver, taker = sizes[1:1 + 2 * twos:2], sizes[2:2 + 2 * twos:2]
    room = jnp.minimum(giver - 1, most - taker)
    shifted = jax.random.randint(jax.random.fold_in(rng, 1), (twos,), 0, 1 << 20) % (room + 1)
    sizes = sizes.at[1:1 + 2 * twos:2].set(giver - shifted).at[2:2 + 2 * twos:2].set(taker + shifted)
    return sizes[jax.random.permutation(jax.random.fold_in(rng, 2), amount)]


def centred(key, dims, scale, reach, cuts=(), held_as=jnp.bfloat16):
    drawn = scale * jax.random.normal(key, dims, jnp.float32)
    if cuts:
        drawn = drawn * steps_of(key, dims, cuts, -0.22, 0.18)
    return jnp.clip(drawn, -reach, reach).astype(held_as)


def setup_inputs(seed: int = 0) -> dict:
    streams_of = jax.random.split(jax.random.key(seed), 9)
    tokens = centred(streams_of[0], (IMAGES, SLOT_TOTAL, D), 1.0, 6.0, ((0, 8), (1, 4)), jnp.float32)
    cotangent = centred(streams_of[1], (IMAGES, SLOT_TOTAL, D), 1.0, 6.0, ((0, 8), (1, 4)), jnp.float32)
    counts = jax.vmap(lambda own: uneven(own, N_SEQ, LEN, CAP, 2))(jax.random.split(streams_of[2], IMAGES)).reshape((IMAGES, N_SEQ)).astype(jnp.int32)
    owner_table = draw_owner_table(jax.random.fold_in(streams_of[8], 71), 0)
    owned_weights = draw_owned_weights(jax.random.fold_in(streams_of[8], 71), 0)
    owned_moments = draw_owned_moments(jax.random.fold_in(streams_of[8], 71), 0)
    vectors = draw_vectors(jax.random.fold_in(streams_of[8], 71), 0)
    vector_moments = draw_vector_moments(jax.random.fold_in(streams_of[8], 71), 0)
    return dict(tokens=tokens, cotangent=cotangent, counts=counts, owner_table=owner_table, owned_weights=owned_weights, owned_moments=owned_moments, vectors=vectors, vector_moments=vector_moments)


@jax.custom_vjp
def low(v):
    return lax.optimization_barrier(v.astype(jnp.bfloat16)).astype(jnp.float32)

@jax.custom_vjp
def low_back(v):
    return v

def low_keep(v):
    return (low(v), None)

def low_pass(kept, grad):
    return (grad,)

def back_keep(v):
    return (v, None)

def back_low(kept, grad):
    return (low(grad),)
low.defvjp(low_keep, low_pass)
low_back.defvjp(back_keep, back_low)
norm_eps = 1e-06
coef_a = 3.4445
coef_b = -4.775
coef_c = 2.0315
momentum_decay = 0.95
matrix_rate = 0.15
matrix_decay = 0.1
beta_first = 0.9
beta_second = 0.999
vector_rate = 0.5
adam_eps = 1e-08
highest = lax.Precision.HIGHEST

def layer_norm(inputs, gain_row, shift_row):
    average = lax.optimization_barrier(jnp.mean(inputs, axis=-1, keepdims=True))
    centered = inputs - average
    variance = lax.optimization_barrier(jnp.mean(centered * centered, axis=-1, keepdims=True))
    return centered * lax.rsqrt(variance + norm_eps) * gain_row + shift_row

def gelu_tanh(inputs):
    return 0.5 * inputs * (1.0 + jnp.tanh(0.7978845608028654 * (inputs + 0.044715 * inputs * inputs * inputs)))

def encoder_block(weights, vector_values, inputs, key_valid):
    w_query, w_key, w_value, w_out, w_up, w_down = weights
    model_width = inputs.shape[-1]
    head_size = model_width // HEADS
    row_params = vector_values[:8 * model_width].reshape(8, model_width)
    up_bias = vector_values[8 * model_width:]
    images = inputs.shape[0]
    slot_count = inputs.shape[1]
    normed = low(layer_norm(inputs, row_params[0], row_params[1]))
    queries = low(low_back(jnp.einsum('gsd,de->gse', normed, w_query, precision=highest) + row_params[2]))
    key_rows = low(low_back(jnp.einsum('gsd,de->gse', normed, w_key, precision=highest)))
    value_rows = low(low_back(jnp.einsum('gsd,de->gse', normed, w_value, precision=highest) + row_params[3]))
    query_heads = queries.reshape(images, slot_count, HEADS, head_size)
    key_heads = key_rows.reshape(images, slot_count, HEADS, head_size)
    value_heads = value_rows.reshape(images, slot_count, HEADS, head_size)
    scores = jnp.einsum('gqhe,gkhe->ghqk', query_heads, key_heads, precision=highest) * (1.0 / math.sqrt(head_size))
    scores = low_back(scores)
    scores = jnp.where(key_valid[:, None, None, :], scores, -1e+30)
    row_max = lax.optimization_barrier(jnp.max(scores, axis=-1, keepdims=True))
    exponent = jnp.exp(scores - row_max)
    soft_weights = low(exponent / lax.optimization_barrier(jnp.sum(exponent, axis=-1, keepdims=True)))
    context = jnp.einsum('ghqk,gkhe->gqhe', soft_weights, value_heads, precision=highest).reshape(images, slot_count, model_width)
    context = low(low_back(context))
    branch = low_back(jnp.einsum('gsd,de->gse', context, w_out, precision=highest) + row_params[4])
    middle = inputs + branch
    normed_two = low(layer_norm(middle, row_params[5], row_params[6]))
    pre_act = low_back(jnp.einsum('gsd,df->gsf', normed_two, w_up, precision=highest) + up_bias)
    hidden = low(gelu_tanh(pre_act))
    out_branch = low_back(jnp.einsum('gsf,df->gsd', hidden, w_down, precision=highest) + row_params[7])
    return middle + out_branch

def orthogonalize(direction):
    orthogonal = direction / (jnp.sqrt(jnp.sum(direction * direction)) + 1e-07)
    for sweep_index in range(NS_ITERS):
        gram_matrix = jnp.dot(orthogonal, orthogonal.T, precision=highest)
        mixing = coef_b * gram_matrix + coef_c * jnp.dot(gram_matrix, gram_matrix, precision=highest)
        orthogonal = coef_a * orthogonal + jnp.dot(mixing, orthogonal, precision=highest)
    return orthogonal

def to_slab(matrix_value, col_width):
    shaped = matrix_value.reshape(D, N_SEQ, col_width // N_SEQ)
    return jnp.pad(shaped, ((0, 0), (0, 0), (0, FF // N_SEQ - col_width // N_SEQ)))

def reference(tokens, cotangent, counts, owner_table, owned_weights, owned_moments, vectors, vector_moments):
    widths = (D, D, D, D, FF, FF)
    slot_ids = jnp.arange(SLOT_TOTAL, dtype=jnp.int32)
    block_of = (slot_ids // CAP).astype(jnp.int32)
    valid = (slot_ids % CAP)[None, :] < counts[:, block_of]
    valid_mask = valid[:, :, None].astype(jnp.float32)
    matrices = []
    for matrix in range(6):
        col_width = widths[matrix]
        owned_slot = owned_weights[owner_table[matrix]]
        matrices.append(owned_slot[:, :, :col_width // N_SEQ].reshape(D, col_width))
    per_group = math.gcd(IMAGES, 4)
    group_count = IMAGES // per_group

    def forward(inputs, weights, vector_values):
        lowered = tuple((low(weight) for weight in weights))
        low_vectors = low(vector_values)
        shaped = inputs.reshape(group_count, per_group, SLOT_TOTAL, D)
        masks = valid.reshape(group_count, per_group, SLOT_TOTAL)

        def one_group(bundle):
            return encoder_block(lowered, low_vectors, bundle[0], bundle[1])
        results = lax.map(jax.checkpoint(one_group), (shaped, masks))
        return results.reshape(IMAGES, SLOT_TOTAL, D)
    output, pullback = jax.vjp(forward, tokens, tuple(matrices), vectors)
    grad_input, grad_mats, grad_vectors = pullback(cotangent * valid_mask)
    first_slots = jnp.zeros_like(owned_moments)
    new_slots = jnp.zeros_like(owned_weights)
    for matrix in range(6):
        col_width = widths[matrix]
        moment = owned_moments[owner_table[matrix]][:, :, :col_width // N_SEQ].reshape(D, col_width)
        moment_new = momentum_decay * moment + grad_mats[matrix]
        direction = grad_mats[matrix] + momentum_decay * moment_new
        orthogonal = orthogonalize(direction)
        updated = matrices[matrix] * (1.0 - matrix_rate * matrix_decay) - matrix_rate * (0.2 * math.sqrt(max(D, col_width))) * orthogonal
        first_slots = first_slots.at[owner_table[matrix]].set(to_slab(moment_new, col_width))
        new_slots = new_slots.at[owner_table[matrix]].set(to_slab(updated, col_width))
    first_new = beta_first * vector_moments[0] + (1.0 - beta_first) * grad_vectors
    second_new = beta_second * vector_moments[1] + (1.0 - beta_second) * grad_vectors * grad_vectors
    first_fix = 1.0 - beta_first ** STEP
    second_fix = 1.0 - beta_second ** STEP
    vector_new = vectors - vector_rate * (first_new / first_fix) / (jnp.sqrt(second_new / second_fix) + adam_eps)
    return (output * valid_mask, grad_input * valid_mask, first_slots, new_slots, first_new, second_new, vector_new)
```

```python
import functools
import math

import jax
import jax.numpy as jnp
from jax import lax
from jax.experimental import pallas as pl
from jax.experimental.pallas import tpu as pltpu
from jax.sharding import PartitionSpec as P

HEADS = 16
FF = 4304
LEN = 729
NS_ITERS = 5
STEP = 10

norm_eps = 1e-06
coef_a = 3.4445
coef_b = -4.775
coef_c = 2.0315
momentum_decay = 0.95
matrix_rate = 0.15
matrix_decay = 0.1
beta_first = 0.9
beta_second = 0.999
vector_rate = 0.5
adam_eps = 1e-08
low = jnp.bfloat16
f32 = jnp.float32


def call(body, name, **kw):
    vmem = kw.pop("vmem", 48)
    return pl.pallas_call(
        body,
        name=name,
        compiler_params=pltpu.CompilerParams(vmem_limit_bytes=vmem * 1024 * 1024),
        **kw,
    )


def dot(left, right, contract):
    return lax.dot_general(
        left, right, ((tuple(contract[:1]), tuple(contract[1:])), ((), ())), preferred_element_type=f32
    )


def split(x):
    top = x.astype(low)
    return top, (x - top.astype(f32)).astype(low)


def prep_square_body(slab_ref, out_ref):
    rows = slab_ref[:, 0, :]
    extra = out_ref.shape[0] - rows.shape[0]
    out_ref[...] = jnp.concatenate([rows, jnp.zeros((extra, rows.shape[1]), f32)], axis=0)


def prep_body(total, square_ref, slab_ref, out_ref):
    rows = slab_ref[:, 0, :]
    at = pl.program_id(0) * rows.shape[0] + lax.broadcasted_iota(jnp.int32, rows.shape, 0)
    rows = jnp.where(at < total, rows, 0.0)
    out_ref[...] = jnp.concatenate([square_ref[...], rows], axis=0).astype(low)


def prep(slab, heads, head_size, head_pad, parts, square_chunk, wide_chunk):
    total, _, width = slab.shape
    square = call(
        prep_square_body,
        "prep_square",
        grid=(heads,),
        in_specs=[pl.BlockSpec((head_size, 1, width), lambda i: (i, 0, 0))],
        out_specs=pl.BlockSpec((head_pad, width), lambda i: (i, 0)),
        out_shape=jax.ShapeDtypeStruct((parts * square_chunk, width), f32),
    )(slab)
    return call(
        functools.partial(prep_body, total),
        "prep",
        grid=(parts,),
        in_specs=[
            pl.BlockSpec((square_chunk, width), lambda i: (i, 0)),
            pl.BlockSpec((wide_chunk, 1, width), lambda i: (i, 0, 0)),
        ],
        out_specs=pl.BlockSpec((square_chunk + wide_chunk, width), lambda i: (i, 0)),
        out_shape=jax.ShapeDtypeStruct((parts * (square_chunk + wide_chunk), width), low),
    )(square, slab)


def momentum_body(total, moment_ref, grad_ref, first_ref, top_ref, rest_ref):
    grad = grad_ref[...].astype(f32)
    first = momentum_decay * moment_ref[:, 0, :] + grad
    first_ref[...] = first.reshape(first_ref.shape)
    at = pl.program_id(0) * grad.shape[0] + lax.broadcasted_iota(jnp.int32, grad.shape, 0)
    top, rest = split(jnp.where(at < total, grad + momentum_decay * first, 0.0))
    top_ref[...] = top
    rest_ref[...] = rest


def momentum(moments, grad):
    total, _, width = moments.shape
    rows_pad = grad.shape[0]
    block = rows_pad // 4
    slab_spec = pl.BlockSpec((block, 1, width), lambda i: (i, 0, 0))
    flat_spec = pl.BlockSpec((block, width), lambda i: (i, 0))
    return call(
        functools.partial(momentum_body, total),
        "momentum",
        grid=(4,),
        in_specs=[slab_spec, flat_spec],
        out_specs=[slab_spec, flat_spec, flat_spec],
        out_shape=[
            jax.ShapeDtypeStruct(moments.shape, f32),
            jax.ShapeDtypeStruct((rows_pad, width), low),
            jax.ShapeDtypeStruct((rows_pad, width), low),
        ],
    )(moments, grad)


def momentum_again_body(total, moment_ref, grad_ref, *refs):
    momentum_body(total, moment_ref, grad_ref, *refs[3:])


def momentum_again(moments, grad, first, top, rest):
    total, _, width = moments.shape
    rows = grad.shape[0]
    slab_spec = pl.BlockSpec((rows, 1, width), lambda i: (i, 0, 0))
    flat_spec = pl.BlockSpec((rows, width), lambda i: (i, 0))
    return call(
        functools.partial(momentum_again_body, total),
        "momentum_again",
        grid=(1,),
        in_specs=[slab_spec, flat_spec] + [pl.BlockSpec(memory_space=pl.ANY)] * 3,
        out_specs=[slab_spec, flat_spec, flat_spec],
        out_shape=[jax.ShapeDtypeStruct(x.shape, x.dtype) for x in (first, top, rest)],
        input_output_aliases={2: 0, 3: 1, 4: 2},
    )(moments, grad, first, top, rest)


def packed_at(column):
    return 128 * (column * (column + 1) // 2)


def gram_body(start, top_ref, rest_ref, *refs):
    base_ref, out_ref = (refs + refs)[:2] if len(refs) == 2 else (None, refs[0])
    width = top_ref.shape[1]
    depth = pl.ds(start, top_ref.shape[0] - start)
    for j in range(0, width, 256):
        wide = min(256, width - j)
        for i in range(0, j + wide, 256):
            tall = min(256, width - i)
            rows, columns = pl.ds(i, tall), pl.ds(j, wide)
            value = (
                dot(top_ref[depth, rows], top_ref[depth, columns], (0, 0))
                + dot(top_ref[depth, rows], rest_ref[depth, columns], (0, 0))
                + dot(rest_ref[depth, rows], top_ref[depth, columns], (0, 0))
            )
            for c in range(j // 128, (j + wide) // 128):
                used = min(tall, 128 * (c + 1) - i)
                lanes = 128 * c - j
                at = pl.ds(packed_at(c) + i, used)
                piece = value[:used, lanes : lanes + 128]
                out_ref[at, :] = piece if base_ref is None else base_ref[at, :] + piece


def gram_of(top, rest, start, depth, base=None):
    width = top.shape[1]
    count = width // 128
    part = pl.BlockSpec((depth, width), lambda i: (0, 0))
    whole = pl.BlockSpec((packed_at(count), 128), lambda i: (0, 0))
    bases = [] if base is None else [base]
    return call(
        functools.partial(gram_body, start),
        "gram" if base is None else "gram_add",
        grid=(1,),
        in_specs=[part, part] + [whole] * len(bases),
        out_specs=whole,
        out_shape=jax.ShapeDtypeStruct((packed_at(count), 128), f32),
    )(top, rest, *bases)


def iterate_body(
    total,
    rate_ref,
    gram_ref,
    top_hbm,
    rest_hbm,
    slab_hbm,
    out_hbm,
    a_top,
    a_rest,
    b_top,
    t_top,
    t_rest,
    x_ref,
    slab_ref,
    sem,
):
    width = a_top.shape[0]
    rows_pad = x_ref.shape[0]
    fetch_top = pltpu.make_async_copy(top_hbm, b_top.at[pl.ds(0, rows_pad)], sem.at[0])
    fetch_rest = pltpu.make_async_copy(rest_hbm, t_top.at[pl.ds(0, rows_pad)], sem.at[1])
    fetch_slab = pltpu.make_async_copy(slab_hbm, slab_ref.at[pl.ds(0, total)], sem.at[2])
    fetch_top.start()
    fetch_rest.start()
    fetch_slab.start()
    count = width // 128
    diagonal = lax.broadcasted_iota(jnp.int32, (128, 128), 0) == lax.broadcasted_iota(
        jnp.int32, (128, 128), 1
    )
    trace = jnp.zeros((128, 128), f32)
    for c in range(count):
        trace = trace + jnp.where(diagonal, gram_ref[pl.ds(packed_at(c) + 128 * c, 128), :], 0.0)
    scaling = 1.0 / (jnp.sqrt(jnp.sum(trace)) + 1e-07)
    squared = scaling * scaling

    def put(top_ref, rest_ref, i, j, value):
        tall, wide = value.shape
        top, rest = split(value)
        top_ref[pl.ds(i, tall), pl.ds(j, wide)] = top
        rest_ref[pl.ds(i, tall), pl.ds(j, wide)] = rest
        if i != j:
            top, rest = split(value.T)
            top_ref[pl.ds(j, wide), pl.ds(i, tall)] = top
            rest_ref[pl.ds(j, wide), pl.ds(i, tall)] = rest

    for c in range(count):
        for r in range(c + 1):
            put(a_top, a_rest, 128 * r, 128 * c, gram_ref[pl.ds(packed_at(c) + 128 * r, 128), :] * squared)

    step = rows_pad // 4
    fetch_top.wait()
    fetch_rest.wait()

    @pl.loop(0, 4)
    def _(r):
        rows = pl.ds(r * step, step)
        x_ref[rows, :] = (b_top[rows, :].astype(f32) + t_top[rows, :].astype(f32)) * scaling

    def both(top_ref, rest_ref, rows, columns):
        return top_ref[rows, columns].astype(f32) + rest_ref[rows, columns].astype(f32)

    def symmetric(left, rights, finish):
        for j in range(0, width, 256):
            wide = min(256, width - j)
            columns = pl.ds(j, wide)
            for i in range(0, j + wide, 256):
                rows = pl.ds(i, min(256, width - i))
                value = dot(left[rows, :], rights[0][:, columns], (1, 0))
                for right in rights[1:]:
                    value = value + dot(left[rows, :], right[:, columns], (1, 0))
                finish(i, j, rows, columns, value)


    def recenter(center):
        total_mean = jnp.zeros((128, 128), f32)
        for c in range(count):
            at = pl.ds(128 * c, 128)
            total_mean = total_mean + jnp.where(diagonal, both(a_top, a_rest, at, at), 0.0)
        mean = jnp.sum(total_mean) / width
        for c in range(count):
            at = pl.ds(128 * c, 128)
            top, rest = split(both(a_top, a_rest, at, at) - jnp.where(diagonal, mean, 0.0))
            a_top[at, at] = top
            a_rest[at, at] = rest
        return center + mean

    def mix(center):
        def finish(i, j, rows, columns, value):
            value = (coef_b + 2.0 * coef_c * center) * both(
                a_top, a_rest, rows, columns
            ) + coef_c * value
            b_top[rows, columns] = value.astype(low)
            if i != j:
                b_top[columns, rows] = value.T.astype(low)

        symmetric(a_top, (a_top,), finish)
        return coef_a + coef_b * center + coef_c * center * center

    def stepped(rows, lead):
        x = x_ref[rows, :]
        return lead * x + dot(x.astype(low), b_top[...], (1, 0))

    def propagate(center, lead, lefts, rights):
        tall = width // 3

        @pl.loop(0, 3)
        def _(r):
            rows = pl.ds(r * tall, tall)
            value = lead * both(a_top, a_rest, rows, slice(None)) + center * b_top[rows, :].astype(f32)
            for left in lefts:
                value = value + dot(left[rows, :], b_top[...], (1, 0))
            top, rest = split(value)
            t_top[rows, :] = top
            t_rest[rows, :] = rest

        def finish(i, j, rows, columns, value):
            carried = lead * both(t_top, t_rest, rows, columns)
            carried = carried + lead * center * b_top[rows, columns].astype(f32)
            put(a_top, a_rest, i, j, carried + value)

        symmetric(b_top, rights, finish)
        return lead * lead * center

    def sweep(center, lefts, rights):
        center = recenter(center)
        lead = mix(center)

        @pl.loop(0, 4)
        def _(r):
            rows = pl.ds(r * step, step)
            x_ref[rows, :] = stepped(rows, lead)

        return propagate(center, lead, lefts, rights)

    def exact(_, center):
        return sweep(center, (a_top, a_rest), (t_top, t_rest))

    center = lax.fori_loop(0, NS_ITERS - 2, exact, jnp.float32(0.0))
    center = sweep(center, (a_top,), (t_top,))
    lead = mix(recenter(center))
    fetch_slab.wait()
    rate = rate_ref[0]

    @pl.loop(0, 4)
    def _(r):
        rows = pl.ds(r * step, step)
        new = slab_ref[rows, 0, :] * (1.0 - matrix_rate * matrix_decay) - rate * stepped(rows, lead)
        slab_ref[rows, :, :] = new.reshape(step, 1, width)

    leave = pltpu.make_async_copy(slab_ref.at[pl.ds(0, total)], out_hbm, sem.at[3])
    leave.start()
    leave.wait()


def iterate(rate, gram, top, rest, slab):
    total, _, width = slab.shape
    rows_pad = top.shape[0]
    square = pltpu.VMEM((width, width), low)
    flops = 2 * width * width * (15 * width + 5 * rows_pad)
    return call(
        functools.partial(iterate_body, total),
        "iterate",
        vmem=56,
        in_specs=[
            pl.BlockSpec(memory_space=pltpu.SMEM),
            pl.BlockSpec(memory_space=pltpu.VMEM),
            pl.BlockSpec(memory_space=pl.ANY),
            pl.BlockSpec(memory_space=pl.ANY),
            pl.BlockSpec(memory_space=pl.ANY),
        ],
        out_specs=pl.BlockSpec(memory_space=pl.ANY),
        out_shape=jax.ShapeDtypeStruct(slab.shape, f32),
        scratch_shapes=[square] * 5
        + [
            pltpu.VMEM((rows_pad, width), f32),
            pltpu.VMEM((rows_pad, 1, width), f32),
            pltpu.SemaphoreType.DMA((4,)),
        ],
        cost_estimate=pl.CostEstimate(flops=flops, bytes_accessed=20_000_000, transcendentals=0),
    )(rate, gram, top, rest, slab)


def attend_body(scale, qkv_ref, context_ref, soft_ref):
    query, key, value = qkv_ref[0, 0], qkv_ref[1, 0], qkv_ref[2, 0]
    scores = dot(key, query, (0, 0)) * scale
    at = lax.broadcasted_iota(jnp.int32, scores.shape, 0)
    scores = jnp.where(at < LEN, scores, -1e30)
    exponent = jnp.exp(scores - jnp.max(scores, axis=0, keepdims=True))
    soft = (exponent / jnp.sum(exponent, axis=0, keepdims=True)).astype(low)
    soft_ref[0] = soft
    context = dot(value, soft, (1, 0))
    context_ref[0] = context[: context_ref.shape[1]].astype(low)


def attend(qkv, head_size, scale):
    _, groups, head_pad, rows = qkv.shape
    return call(
        functools.partial(attend_body, scale),
        "attend",
        grid=(groups,),
        in_specs=[pl.BlockSpec((3, 1, head_pad, rows), lambda h: (0, h, 0, 0))],
        out_specs=[
            pl.BlockSpec((1, head_size, rows), lambda h: (h, 0, 0)),
            pl.BlockSpec((1, rows, rows), lambda h: (h, 0, 0)),
        ],
        out_shape=[
            jax.ShapeDtypeStruct((groups, head_size, rows), low),
            jax.ShapeDtypeStruct((groups, rows, rows), low),
        ],
    )(qkv)


def attend_back_body(scale, qkv_ref, soft_ref, grad_ref, out_ref):
    query, key, value = qkv_ref[0, 0], qkv_ref[1, 0], qkv_ref[2, 0]
    grad, soft = grad_ref[0], soft_ref[0]
    grad_soft = dot(value, grad, (0, 0))
    soft_f32 = soft.astype(f32)
    along = jnp.sum(soft_f32 * grad_soft, axis=0, keepdims=True)
    grad_scores = (soft_f32 * (grad_soft - along)).astype(low)
    out_ref[0, 0] = (dot(key, grad_scores, (1, 0)) * scale).astype(low)
    out_ref[1, 0] = (dot(query, grad_scores, (1, 1)) * scale).astype(low)
    out_ref[2, 0] = dot(grad, soft, (1, 1)).astype(low)


def attend_back(qkv, soft, grad, scale):
    _, groups, head_pad, rows = qkv.shape
    three = pl.BlockSpec((3, 1, head_pad, rows), lambda h: (0, h, 0, 0))
    return call(
        functools.partial(attend_back_body, scale),
        "attend_back",
        grid=(groups,),
        in_specs=[
            three,
            pl.BlockSpec((1, rows, rows), lambda h: (h, 0, 0)),
            pl.BlockSpec((1, head_pad, rows), lambda h: (h, 0, 0)),
        ],
        out_specs=three,
        out_shape=jax.ShapeDtypeStruct(qkv.shape, low),
    )(qkv, soft, grad)


def whiten(inputs):
    average = jnp.mean(inputs, axis=-1, keepdims=True)
    centered = inputs - average
    variance = jnp.mean(centered * centered, axis=-1, keepdims=True)
    inverse = lax.rsqrt(variance + norm_eps)
    return centered * inverse, inverse


def whiten_back(grad, gain_row, hat, inverse):
    scaled = grad * gain_row
    mean_one = jnp.mean(scaled, axis=-1, keepdims=True)
    mean_two = jnp.mean(scaled * hat, axis=-1, keepdims=True)
    return inverse * (scaled - mean_one - hat * mean_two)


def gelu_both(inputs):
    squared = inputs * inputs
    curve = jnp.tanh(0.7978845608028654 * (inputs + 0.044715 * inputs * squared))
    value = 0.5 * inputs * (1.0 + curve)
    slope = 0.5 * (1.0 + curve) + 0.5 * inputs * (1.0 - curve * curve) * 0.7978845608028654 * (
        1.0 + 3.0 * 0.044715 * squared
    )
    return value, slope


def product(form, left, right):
    return jnp.einsum(form, left, right, preferred_element_type=f32)


def flip(x, axis, mask):
    count = lax.axis_size(axis)
    return lax.ppermute(x, axis, [(i, i ^ mask) for i in range(count)])


def gather_chunks(pieces):
    count = lax.axis_size("dp")
    half = count // 2
    me = lax.axis_index("dp")
    pair, core = me >> 1, me & 1
    joined = jnp.concatenate(pieces, axis=0) if len(pieces) > 1 else pieces[0]
    arrived = [joined] + [flip(joined, "dp", mask << 1) for mask in range(1, half)]
    result, at = [], 0
    for piece in pieces:
        whole = jnp.zeros((half, 2) + piece.shape, piece.dtype)
        for mask in range(half):
            part = arrived[mask][at : at + piece.shape[0]]
            whole = lax.dynamic_update_slice(whole, part[None, None], (pair ^ mask, core, 0, 0))
        mine = lax.dynamic_slice_in_dim(whole, core, 1, 1)
        other = flip(mine, "dp", 1)
        whole = lax.dynamic_update_slice_in_dim(whole, other, 1 - core, 1)
        result.append(whole.reshape((count,) + piece.shape))
        at += piece.shape[0]
    return result


def scatter_sum(whole, order):
    count, rows, columns = whole.shape
    bits = count.bit_length() - 1
    me = lax.axis_index("dp")
    whole = whole.reshape((2,) * bits + (rows, columns))
    for bit in order:
        at = bits - 1 - bit
        mine = (me >> bit) & 1
        kept = lax.dynamic_slice_in_dim(whole, mine, 1, at)
        sent = lax.dynamic_slice_in_dim(whole, 1 - mine, 1, at)
        got = flip(sent, "dp", 1 << bit)
        whole = (kept.astype(f32) + got.astype(f32)).astype(low)
    return whole.reshape(rows, columns)


def gather_seq(piece):
    count = lax.axis_size("seq")
    me = lax.axis_index("seq")
    whole = jnp.zeros((count,) + piece.shape, piece.dtype)
    whole = lax.dynamic_update_slice_in_dim(whole, piece[None], me, 0)
    for shift in range(1, count):
        got = lax.ppermute(piece, "seq", [(i, (i + shift) % count) for i in range(count)])
        whole = lax.dynamic_update_slice_in_dim(whole, got[None], (me - shift) % count, 0)
    return whole


def total_sum(x):
    for axis in ("dp", "seq"):
        step = 1
        while step < lax.axis_size(axis):
            x = x + flip(x, axis, step)
            step *= 2
    return x


def after(x, token):
    return x + jnp.minimum(jnp.abs(token), 0.0).astype(x.dtype)


def local(
    tokens, cotangent, counts, owner_table, owned_weights, owned_moments, vectors, vector_moments
):
    seq_count = lax.axis_size("seq")
    dp_count = lax.axis_size("dp")
    bits = dp_count.bit_length() - 1
    seq_index = lax.axis_index("seq")
    dp_index = lax.axis_index("dp")
    capacity = tokens.shape[1]
    width = tokens.shape[2]
    slots = capacity * seq_count
    head_size = width // HEADS
    head_pad = -(-head_size // 16) * 16
    heads = HEADS // seq_count
    score_scale = 1.0 / math.sqrt(head_size)
    widths = (width, width, width, width, FF, FF)
    cols = width // seq_count
    ff_cols = FF // seq_count
    share = -(-LEN // (16 * seq_count)) * 16
    packed = share * seq_count
    square_rows = heads * head_pad
    square_chunk = -(-square_rows // (8 * dp_count)) * 8
    square_total = square_chunk * dp_count
    sent_chunk = -(-(-(-ff_cols // dp_count) + square_chunk) // 16) * 16
    wide_chunk = sent_chunk - square_chunk
    wide_rows = wide_chunk * dp_count
    orders = (tuple(range(bits)), (0,) + tuple(range(bits - 1, 0, -1)))

    rows_in = tokens[0]
    vector_count = vectors.shape[0]
    vector_rows = -(-vector_count // width)
    extra = -(-vector_rows // 16) * 16
    payload = jnp.pad(vectors, (0, extra * width - vector_count)).reshape(extra, width)
    payload = jnp.concatenate([rows_in.astype(low), payload.astype(low)], axis=0)
    gathered = lax.all_gather(payload, "seq", axis=0, tiled=False)
    token_slots = gathered.reshape(seq_count * (capacity + extra), width)

    counts_row = counts[0]
    starts = jnp.cumsum(counts_row) - counts_row

    def rows_of(per):
        ids = jnp.arange(per * seq_count)
        real = (ids % per) < jnp.repeat(counts_row, per)
        return jnp.where(real, jnp.repeat(starts, per) + ids % per, packed)

    def picks(row):
        return (jnp.arange(packed)[:, None] == row[None, :]).astype(low)

    slot_row = rows_of(capacity)
    pick = picks(slot_row)
    token_pick = picks(rows_of(capacity + extra))
    own_row = lax.dynamic_slice_in_dim(slot_row, seq_index * capacity, capacity)
    own_pick = picks(own_row)
    own_valid = (own_row < packed)[:, None].astype(f32)
    cot_own = after((cotangent[0] * own_valid).astype(low), token_slots[0, 0])
    cot_slots = gather_seq(cot_own).reshape(slots, width)

    slab = jnp.transpose(owned_weights[0], (2, 1, 0))
    moments = jnp.transpose(owned_moments[0], (2, 1, 0))

    def send(x):
        return lax.all_to_all(x, "dp", split_axis=0, concat_axis=0, tiled=True)

    sent = prep(slab, heads, head_size, head_pad, dp_count, square_chunk, wide_chunk)
    got = send(sent.reshape(dp_count, sent_chunk, width))
    chunks = [lax.dynamic_index_in_dim(got, owner_table[m], 0, keepdims=False) for m in range(6)]
    squares = [chunk[:square_chunk] for chunk in chunks[:4]]
    (w_qkv,) = gather_chunks([jnp.concatenate(squares[:3], axis=0)])
    w_qkv = w_qkv.reshape(dp_count, 3, square_chunk, width).transpose(1, 0, 2, 3)
    w_qkv = w_qkv.reshape(3, square_total, width)[:, :square_rows].reshape(3 * square_rows, width)
    w_out_part = gather_seq(squares[3]).reshape(seq_count * square_chunk, width)
    w_out_part = after(w_out_part, w_qkv[0, 0])
    w_out, w_up, w_down = gather_chunks(
        [w_out_part, chunks[4][square_chunk:], chunks[5][square_chunk:]]
    )
    w_up = w_up.reshape(wide_rows, width)
    w_down = w_down.reshape(wide_rows, width)
    w_out = w_out.reshape(dp_count, seq_count, square_chunk, width).transpose(1, 0, 2, 3)
    w_out = w_out.reshape(seq_count, square_total, width)[:, :square_rows]
    w_out = w_out.reshape(seq_count * heads, head_pad, width)[:, :head_size].reshape(width, width)
    w_out_own = lax.dynamic_slice_in_dim(w_out, seq_index * cols, cols, axis=1)
    w_out_own = jnp.pad(
        w_out_own.reshape(width, heads, head_size), ((0, 0), (0, 0), (0, head_pad - head_size))
    ).reshape(width, square_rows)

    vector_full = gathered[:, capacity : capacity + vector_rows].reshape(seq_count, -1)
    vector_full = vector_full[:, :vector_count].reshape(-1).astype(f32)
    row_params = vector_full[: 8 * width].reshape(8, width)
    up_bias = lax.dynamic_slice_in_dim(vector_full, 8 * width + seq_index * ff_cols, ff_cols)
    up_bias = jnp.pad(up_bias, (0, wide_rows - ff_cols))

    def head_bias(row):
        own = lax.dynamic_slice_in_dim(row, seq_index * cols, cols).reshape(heads, head_size)
        return jnp.pad(own, ((0, 0), (0, head_pad - head_size))).reshape(square_rows)

    qkv_bias = jnp.concatenate(
        [head_bias(row_params[2]), jnp.zeros((square_rows,), f32), head_bias(row_params[3])]
    )

    token_rows = product("rc,cd->rd", token_pick, token_slots)
    normed = (whiten(token_rows)[0] * row_params[0] + row_params[1]).astype(low)
    qkv = (product("ed,rd->er", w_qkv, normed) + qkv_bias[:, None]).astype(low)
    qkv = qkv.reshape(3, heads, head_pad, packed)
    context_own, soft = attend(qkv, head_size, score_scale)
    context = lax.all_gather(context_own.reshape(cols, packed), "seq", axis=0, tiled=True)
    grad_rows = product("rc,cd->rd", pick, cot_slots).astype(low)
    middle = token_rows + product("er,oe->ro", context, w_out) + after(row_params[4], grad_rows[0, 0])
    hat_two, inverse_two = whiten(middle)
    normed_two = (hat_two * row_params[5] + row_params[6]).astype(low)
    pre_act = product("rd,fd->rf", normed_two, w_up) + up_bias
    hidden_f32, slope = gelu_both(pre_act)
    hidden = hidden_f32.astype(low)

    grad_hidden = product("rd,fd->rf", grad_rows, w_down)
    grad_pre = (slope * grad_hidden).astype(low)
    grad_normed_two_part = product("rf,fd->rd", grad_pre, w_up).astype(low)
    token = grad_normed_two_part[0, 0]
    hidden_late = after(hidden, token)
    grad_pre_late = after(grad_pre, token)
    grad_down = product("rf,rd->fd", hidden_late, grad_rows)
    grad_up = product("rf,rd->fd", grad_pre_late, normed_two)
    grad_up_bias = jnp.sum(grad_pre_late.astype(f32), axis=0)[:ff_cols]

    def parts(x, rows):
        return x.astype(low).reshape(dp_count, rows, width)

    sum_down = scatter_sum(parts(grad_down, wide_chunk), orders[0])
    sum_up = scatter_sum(parts(grad_up, wide_chunk), orders[1])
    grad_normed_two = after(
        lax.psum_scatter(grad_normed_two_part, "seq", scatter_dimension=0, tiled=True),
        sum_down[0, 0] + sum_up[0, 0],
    ).astype(f32)

    def to_owner(pairs):
        total = 0
        for piece, m in pairs:
            here = (jnp.arange(dp_count) == owner_table[m])[:, None, None]
            total = total + jnp.where(here, piece[None], jnp.zeros((), low))
        return total

    back_wide = send(to_owner([(sum_up, 4), (sum_down, 5)])).reshape(wide_rows, width)
    first_moment, top, rest = momentum(moments, back_wide)
    early_gram = gram_of(top, rest, cols, wide_rows)

    def own_share(x):
        return lax.dynamic_slice_in_dim(x, seq_index * share, share)

    own_grad = own_share(grad_rows).astype(f32)
    own_hat = own_share(hat_two)
    grad_bias_down = jnp.sum(own_grad, axis=0)
    grad_gain_two = jnp.sum(grad_normed_two * own_hat, axis=0)
    grad_shift_two = jnp.sum(grad_normed_two, axis=0)
    grad_mid_norm = whiten_back(grad_normed_two, row_params[5], own_hat, own_share(inverse_two))
    grad_attn_own = (own_grad + grad_mid_norm).astype(low)
    grad_bias_out = jnp.sum(grad_attn_own.astype(f32), axis=0)
    grad_attn = lax.all_gather(grad_attn_own, "seq", axis=0, tiled=True)

    grad_context = product("de,rd->er", w_out_own, grad_attn).astype(low)
    grad_qkv = attend_back(qkv, soft, grad_context.reshape(heads, head_pad, packed), score_scale)
    grad_qkv_flat = grad_qkv.reshape(3 * square_rows, packed)
    grad_attn_cols = lax.dynamic_slice_in_dim(grad_attn, seq_index * cols, cols, axis=1)
    grad_w_out = product("rd,er->de", grad_attn_cols, context)
    grad_w_qkv = product("er,rd->ed", grad_qkv_flat, normed)
    grad_qkv_bias = jnp.sum(grad_qkv.astype(f32), axis=3)[:, :, :head_size].reshape(3, cols)

    grad_normed_part = product("er,ed->rd", grad_qkv_flat, w_qkv) + jnp.minimum(
        jnp.abs(grad_w_qkv[0, 0] + grad_w_out[0, 0]), 0.0
    )
    unpick = (slot_row[:, None] == jnp.arange(packed)[None, :]).astype(low)
    grad_normed_slots = product("cr,rd->cd", unpick, grad_normed_part.astype(low)).astype(low)
    grad_normed = lax.psum_scatter(
        grad_normed_slots, "seq", scatter_dimension=0, tiled=True
    ).astype(f32)

    def square_parts(x):
        x = jnp.pad(x.astype(low), ((0, square_total - square_rows), (0, 0)))
        return x.reshape(dp_count, square_chunk, width)

    late = [square_parts(grad_w_qkv[m * square_rows : (m + 1) * square_rows]) for m in range(3)]
    grad_w_out = jnp.pad(
        grad_w_out.reshape(heads, head_size, width), ((0, 0), (0, head_pad - head_size), (0, 0))
    )
    late.append(square_parts(grad_w_out.reshape(square_rows, width)))
    token = back_wide[0, 0]
    sum_qk = scatter_sum(after(jnp.concatenate(late[:2], axis=1), token), orders[0])
    sum_vo = scatter_sum(after(jnp.concatenate(late[2:], axis=1), token), orders[1])
    back_square = send(
        to_owner(
            [
                (sum_qk[:square_chunk], 0),
                (sum_qk[square_chunk:], 1),
                (sum_vo[:square_chunk], 2),
                (sum_vo[square_chunk:], 3),
            ]
        )
    ).reshape(square_total, width)[:square_rows]
    back_square = back_square.reshape(heads, head_pad, width)[:, :head_size].reshape(cols, width)
    first_moment, top, rest = momentum_again(
        moments, back_wide[:cols] + back_square, first_moment, top, rest
    )
    partial_gram = gram_of(top, rest, 0, cols, early_gram)
    partial_gram = after(partial_gram, grad_normed[0, 0])
    gram_share = lax.psum_scatter(partial_gram, "seq", scatter_dimension=0, tiled=True)
    first_gram = lax.all_gather(gram_share, "seq", axis=0, tiled=True)
    token = first_gram[0, 0]
    update_scale = jnp.zeros((), f32)
    for m in range(6):
        update_scale = jnp.where(
            owner_table[m] == dp_index,
            jnp.float32(matrix_rate * 0.2 * math.sqrt(max(width, widths[m]))),
            update_scale,
        )
    updated = iterate(update_scale.reshape(1), first_gram, top, rest, slab)

    placed_middle = jnp.where(
        (jnp.arange(packed) // share == seq_index)[:, None], middle + row_params[7], 0.0
    )
    out_part = (product("rf,fd->rd", hidden, w_down) + placed_middle).astype(low)
    out_slots = after(product("cr,rd->cd", unpick, out_part).astype(low), token)
    block_out = lax.psum_scatter(out_slots, "seq", scatter_dimension=0, tiled=True).astype(f32)
    hat_one, inverse_one = whiten(rows_in)
    grad_gain_one = jnp.sum(grad_normed * hat_one, axis=0)
    grad_shift_one = jnp.sum(grad_normed, axis=0)
    grad_in_norm = whiten_back(grad_normed, row_params[0], hat_one, inverse_one)
    grad_mid_slots = product("rc,rd->cd", own_pick, grad_attn)
    grad_tokens = (grad_mid_slots + grad_in_norm) * own_valid

    def spot(piece):
        return lax.dynamic_update_slice_in_dim(
            jnp.zeros((piece.shape[0] * seq_count,), f32), piece, seq_index * piece.shape[0], 0
        )

    vector_grad = jnp.concatenate(
        [
            grad_gain_one,
            grad_shift_one,
            spot(grad_qkv_bias[0]),
            spot(grad_qkv_bias[2]),
            grad_bias_out,
            grad_gain_two,
            grad_shift_two,
            grad_bias_down,
            spot(grad_up_bias),
        ]
    )
    padded = -(-vector_grad.shape[0] // 1024) * 1024
    vector_grad = jnp.pad(vector_grad, (0, padded - vector_grad.shape[0])).reshape(-1, 128)
    vector_sum = total_sum(vector_grad).reshape(-1)
    vector_total = lax.dynamic_slice_in_dim(vector_sum, seq_index * vector_count, vector_count)

    first_new = beta_first * vector_moments[0] + (1.0 - beta_first) * vector_total
    second_new = beta_second * vector_moments[1] + (1.0 - beta_second) * vector_total * vector_total
    first_fix = 1.0 - beta_first**STEP
    second_fix = 1.0 - beta_second**STEP
    vector_new = vectors - vector_rate * (first_new / first_fix) / (
        jnp.sqrt(second_new / second_fix) + adam_eps
    )
    return (
        block_out[None],
        grad_tokens[None],
        jnp.transpose(first_moment, (2, 1, 0))[None],
        jnp.transpose(updated, (2, 1, 0))[None],
        first_new,
        second_new,
        vector_new,
    )


def solution(mesh):
    in_specs = (
        P("dp", "seq", None),
        P("dp", "seq", None),
        P("dp", None),
        P(),
        P("dp", None, "seq", None),
        P("dp", None, "seq", None),
        P("seq"),
        P(None, "seq"),
    )
    out_specs = (
        P("dp", "seq", None),
        P("dp", "seq", None),
        P("dp", None, "seq", None),
        P("dp", None, "seq", None),
        P("seq"),
        P("seq"),
        P("seq"),
    )
    return jax.shard_map(local, mesh=mesh, in_specs=in_specs, out_specs=out_specs, check_vma=False)
```

```python
import functools
import math

import jax
import jax.numpy as jnp
from jax import lax
from jax.experimental import pallas as pl
from jax.experimental.pallas import tpu as pltpu
from jax.sharding import PartitionSpec as P

HEADS = 16
FF = 4304
LEN = 729
NS_ITERS = 5
STEP = 10

norm_eps = 1e-06
coef_a = 3.4445
coef_b = -4.775
coef_c = 2.0315
momentum_decay = 0.95
matrix_rate = 0.15
matrix_decay = 0.1
beta_first = 0.9
beta_second = 0.999
vector_rate = 0.5
adam_eps = 1e-08
low = jnp.bfloat16
f32 = jnp.float32


def call(body, name, **kw):
    vmem = kw.pop("vmem", 48)
    return pl.pallas_call(
        body,
        name=name,
        compiler_params=pltpu.CompilerParams(vmem_limit_bytes=vmem * 1024 * 1024),
        **kw,
    )


def dot(left, right, contract):
    return lax.dot_general(
        left, right, ((tuple(contract[:1]), tuple(contract[1:])), ((), ())), preferred_element_type=f32
    )


def split(x):
    top = x.astype(low)
    return top, (x - top.astype(f32)).astype(low)


def prep_square_body(slab_ref, first_ref, out_ref):
    rows = slab_ref[:, 0, :]
    extra = out_ref.shape[0] - rows.shape[0]
    padded = jnp.concatenate([rows, jnp.zeros((extra, rows.shape[1]), f32)], axis=0)
    out_ref[...] = padded.astype(low)


def prep_square(slab, first, heads, head_size, head_pad):
    width = slab.shape[2]
    return call(
        prep_square_body,
        "prep_square",
        grid=(heads,),
        in_specs=[
            pl.BlockSpec((head_size, 1, width), lambda i: (i, 0, 0)),
            pl.BlockSpec(memory_space=pl.ANY),
        ],
        out_specs=pl.BlockSpec((head_pad, width), lambda i: (i, 0)),
        out_shape=jax.ShapeDtypeStruct((heads * head_pad, width), low),
    )(slab, first)


def prep_wide_body(total, slab_ref, out_ref):
    rows = slab_ref[:, 0, :]
    at = pl.program_id(0) * rows.shape[0] + lax.broadcasted_iota(jnp.int32, rows.shape, 0)
    out_ref[...] = jnp.where(at < total, rows, 0.0).astype(low)


def prep_wide(slab, rows_pad):
    total, _, width = slab.shape
    block = rows_pad // 4
    return call(
        functools.partial(prep_wide_body, total),
        "prep_wide",
        grid=(4,),
        in_specs=[pl.BlockSpec((block, 1, width), lambda i: (i, 0, 0))],
        out_specs=pl.BlockSpec((block, width), lambda i: (i, 0)),
        out_shape=jax.ShapeDtypeStruct((rows_pad, width), low),
    )(slab)


def momentum_body(total, moment_ref, grad_ref, first_ref, top_ref, rest_ref):
    grad = grad_ref[...].astype(f32)
    first = momentum_decay * moment_ref[:, 0, :] + grad
    first_ref[...] = first.reshape(first_ref.shape)
    at = pl.program_id(0) * grad.shape[0] + lax.broadcasted_iota(jnp.int32, grad.shape, 0)
    top, rest = split(jnp.where(at < total, grad + momentum_decay * first, 0.0))
    top_ref[...] = top
    rest_ref[...] = rest


def momentum(moments, grad):
    total, _, width = moments.shape
    rows_pad = grad.shape[0]
    block = rows_pad // 4
    slab_spec = pl.BlockSpec((block, 1, width), lambda i: (i, 0, 0))
    flat_spec = pl.BlockSpec((block, width), lambda i: (i, 0))
    return call(
        functools.partial(momentum_body, total),
        "momentum",
        grid=(4,),
        in_specs=[slab_spec, flat_spec],
        out_specs=[slab_spec, flat_spec, flat_spec],
        out_shape=[
            jax.ShapeDtypeStruct(moments.shape, f32),
            jax.ShapeDtypeStruct((rows_pad, width), low),
            jax.ShapeDtypeStruct((rows_pad, width), low),
        ],
    )(moments, grad)


def momentum_again_body(total, moment_ref, grad_ref, *refs):
    momentum_body(total, moment_ref, grad_ref, *refs[-3:])


def momentum_again(moments, grad, first, top, rest, *others):
    total, _, width = moments.shape
    rows = grad.shape[0]
    slab_spec = pl.BlockSpec((rows, 1, width), lambda i: (i, 0, 0))
    flat_spec = pl.BlockSpec((rows, width), lambda i: (i, 0))
    return call(
        functools.partial(momentum_again_body, total),
        "momentum_again",
        grid=(1,),
        in_specs=[slab_spec, flat_spec] + [pl.BlockSpec(memory_space=pl.ANY)] * (3 + len(others)),
        out_specs=[slab_spec, flat_spec, flat_spec],
        out_shape=[jax.ShapeDtypeStruct(x.shape, x.dtype) for x in (first, top, rest)],
        input_output_aliases={2: 0, 3: 1, 4: 2},
    )(moments, grad, first, top, rest, *others)


def packed_at(column):
    return 128 * (column * (column + 1) // 2)


def upper(width):
    for j in range(0, width, 256):
        for i in range(0, min(j + 256, width), 256):
            yield i, j, pl.ds(i, min(256, width - i)), pl.ds(j, min(256, width - j))


def gram_body(top_ref, rest_ref, out_ref):
    for i, j, rows, columns in upper(top_ref.shape[1]):
        value = (
            dot(top_ref[:, rows], top_ref[:, columns], (0, 0))
            + dot(top_ref[:, rows], rest_ref[:, columns], (0, 0))
            + dot(rest_ref[:, rows], top_ref[:, columns], (0, 0))
        )
        for c in range(j // 128, (j + value.shape[1]) // 128):
            used = min(value.shape[0], 128 * (c + 1) - i)
            lanes = 128 * c - j
            out_ref[pl.ds(packed_at(c) + i, used), :] = value[:used, lanes : lanes + 128]


def gram_of(top, rest):
    count = top.shape[1] // 128
    return call(
        gram_body,
        "gram",
        in_specs=[pl.BlockSpec(memory_space=pltpu.VMEM)] * 2,
        out_specs=pl.BlockSpec(memory_space=pltpu.VMEM),
        out_shape=jax.ShapeDtypeStruct((packed_at(count), 128), f32),
    )(top, rest)


class Iterate:
    def __init__(self, a_top, a_rest, b_top, t_top, t_rest, x_ref):
        self.a = a_top, a_rest
        self.b = b_top
        self.t = t_top, t_rest
        self.x = x_ref
        self.width = a_top.shape[0]
        self.step = x_ref.shape[0] // 4
        self.diagonal = lax.broadcasted_iota(jnp.int32, (128, 128), 0) == lax.broadcasted_iota(
            jnp.int32, (128, 128), 1
        )

    def put(self, i, j, value):
        tall, wide = value.shape
        for x, rows, columns in ((value, pl.ds(i, tall), pl.ds(j, wide)),) + (
            ((value.T, pl.ds(j, wide), pl.ds(i, tall)),) if i != j else ()
        ):
            top, rest = split(x)
            self.a[0][rows, columns] = top
            self.a[1][rows, columns] = rest

    def both(self, pair, rows, columns):
        return pair[0][rows, columns].astype(f32) + pair[1][rows, columns].astype(f32)

    def symmetric(self, left, rights, finish):
        for i, j, rows, columns in upper(self.width):
            value = dot(left[rows, :], rights[0][:, columns], (1, 0))
            for right in rights[1:]:
                value = value + dot(left[rows, :], right[:, columns], (1, 0))
            finish(i, j, rows, columns, value)

    def recenter(self, center):
        total = jnp.zeros((128, 128), f32)
        for c in range(0, self.width, 128):
            at = pl.ds(c, 128)
            total = total + jnp.where(self.diagonal, self.both(self.a, at, at), 0.0)
        mean = jnp.sum(total) / self.width
        for c in range(0, self.width, 128):
            at = pl.ds(c, 128)
            top, rest = split(self.both(self.a, at, at) - jnp.where(self.diagonal, mean, 0.0))
            self.a[0][at, at] = top
            self.a[1][at, at] = rest
        return center + mean

    def mix(self, center):
        def finish(i, j, rows, columns, value):
            value = (coef_b + 2.0 * coef_c * center) * self.both(
                self.a, rows, columns
            ) + coef_c * value
            self.b[rows, columns] = value.astype(low)
            if i != j:
                self.b[columns, rows] = value.T.astype(low)

        self.symmetric(self.a[0], (self.a[0],), finish)
        return coef_a + coef_b * center + coef_c * center * center

    def stepped(self, rows, lead):
        x = self.x[rows, :]
        return lead * x + dot(x.astype(low), self.b[...], (1, 0))

    def propagate(self, center, lead, passes):
        tall = self.width // 3

        @pl.loop(0, 3)
        def _(r):
            rows = pl.ds(r * tall, tall)
            value = lead * self.both(self.a, rows, slice(None)) + center * self.b[rows, :].astype(f32)
            for left in self.a[:passes]:
                value = value + dot(left[rows, :], self.b[...], (1, 0))
            top, rest = split(value)
            self.t[0][rows, :] = top
            self.t[1][rows, :] = rest

        def finish(i, j, rows, columns, value):
            carried = lead * self.both(self.t, rows, columns)
            carried = carried + lead * center * self.b[rows, columns].astype(f32)
            self.put(i, j, carried + value)

        self.symmetric(self.b, self.t[:passes], finish)
        return lead * lead * center

    def sweep(self, center, passes=2):
        center = self.recenter(center)
        lead = self.mix(center)

        @pl.loop(0, 4)
        def _(r):
            rows = pl.ds(r * self.step, self.step)
            self.x[rows, :] = self.stepped(rows, lead)

        return self.propagate(center, lead, passes)


def iterate_body(
    total,
    square_ref,
    rate_ref,
    gram_ref,
    full_hbm,
    top_hbm,
    rest_hbm,
    slab_hbm,
    first_ref,
    out_hbm,
    a_top,
    a_rest,
    b_top,
    t_top,
    t_rest,
    x_ref,
    slab_ref,
    sem,
):
    state = Iterate(a_top, a_rest, b_top, t_top, t_rest, x_ref)
    width, step = state.width, state.step
    rows_pad = x_ref.shape[0]
    fetch_full = pltpu.make_async_copy(full_hbm, t_rest, sem.at[0])
    fetch_top = pltpu.make_async_copy(top_hbm, b_top.at[pl.ds(0, rows_pad)], sem.at[1])
    fetch_rest = pltpu.make_async_copy(rest_hbm, t_top.at[pl.ds(0, rows_pad)], sem.at[2])
    fetch_slab = pltpu.make_async_copy(slab_hbm, slab_ref.at[pl.ds(0, total)], sem.at[3])
    for fetch in (fetch_full, fetch_top, fetch_rest, fetch_slab):
        fetch.start()
    is_square = square_ref[0] == 1
    trace = jnp.zeros((128, 128), f32)
    for c in range(width // 128):
        block = gram_ref[pl.ds(packed_at(c) + 128 * c, 128), :]
        trace = trace + jnp.where(state.diagonal, block, 0.0)
    fetch_full.wait()

    def add_squares(r, sums):
        part = t_rest[pl.ds(r * 128, 128), :].astype(f32)
        return sums + jnp.sum(part * part, axis=0, keepdims=True)

    squares = lax.fori_loop(0, width // 128, add_squares, jnp.zeros((1, width), f32))
    norm = jnp.sqrt(jnp.where(is_square, jnp.sum(squares), jnp.sum(trace)))
    scaling = 1.0 / (norm + 1e-07)
    scale_two = scaling * scaling

    @pl.when(is_square)
    def _():
        for i, j, rows, columns in upper(width):
            state.put(i, j, dot(t_rest[:, rows], t_rest[:, columns], (0, 0)) * scale_two)

    @pl.when(jnp.logical_not(is_square))
    def _():
        for c in range(width // 128):
            for r in range(c + 1):
                block = gram_ref[pl.ds(packed_at(c) + 128 * r, 128), :]
                state.put(128 * r, 128 * c, block * scale_two)

    fetch_top.wait()
    fetch_rest.wait()
    rest_scaling = jnp.where(is_square, 0.0, scaling)

    @pl.loop(0, 4)
    def _(r):
        rows = pl.ds(r * step, step)
        x_ref[rows, :] = b_top[rows, :].astype(f32) * scaling + t_top[rows, :].astype(f32) * rest_scaling

    center = lax.fori_loop(
        0, NS_ITERS - 2, lambda _, center: state.sweep(center), jnp.float32(0.0)
    )
    center = state.sweep(center, 1)
    lead = state.mix(state.recenter(center))
    fetch_slab.wait()
    rate = rate_ref[0]

    @pl.loop(0, 4)
    def _(r):
        rows = pl.ds(r * step, step)
        new = slab_ref[rows, 0, :] * (1.0 - matrix_rate * matrix_decay) - rate * state.stepped(rows, lead)
        slab_ref[rows, :, :] = new.reshape(step, 1, width)

    leave = pltpu.make_async_copy(slab_ref.at[pl.ds(0, total)], out_hbm, sem.at[0])
    leave.start()
    leave.wait()


def iterate(square, rate, gram, full, top, rest, slab, first):
    total, _, width = slab.shape
    rows_pad = top.shape[0]
    vmem, smem = pl.BlockSpec(memory_space=pltpu.VMEM), pl.BlockSpec(memory_space=pltpu.SMEM)
    far = pl.BlockSpec(memory_space=pl.ANY)
    return call(
        functools.partial(iterate_body, total),
        "iterate",
        vmem=56,
        in_specs=[smem, smem, vmem] + [far] * 5,
        out_specs=far,
        out_shape=jax.ShapeDtypeStruct(slab.shape, f32),
        scratch_shapes=[pltpu.VMEM((width, width), low)] * 5
        + [
            pltpu.VMEM((rows_pad, width), f32),
            pltpu.VMEM((rows_pad, 1, width), f32),
            pltpu.SemaphoreType.DMA((4,)),
        ],
        cost_estimate=pl.CostEstimate(
            flops=80_000_000_000, bytes_accessed=20_000_000, transcendentals=0
        ),
    )(square, rate, gram, full, top, rest, slab, first)


def attend_body(scale, qkv_ref, context_ref, soft_ref):
    query, key, value = qkv_ref[0, 0], qkv_ref[1, 0], qkv_ref[2, 0]
    scores = dot(key, query, (0, 0)) * scale
    at = lax.broadcasted_iota(jnp.int32, scores.shape, 0)
    scores = jnp.where(at < LEN, scores, -1e30)
    exponent = jnp.exp(scores - jnp.max(scores, axis=0, keepdims=True))
    soft = (exponent / jnp.sum(exponent, axis=0, keepdims=True)).astype(low)
    soft_ref[0] = soft
    context = dot(value, soft, (1, 0))
    context_ref[0] = context[: context_ref.shape[1]].astype(low)


def attend(qkv, head_size, scale):
    _, groups, head_pad, rows = qkv.shape
    return call(
        functools.partial(attend_body, scale),
        "attend",
        grid=(groups,),
        in_specs=[pl.BlockSpec((3, 1, head_pad, rows), lambda h: (0, h, 0, 0))],
        out_specs=[
            pl.BlockSpec((1, head_size, rows), lambda h: (h, 0, 0)),
            pl.BlockSpec((1, rows, rows), lambda h: (h, 0, 0)),
        ],
        out_shape=[
            jax.ShapeDtypeStruct((groups, head_size, rows), low),
            jax.ShapeDtypeStruct((groups, rows, rows), low),
        ],
    )(qkv)


def attend_back_body(scale, qkv_ref, soft_ref, grad_ref, first_ref, other_ref, out_ref):
    query, key, value = qkv_ref[0, 0], qkv_ref[1, 0], qkv_ref[2, 0]
    grad, soft = grad_ref[0], soft_ref[0]
    grad_soft = dot(value, grad, (0, 0))
    soft_f32 = soft.astype(f32)
    along = jnp.sum(soft_f32 * grad_soft, axis=0, keepdims=True)
    grad_scores = (soft_f32 * (grad_soft - along)).astype(low)
    out_ref[0, 0] = (dot(key, grad_scores, (1, 0)) * scale).astype(low)
    out_ref[1, 0] = (dot(query, grad_scores, (1, 1)) * scale).astype(low)
    out_ref[2, 0] = dot(grad, soft, (1, 1)).astype(low)


def attend_back(qkv, soft, grad, first, other, scale):
    _, groups, head_pad, rows = qkv.shape
    three = pl.BlockSpec((3, 1, head_pad, rows), lambda h: (0, h, 0, 0))
    return call(
        functools.partial(attend_back_body, scale),
        "attend_back",
        grid=(groups,),
        in_specs=[
            three,
            pl.BlockSpec((1, rows, rows), lambda h: (h, 0, 0)),
            pl.BlockSpec((1, head_pad, rows), lambda h: (h, 0, 0)),
            pl.BlockSpec(memory_space=pl.ANY),
            pl.BlockSpec(memory_space=pl.ANY),
        ],
        out_specs=three,
        out_shape=jax.ShapeDtypeStruct(qkv.shape, low),
    )(qkv, soft, grad, first, other)


def whiten(inputs):
    average = jnp.mean(inputs, axis=-1, keepdims=True)
    centered = inputs - average
    variance = jnp.mean(centered * centered, axis=-1, keepdims=True)
    inverse = lax.rsqrt(variance + norm_eps)
    return centered * inverse, inverse


def whiten_back(grad, gain_row, hat, inverse):
    scaled = grad * gain_row
    mean_one = jnp.mean(scaled, axis=-1, keepdims=True)
    mean_two = jnp.mean(scaled * hat, axis=-1, keepdims=True)
    return inverse * (scaled - mean_one - hat * mean_two)


def gelu_both(inputs):
    squared = inputs * inputs
    curve = jnp.tanh(0.7978845608028654 * (inputs + 0.044715 * inputs * squared))
    value = 0.5 * inputs * (1.0 + curve)
    slope = 0.5 * (1.0 + curve) + 0.5 * inputs * (1.0 - curve * curve) * 0.7978845608028654 * (
        1.0 + 3.0 * 0.044715 * squared
    )
    return value, slope


def product(form, left, right):
    return jnp.einsum(form, left, right, preferred_element_type=f32)


def flip(x, axis, mask):
    count = lax.axis_size(axis)
    return lax.ppermute(x, axis, [(i, i ^ mask) for i in range(count)])


def gather_chunks(piece, first):
    count = lax.axis_size("dp")
    half = count // 2
    me = lax.axis_index("dp")
    pair, core = me >> 1, me & 1
    whole = jnp.zeros((half, 2) + piece.shape, piece.dtype)
    for mask, part in enumerate(exchange(piece, first)):
        whole = lax.dynamic_update_slice(whole, part[None, None], (pair ^ mask, core, 0, 0))
    mine = lax.dynamic_slice_in_dim(whole, core, 1, 1)
    other = flip(mine, "dp", 1)
    whole = lax.dynamic_update_slice_in_dim(whole, other, 1 - core, 1)
    return whole.reshape((count,) + piece.shape)


def scatter_sum(whole, order):
    count, rows, columns = whole.shape
    bits = count.bit_length() - 1
    me = lax.axis_index("dp")
    whole = whole.reshape((2,) * bits + (rows, columns))
    for bit in order:
        at = bits - 1 - bit
        mine = (me >> bit) & 1
        kept = lax.dynamic_slice_in_dim(whole, mine, 1, at)
        sent = lax.dynamic_slice_in_dim(whole, 1 - mine, 1, at)
        got = flip(sent, "dp", 1 << bit)
        whole = (kept.astype(f32) + got.astype(f32)).astype(low)
    return whole.reshape(rows, columns)


def arrivals(piece):
    count = lax.axis_size("seq")
    return [
        lax.ppermute(piece, "seq", [(i, (i + shift) % count) for i in range(count)])
        for shift in range(1, count)
    ]


def gather_seq(piece):
    count = lax.axis_size("seq")
    me = lax.axis_index("seq")
    whole = jnp.zeros((count,) + piece.shape, piece.dtype)
    for shift, part in enumerate([piece] + arrivals(piece)):
        whole = lax.dynamic_update_slice_in_dim(whole, part[None], (me - shift) % count, 0)
    return whole


def total_sum(x):
    for axis in ("dp", "seq"):
        step = 1
        while step < lax.axis_size(axis):
            x = x + flip(x, axis, step)
            step *= 2
    return x


def zero_of(token):
    return jnp.minimum(jnp.abs(token), 0.0)


def after(x, token):
    return x + zero_of(token).astype(x.dtype)


def touch_body(*refs):
    pass


def touch(arrays, *others):
    far = pl.BlockSpec(memory_space=pl.ANY)
    count = len(arrays)
    return call(
        touch_body,
        "touch",
        in_specs=[far] * (count + len(others)),
        out_specs=[far] * count,
        out_shape=[jax.ShapeDtypeStruct(x.shape, x.dtype) for x in arrays],
        input_output_aliases={i: i for i in range(count)},
    )(*arrays, *others)


def relative(me, count):
    place = jnp.arange(count)
    half = count // 2
    return me ^ ((place % half) * 2 + place // half)


def exchange(piece, first):
    half = lax.axis_size("dp") // 2
    arrived = [flip(piece, "dp", mask << 1) for mask in range(1, half)]
    return [piece] + [after(x, first) for x in arrived]


def gather_relative(pieces, first):
    arrived = exchange(jnp.concatenate(pieces, axis=0), first)
    result, at = [], 0
    for piece in pieces:
        rows = piece.shape[0]
        mine = jnp.concatenate([x[at : at + rows] for x in arrived], axis=0)
        result.append(jnp.concatenate([mine, flip(mine, "dp", 1)], axis=0))
        at += rows
    return result


def scatter_relative(whole, order):
    count = lax.axis_size("dp")
    bits = count.bit_length() - 1
    rows, columns = whole.shape[0] // count, whole.shape[1]
    whole = whole.reshape((2,) * bits + (rows, columns))
    for bit in order:
        at = 0 if bit == 0 else bits - bit
        kept = lax.slice_in_dim(whole, 0, 1, axis=at)
        got = flip(lax.slice_in_dim(whole, 1, 2, axis=at), "dp", 1 << bit)
        whole = (kept.astype(f32) + got.astype(f32)).astype(low)
    return whole.reshape(rows, columns)


def local(
    tokens, cotangent, counts, owner_table, owned_weights, owned_moments, vectors, vector_moments
):
    seq_count = lax.axis_size("seq")
    dp_count = lax.axis_size("dp")
    bits = dp_count.bit_length() - 1
    seq_index = lax.axis_index("seq")
    dp_index = lax.axis_index("dp")
    capacity = tokens.shape[1]
    width = tokens.shape[2]
    slots = capacity * seq_count
    head_size = width // HEADS
    head_pad = -(-head_size // 16) * 16
    heads = HEADS // seq_count
    score_scale = 1.0 / math.sqrt(head_size)
    widths = (width, width, width, width, FF, FF)
    cols = width // seq_count
    ff_cols = FF // seq_count
    share = -(-LEN // (16 * seq_count)) * 16
    packed = share * seq_count
    square_rows = heads * head_pad
    square_chunk = -(-square_rows // (8 * dp_count)) * 8
    square_total = square_chunk * dp_count
    wide_chunk = -(-ff_cols // (8 * dp_count)) * 8
    wide_rows = wide_chunk * dp_count
    orders = (tuple(range(bits)), (0,) + tuple(range(bits - 1, 0, -1)))

    rows_in = tokens[0]
    vector_count = vectors.shape[0]
    vector_rows = -(-vector_count // width)
    extra = -(-vector_rows // 16) * 16
    payload = jnp.pad(vectors, (0, extra * width - vector_count)).reshape(extra, width)
    own_ids = jnp.arange(capacity)[:, None]
    own_valid = (own_ids < lax.dynamic_index_in_dim(counts[0], seq_index, 0)).astype(f32)
    cot_own = (cotangent[0] * own_valid).astype(low)
    payload = jnp.concatenate([rows_in.astype(low), payload.astype(low), cot_own], axis=0)
    gathered = lax.all_gather(payload, "seq", axis=0, tiled=False)
    token_slots = gathered[:, : capacity + extra].reshape(seq_count * (capacity + extra), width)
    cot_slots = gathered[:, capacity + extra :].reshape(slots, width)

    counts_row = counts[0]
    starts = jnp.cumsum(counts_row) - counts_row

    def rows_of(per):
        ids = jnp.arange(per * seq_count)
        real = (ids % per) < jnp.repeat(counts_row, per)
        return jnp.where(real, jnp.repeat(starts, per) + ids % per, packed)

    def picks(row):
        return (jnp.arange(packed)[:, None] == row[None, :]).astype(low)

    slot_row = rows_of(capacity)
    token_pick = picks(rows_of(capacity + extra))
    own_row = lax.dynamic_slice_in_dim(slot_row, seq_index * capacity, capacity)
    own_pick = picks(own_row)
    grad_rows = product("rc,cd->rd", picks(slot_row), cot_slots).astype(low)

    slab = jnp.transpose(owned_weights[0], (2, 1, 0))
    moments = jnp.transpose(owned_moments[0], (2, 1, 0))

    def send(x):
        return lax.all_to_all(x, "dp", split_axis=0, concat_axis=0, tiled=True)

    square_own = prep_square(slab, payload, heads, head_size, head_pad)
    near = jnp.stack(exchange(square_own, gathered[0, 0, 0]))
    far = flip(near, "dp", 1)
    squares = []
    for m in range(4):
        away = owner_table[m] ^ dp_index
        from_near = lax.dynamic_index_in_dim(near, away >> 1, 0, keepdims=False)
        from_far = lax.dynamic_index_in_dim(far, away >> 1, 0, keepdims=False)
        squares.append(jnp.where((away & 1) == 0, from_near, from_far))
    w_qkv = jnp.concatenate(squares[:3], axis=0)
    w_out_piece = jnp.pad(squares[3], ((0, square_total - square_rows), (0, 0)))
    w_out_piece = lax.dynamic_slice_in_dim(w_out_piece, dp_index * square_chunk, square_chunk)
    w_out_part = gather_seq(w_out_piece).reshape(seq_count * square_chunk, width)
    wide_sent = prep_wide(slab, wide_rows).reshape(dp_count, wide_chunk, width)
    got_wide = send(wide_sent)
    wide_pieces = [lax.dynamic_index_in_dim(got_wide, owner_table[m], 0, keepdims=False) for m in (4, 5)]

    w_up, w_down = gather_relative(wide_pieces, gathered[0, 0, 0])

    vector_full = gathered[:, capacity : capacity + vector_rows].reshape(seq_count, -1)
    vector_full = vector_full[:, :vector_count].reshape(-1).astype(f32)
    row_params = vector_full[: 8 * width].reshape(8, width)
    up_bias = lax.dynamic_slice_in_dim(vector_full, 8 * width + seq_index * ff_cols, ff_cols)
    up_bias = jnp.pad(up_bias, (0, wide_rows - ff_cols)).reshape(dp_count, wide_chunk)
    up_bias = jnp.take(up_bias, relative(dp_index, dp_count), axis=0).reshape(wide_rows)

    def head_bias(row):
        own = lax.dynamic_slice_in_dim(row, seq_index * cols, cols).reshape(heads, head_size)
        return jnp.pad(own, ((0, 0), (0, head_pad - head_size))).reshape(square_rows)

    qkv_bias = jnp.concatenate(
        [head_bias(row_params[2]), jnp.zeros((square_rows,), f32), head_bias(row_params[3])]
    )

    token_rows = product("rc,cd->rd", token_pick, token_slots)
    hat_packed = whiten(token_rows)[0]
    normed = (hat_packed * row_params[0] + row_params[1]).astype(low)
    qkv_bias = after(qkv_bias, w_up[0, 0] + w_down[0, 0] + grad_rows[0, 0] + w_out_part[0, 0])
    qkv = (product("ed,rd->er", w_qkv, normed) + qkv_bias[:, None]).astype(low)
    qkv = qkv.reshape(3, heads, head_pad, packed)
    context_own, soft = attend(qkv, head_size, score_scale)
    token = context_own[0, 0, 0]
    w_out = gather_chunks(w_out_part, token)
    w_out = w_out.reshape(dp_count, seq_count, square_chunk, width).transpose(1, 0, 2, 3)
    w_out = w_out.reshape(seq_count, square_total, width)[:, :square_rows]
    w_out = w_out.reshape(seq_count * heads, head_pad, width)[:, :head_size].reshape(width, width)
    w_out_own = lax.dynamic_slice_in_dim(w_out, seq_index * cols, cols, axis=1)
    w_out_own = jnp.pad(
        w_out_own.reshape(width, heads, head_size), ((0, 0), (0, 0), (0, head_pad - head_size))
    ).reshape(width, square_rows)
    context = lax.all_gather(context_own.reshape(cols, packed), "seq", axis=0, tiled=True)
    middle = token_rows + product("er,oe->ro", context, w_out) + row_params[4]
    hat_two, inverse_two = whiten(middle)
    normed_two = (hat_two * row_params[5] + row_params[6]).astype(low)
    pre_act = product("rd,fd->rf", normed_two, w_up) + up_bias
    hidden_f32, slope = gelu_both(pre_act)
    hidden = hidden_f32.astype(low)

    grad_hidden = product("rd,fd->rf", grad_rows, w_down)
    grad_pre = (slope * grad_hidden).astype(low)
    grad_down = product("rf,rd->fd", hidden, grad_rows).astype(low)
    grad_up = product("rf,rd->fd", grad_pre, normed_two).astype(low)
    grad_normed_two_part = (
        product("rf,fd->rd", grad_pre, w_up) + zero_of(grad_down[0, 0] + grad_up[0, 0]).astype(f32)
    ).astype(low)
    grad_up_bias = jnp.sum(grad_pre.astype(f32), axis=0).reshape(dp_count, wide_chunk)
    back = jnp.arange(dp_count) ^ dp_index
    grad_up_bias = jnp.take(grad_up_bias, (back & 1) * (dp_count // 2) + (back >> 1), axis=0)
    grad_up_bias = grad_up_bias.reshape(wide_rows)[:ff_cols]

    sum_down = scatter_relative(grad_down, orders[0])
    sum_up = scatter_relative(grad_up, orders[1])
    def to_owner(pairs):
        total = 0
        for piece, m in pairs:
            here = (jnp.arange(dp_count) == owner_table[m])[:, None, None]
            total = total + jnp.where(here, piece[None], jnp.zeros((), low))
        return total

    wide_back = to_owner([(sum_up, 4), (sum_down, 5)])
    grad_normed_two = after(
        lax.psum_scatter(grad_normed_two_part, "seq", scatter_dimension=0, tiled=True),
        wide_back[0, 0, 0],
    ).astype(f32)
    back_wide = send(wide_back).reshape(wide_rows, width)
    def own_share(x):
        return lax.dynamic_slice_in_dim(x, seq_index * share, share)

    own_grad = own_share(grad_rows).astype(f32)
    own_hat = own_share(hat_two)
    grad_bias_down = jnp.sum(own_grad, axis=0)
    grad_gain_two = jnp.sum(grad_normed_two * own_hat, axis=0)
    grad_shift_two = jnp.sum(grad_normed_two, axis=0)
    grad_mid_norm = whiten_back(grad_normed_two, row_params[5], own_hat, own_share(inverse_two))
    grad_attn_own = (own_grad + grad_mid_norm).astype(low)
    grad_bias_out = jnp.sum(grad_attn_own.astype(f32), axis=0)
    grad_attn = lax.all_gather(grad_attn_own, "seq", axis=0, tiled=True)
    unpick = (slot_row[:, None] == jnp.arange(packed)[None, :]).astype(low)
    placed_middle = jnp.where(
        (jnp.arange(packed) // share == seq_index)[:, None], middle + row_params[7], 0.0
    )
    out_part = (
        product("rf,fd->rd", hidden, w_down) + placed_middle + zero_of(grad_attn_own[0, 0]).astype(f32)
    ).astype(low)
    out_slots = product("cr,rd->cd", unpick, out_part).astype(low)
    first_moment, top, rest = momentum(moments, back_wide)
    wide_gram = gram_of(top, rest)
    gram_share = lax.psum_scatter(wide_gram, "seq", scatter_dimension=0, tiled=True)
    first_gram = lax.all_gather(gram_share, "seq", axis=0, tiled=True)


    grad_context = product("de,rd->er", w_out_own, grad_attn).astype(low)
    grad_qkv = attend_back(qkv, soft, grad_context.reshape(heads, head_pad, packed), wide_gram, out_slots, score_scale)
    grad_qkv_flat = grad_qkv.reshape(3 * square_rows, packed)
    grad_attn_cols = lax.dynamic_slice_in_dim(grad_attn, seq_index * cols, cols, axis=1)
    grad_w_out = product("rd,er->de", grad_attn_cols, context)
    grad_w_qkv = product("er,rd->ed", grad_qkv_flat, normed)
    grad_qkv_bias = jnp.sum(grad_qkv.astype(f32), axis=3)[:, :, :head_size].reshape(3, cols)

    grad_normed_part = product("er,ed->rd", grad_qkv_flat, w_qkv)
    grad_gain_one = jnp.sum(grad_normed_part * hat_packed, axis=0)
    grad_shift_one = jnp.sum(grad_normed_part, axis=0)
    grad_normed_slots = product("cr,rd->cd", unpick, grad_normed_part.astype(low)).astype(low)

    grad_mid_slots = product("rc,rd->cd", own_pick, grad_attn)

    def square_parts(x):
        x = jnp.pad(x.astype(low), ((0, square_total - square_rows), (0, 0)))
        return x.reshape(dp_count, square_chunk, width)

    late = [square_parts(grad_w_qkv[m * square_rows : (m + 1) * square_rows]) for m in range(3)]
    grad_w_out = jnp.pad(
        grad_w_out.reshape(heads, head_size, width), ((0, 0), (0, head_pad - head_size), (0, 0))
    )
    late.append(square_parts(grad_w_out.reshape(square_rows, width)))
    sum_qk = scatter_sum(jnp.concatenate(late[:2], axis=1), orders[0])
    sum_vo = scatter_sum(jnp.concatenate(late[2:], axis=1), orders[1])
    square_back = to_owner(
        [
            (sum_qk[:square_chunk], 0),
            (sum_qk[square_chunk:], 1),
            (sum_vo[:square_chunk], 2),
            (sum_vo[square_chunk:], 3),
        ]
    )
    back_square = send(after(square_back, gram_share[0, 0])).reshape(square_total, width)[:square_rows]
    back_square = back_square.reshape(heads, head_pad, width)[:, :head_size].reshape(cols, width)
    first_moment, top, rest = momentum_again(
        moments, back_wide[:cols] + back_square, first_moment, top, rest, grad_normed_slots, grad_mid_slots
    )
    def spot(piece):
        return lax.dynamic_update_slice_in_dim(
            jnp.zeros((piece.shape[0] * seq_count,), f32), piece, seq_index * piece.shape[0], 0
        )

    vector_grad = jnp.concatenate(
        [
            grad_gain_one,
            grad_shift_one,
            spot(grad_qkv_bias[0]),
            spot(grad_qkv_bias[2]),
            grad_bias_out,
            grad_gain_two,
            grad_shift_two,
            grad_bias_down,
            spot(grad_up_bias),
        ]
    )
    padded = -(-vector_grad.shape[0] // 1024) * 1024
    vector_grad = jnp.pad(vector_grad, (0, padded - vector_grad.shape[0])).reshape(-1, 128)
    vector_block = total_sum(after(vector_grad, top[0, 0].astype(f32)))
    (direction,) = touch([top[:cols]], first_gram, vector_block)
    direction = lax.all_gather(direction, "seq", axis=0, tiled=True)
    is_square = jnp.any(owner_table[:4] == dp_index).astype(jnp.int32).reshape(1)
    grad_normed_slots, out_slots = touch([grad_normed_slots, out_slots], direction, first_gram)
    update_scale = jnp.zeros((), f32)
    for m in range(6):
        update_scale = jnp.where(
            owner_table[m] == dp_index,
            jnp.float32(matrix_rate * 0.2 * math.sqrt(max(width, widths[m]))),
            update_scale,
        )

    grad_normed = lax.psum_scatter(
        grad_normed_slots, "seq", scatter_dimension=0, tiled=True
    ).astype(f32)
    block_out = lax.psum_scatter(
        out_slots, "seq", scatter_dimension=0, tiled=True
    ).astype(f32)
    hat_one, inverse_one = whiten(rows_in)
    grad_in_norm = whiten_back(grad_normed, row_params[0], hat_one, inverse_one)
    grad_tokens = (grad_mid_slots + grad_in_norm) * own_valid

    vector_total = lax.dynamic_slice_in_dim(
        vector_block.reshape(-1), seq_index * vector_count, vector_count
    )
    updated = iterate(
        is_square, update_scale.reshape(1), first_gram, direction, top, rest, slab, vector_block
    )

    first_new = beta_first * vector_moments[0] + (1.0 - beta_first) * vector_total
    second_new = beta_second * vector_moments[1] + (1.0 - beta_second) * vector_total * vector_total
    first_fix = 1.0 - beta_first**STEP
    second_fix = 1.0 - beta_second**STEP
    vector_new = vectors - vector_rate * (first_new / first_fix) / (
        jnp.sqrt(second_new / second_fix) + adam_eps
    )
    return (
        block_out[None],
        grad_tokens[None],
        jnp.transpose(first_moment, (2, 1, 0))[None],
        jnp.transpose(updated, (2, 1, 0))[None],
        first_new,
        second_new,
        vector_new,
    )


def solution(mesh):
    in_specs = (
        P("dp", "seq", None),
        P("dp", "seq", None),
        P("dp", None),
        P(),
        P("dp", None, "seq", None),
        P("dp", None, "seq", None),
        P("seq"),
        P(None, "seq"),
    )
    out_specs = (
        P("dp", "seq", None),
        P("dp", "seq", None),
        P("dp", None, "seq", None),
        P("dp", None, "seq", None),
        P("seq"),
        P("seq"),
        P("seq"),
    )
    return jax.shard_map(local, mesh=mesh, in_specs=in_specs, out_specs=out_specs, check_vma=False)
```

```python
import functools
import math

import jax
import jax.numpy as jnp
from jax import lax
from jax.experimental import pallas as pl
from jax.experimental.pallas import tpu as pltpu
from jax.sharding import PartitionSpec as P

HEADS = 16
FF = 4304
LEN = 729
NS_ITERS = 5
STEP = 10

norm_eps = 1e-06
coef_a = 3.4445
coef_b = -4.775
coef_c = 2.0315
momentum_decay = 0.95
matrix_rate = 0.15
matrix_decay = 0.1
beta_first = 0.9
beta_second = 0.999
vector_rate = 0.5
adam_eps = 1e-08
low = jnp.bfloat16
f32 = jnp.float32


def call(body, name, **kw):
    vmem = kw.pop("vmem", 48)
    return pl.pallas_call(
        body,
        name=name,
        compiler_params=pltpu.CompilerParams(vmem_limit_bytes=vmem * 1024 * 1024),
        **kw,
    )


def dot(left, right, contract):
    return lax.dot_general(
        left, right, ((tuple(contract[:1]), tuple(contract[1:])), ((), ())), preferred_element_type=f32
    )


def split(x):
    top = x.astype(low)
    return top, (x - top.astype(f32)).astype(low)


def prep_square_body(slab_ref, first_ref, out_ref):
    rows = slab_ref[:, 0, :]
    extra = out_ref.shape[0] - rows.shape[0]
    padded = jnp.concatenate([rows, jnp.zeros((extra, rows.shape[1]), f32)], axis=0)
    out_ref[...] = padded.astype(low)


def prep_square(slab, first, heads, head_size, head_pad):
    width = slab.shape[2]
    return call(
        prep_square_body,
        "prep_square",
        grid=(heads,),
        in_specs=[
            pl.BlockSpec((head_size, 1, width), lambda i: (i, 0, 0)),
            pl.BlockSpec(memory_space=pl.ANY),
        ],
        out_specs=pl.BlockSpec((head_pad, width), lambda i: (i, 0)),
        out_shape=jax.ShapeDtypeStruct((heads * head_pad, width), low),
    )(slab, first)


def prep_wide_body(total, slab_ref, out_ref):
    rows = slab_ref[:, 0, :]
    at = pl.program_id(0) * rows.shape[0] + lax.broadcasted_iota(jnp.int32, rows.shape, 0)
    out_ref[...] = jnp.where(at < total, rows, 0.0).astype(low)


def prep_wide(slab, rows_pad):
    total, _, width = slab.shape
    block = rows_pad // 4
    return call(
        functools.partial(prep_wide_body, total),
        "prep_wide",
        grid=(4,),
        in_specs=[pl.BlockSpec((block, 1, width), lambda i: (i, 0, 0))],
        out_specs=pl.BlockSpec((block, width), lambda i: (i, 0)),
        out_shape=jax.ShapeDtypeStruct((rows_pad, width), low),
    )(slab)


def momentum_body(total, moment_ref, grad_ref, first_ref, top_ref, rest_ref):
    grad = grad_ref[...].astype(f32)
    first = momentum_decay * moment_ref[:, 0, :] + grad
    first_ref[...] = first.reshape(first_ref.shape)
    at = pl.program_id(0) * grad.shape[0] + lax.broadcasted_iota(jnp.int32, grad.shape, 0)
    top, rest = split(jnp.where(at < total, grad + momentum_decay * first, 0.0))
    top_ref[...] = top
    rest_ref[...] = rest


def momentum(moments, grad):
    total, _, width = moments.shape
    rows_pad = grad.shape[0]
    block = rows_pad // 4
    slab_spec = pl.BlockSpec((block, 1, width), lambda i: (i, 0, 0))
    flat_spec = pl.BlockSpec((block, width), lambda i: (i, 0))
    return call(
        functools.partial(momentum_body, total),
        "momentum",
        grid=(4,),
        in_specs=[slab_spec, flat_spec],
        out_specs=[slab_spec, flat_spec, flat_spec],
        out_shape=[
            jax.ShapeDtypeStruct(moments.shape, f32),
            jax.ShapeDtypeStruct((rows_pad, width), low),
            jax.ShapeDtypeStruct((rows_pad, width), low),
        ],
    )(moments, grad)


def momentum_again_body(total, moment_ref, grad_ref, *refs):
    momentum_body(total, moment_ref, grad_ref, *refs[-3:])


def momentum_again(moments, grad, first, top, rest, *others):
    total, _, width = moments.shape
    rows = grad.shape[0]
    slab_spec = pl.BlockSpec((rows, 1, width), lambda i: (i, 0, 0))
    flat_spec = pl.BlockSpec((rows, width), lambda i: (i, 0))
    return call(
        functools.partial(momentum_again_body, total),
        "momentum_again",
        grid=(1,),
        in_specs=[slab_spec, flat_spec] + [pl.BlockSpec(memory_space=pl.ANY)] * (3 + len(others)),
        out_specs=[slab_spec, flat_spec, flat_spec],
        out_shape=[jax.ShapeDtypeStruct(x.shape, x.dtype) for x in (first, top, rest)],
        input_output_aliases={2: 0, 3: 1, 4: 2},
    )(moments, grad, first, top, rest, *others)


def packed_at(column):
    return 128 * (column * (column + 1) // 2)


def upper(width):
    for j in range(0, width, 256):
        for i in range(0, min(j + 256, width), 256):
            yield i, j, pl.ds(i, min(256, width - i)), pl.ds(j, min(256, width - j))


def gram_body(top_ref, rest_ref, out_ref):
    for i, j, rows, columns in upper(top_ref.shape[1]):
        value = (
            dot(top_ref[:, rows], top_ref[:, columns], (0, 0))
            + dot(top_ref[:, rows], rest_ref[:, columns], (0, 0))
            + dot(rest_ref[:, rows], top_ref[:, columns], (0, 0))
        )
        for c in range(j // 128, (j + value.shape[1]) // 128):
            used = min(value.shape[0], 128 * (c + 1) - i)
            lanes = 128 * c - j
            out_ref[pl.ds(packed_at(c) + i, used), :] = value[:used, lanes : lanes + 128]


def gram_of(top, rest):
    count = top.shape[1] // 128
    return call(
        gram_body,
        "gram",
        in_specs=[pl.BlockSpec(memory_space=pltpu.VMEM)] * 2,
        out_specs=pl.BlockSpec(memory_space=pltpu.VMEM),
        out_shape=jax.ShapeDtypeStruct((packed_at(count), 128), f32),
    )(top, rest)


class Iterate:
    def __init__(self, a_top, a_rest, b_top, t_top, t_rest, x_ref):
        self.a = a_top, a_rest
        self.b = b_top
        self.t = t_top, t_rest
        self.x = x_ref
        self.width = a_top.shape[0]
        self.step = x_ref.shape[0] // 4
        self.diagonal = lax.broadcasted_iota(jnp.int32, (128, 128), 0) == lax.broadcasted_iota(
            jnp.int32, (128, 128), 1
        )

    def put(self, i, j, value):
        tall, wide = value.shape
        for x, rows, columns in ((value, pl.ds(i, tall), pl.ds(j, wide)),) + (
            ((value.T, pl.ds(j, wide), pl.ds(i, tall)),) if i != j else ()
        ):
            top, rest = split(x)
            self.a[0][rows, columns] = top
            self.a[1][rows, columns] = rest

    def both(self, pair, rows, columns):
        return pair[0][rows, columns].astype(f32) + pair[1][rows, columns].astype(f32)

    def symmetric(self, left, rights, finish):
        for i, j, rows, columns in upper(self.width):
            value = dot(left[rows, :], rights[0][:, columns], (1, 0))
            for right in rights[1:]:
                value = value + dot(left[rows, :], right[:, columns], (1, 0))
            finish(i, j, rows, columns, value)

    def recenter(self, center):
        total = jnp.zeros((128, 128), f32)
        for c in range(0, self.width, 128):
            at = pl.ds(c, 128)
            total = total + jnp.where(self.diagonal, self.both(self.a, at, at), 0.0)
        mean = jnp.sum(total) / self.width
        for c in range(0, self.width, 128):
            at = pl.ds(c, 128)
            top, rest = split(self.both(self.a, at, at) - jnp.where(self.diagonal, mean, 0.0))
            self.a[0][at, at] = top
            self.a[1][at, at] = rest
        return center + mean

    def mix(self, center):
        def finish(i, j, rows, columns, value):
            value = (coef_b + 2.0 * coef_c * center) * self.both(
                self.a, rows, columns
            ) + coef_c * value
            self.b[rows, columns] = value.astype(low)
            if i != j:
                self.b[columns, rows] = value.T.astype(low)

        self.symmetric(self.a[0], (self.a[0],), finish)
        return coef_a + coef_b * center + coef_c * center * center

    def stepped(self, rows, lead):
        x = self.x[rows, :]
        return lead * x + dot(x.astype(low), self.b[...], (1, 0))

    def propagate(self, center, lead, passes):
        tall = self.width // 3

        @pl.loop(0, 3)
        def _(r):
            rows = pl.ds(r * tall, tall)
            value = lead * self.both(self.a, rows, slice(None)) + center * self.b[rows, :].astype(f32)
            for left in self.a[:passes]:
                value = value + dot(left[rows, :], self.b[...], (1, 0))
            top, rest = split(value)
            self.t[0][rows, :] = top
            self.t[1][rows, :] = rest

        def finish(i, j, rows, columns, value):
            carried = lead * self.both(self.t, rows, columns)
            carried = carried + lead * center * self.b[rows, columns].astype(f32)
            self.put(i, j, carried + value)

        self.symmetric(self.b, self.t[:passes], finish)
        return lead * lead * center

    def sweep(self, center, passes=2):
        center = self.recenter(center)
        lead = self.mix(center)

        @pl.loop(0, 4)
        def _(r):
            rows = pl.ds(r * self.step, self.step)
            self.x[rows, :] = self.stepped(rows, lead)

        return self.propagate(center, lead, passes)


def iterate_body(
    total,
    square_ref,
    rate_ref,
    gram_ref,
    full_hbm,
    top_hbm,
    rest_hbm,
    slab_hbm,
    first_ref,
    out_hbm,
    a_top,
    a_rest,
    b_top,
    t_top,
    t_rest,
    x_ref,
    slab_ref,
    sem,
):
    state = Iterate(a_top, a_rest, b_top, t_top, t_rest, x_ref)
    width, step = state.width, state.step
    rows_pad = x_ref.shape[0]
    fetch_full = pltpu.make_async_copy(full_hbm, t_rest, sem.at[0])
    fetch_top = pltpu.make_async_copy(top_hbm, b_top.at[pl.ds(0, rows_pad)], sem.at[1])
    fetch_rest = pltpu.make_async_copy(rest_hbm, t_top.at[pl.ds(0, rows_pad)], sem.at[2])
    fetch_slab = pltpu.make_async_copy(slab_hbm, slab_ref.at[pl.ds(0, total)], sem.at[3])
    for fetch in (fetch_full, fetch_top, fetch_rest, fetch_slab):
        fetch.start()
    is_square = square_ref[0] == 1
    trace = jnp.zeros((128, 128), f32)
    for c in range(width // 128):
        block = gram_ref[pl.ds(packed_at(c) + 128 * c, 128), :]
        trace = trace + jnp.where(state.diagonal, block, 0.0)
    fetch_full.wait()

    def add_squares(r, sums):
        part = t_rest[pl.ds(r * 128, 128), :].astype(f32)
        return sums + jnp.sum(part * part, axis=0, keepdims=True)

    squares = lax.fori_loop(0, width // 128, add_squares, jnp.zeros((1, width), f32))
    norm = jnp.sqrt(jnp.where(is_square, jnp.sum(squares), jnp.sum(trace)))
    scaling = 1.0 / (norm + 1e-07)
    scale_two = scaling * scaling

    @pl.when(is_square)
    def _():
        for i, j, rows, columns in upper(width):
            state.put(i, j, dot(t_rest[:, rows], t_rest[:, columns], (0, 0)) * scale_two)

    @pl.when(jnp.logical_not(is_square))
    def _():
        for c in range(width // 128):
            for r in range(c + 1):
                block = gram_ref[pl.ds(packed_at(c) + 128 * r, 128), :]
                state.put(128 * r, 128 * c, block * scale_two)

    fetch_top.wait()
    fetch_rest.wait()
    rest_scaling = jnp.where(is_square, 0.0, scaling)

    @pl.loop(0, 4)
    def _(r):
        rows = pl.ds(r * step, step)
        x_ref[rows, :] = b_top[rows, :].astype(f32) * scaling + t_top[rows, :].astype(f32) * rest_scaling

    center = lax.fori_loop(
        0, NS_ITERS - 2, lambda _, center: state.sweep(center), jnp.float32(0.0)
    )
    center = state.sweep(center, 1)
    lead = state.mix(state.recenter(center))
    fetch_slab.wait()
    rate = rate_ref[0]

    @pl.loop(0, 4)
    def _(r):
        rows = pl.ds(r * step, step)
        new = slab_ref[rows, 0, :] * (1.0 - matrix_rate * matrix_decay) - rate * state.stepped(rows, lead)
        slab_ref[rows, :, :] = new.reshape(step, 1, width)

    leave = pltpu.make_async_copy(slab_ref.at[pl.ds(0, total)], out_hbm, sem.at[0])
    leave.start()
    leave.wait()


def iterate(square, rate, gram, full, top, rest, slab, first):
    total, _, width = slab.shape
    rows_pad = top.shape[0]
    vmem, smem = pl.BlockSpec(memory_space=pltpu.VMEM), pl.BlockSpec(memory_space=pltpu.SMEM)
    far = pl.BlockSpec(memory_space=pl.ANY)
    return call(
        functools.partial(iterate_body, total),
        "iterate",
        vmem=56,
        in_specs=[smem, smem, vmem] + [far] * 5,
        out_specs=far,
        out_shape=jax.ShapeDtypeStruct(slab.shape, f32),
        scratch_shapes=[pltpu.VMEM((width, width), low)] * 5
        + [
            pltpu.VMEM((rows_pad, width), f32),
            pltpu.VMEM((rows_pad, 1, width), f32),
            pltpu.SemaphoreType.DMA((4,)),
        ],
        cost_estimate=pl.CostEstimate(
            flops=80_000_000_000, bytes_accessed=20_000_000, transcendentals=0
        ),
    )(square, rate, gram, full, top, rest, slab, first)


def attend_body(scale, qkv_ref, context_ref, soft_ref):
    query, key, value = qkv_ref[0, 0], qkv_ref[1, 0], qkv_ref[2, 0]
    scores = dot(key, query, (0, 0)) * scale
    at = lax.broadcasted_iota(jnp.int32, scores.shape, 0)
    scores = jnp.where(at < LEN, scores, -1e30)
    exponent = jnp.exp(scores - jnp.max(scores, axis=0, keepdims=True))
    soft = (exponent / jnp.sum(exponent, axis=0, keepdims=True)).astype(low)
    soft_ref[0] = soft
    context = dot(value, soft, (1, 0))
    context_ref[0] = context[: context_ref.shape[1]].astype(low)


def attend(qkv, head_size, scale):
    _, groups, head_pad, rows = qkv.shape
    return call(
        functools.partial(attend_body, scale),
        "attend",
        grid=(groups,),
        in_specs=[pl.BlockSpec((3, 1, head_pad, rows), lambda h: (0, h, 0, 0))],
        out_specs=[
            pl.BlockSpec((1, head_size, rows), lambda h: (h, 0, 0)),
            pl.BlockSpec((1, rows, rows), lambda h: (h, 0, 0)),
        ],
        out_shape=[
            jax.ShapeDtypeStruct((groups, head_size, rows), low),
            jax.ShapeDtypeStruct((groups, rows, rows), low),
        ],
    )(qkv)


def attend_back_body(scale, qkv_ref, soft_ref, grad_ref, first_ref, other_ref, out_ref):
    query, key, value = qkv_ref[0, 0], qkv_ref[1, 0], qkv_ref[2, 0]
    grad, soft = grad_ref[0], soft_ref[0]
    grad_soft = dot(value, grad, (0, 0))
    soft_f32 = soft.astype(f32)
    along = jnp.sum(soft_f32 * grad_soft, axis=0, keepdims=True)
    grad_scores = (soft_f32 * (grad_soft - along)).astype(low)
    out_ref[0, 0] = (dot(key, grad_scores, (1, 0)) * scale).astype(low)
    out_ref[1, 0] = (dot(query, grad_scores, (1, 1)) * scale).astype(low)
    out_ref[2, 0] = dot(grad, soft, (1, 1)).astype(low)


def attend_back(qkv, soft, grad, first, other, scale):
    _, groups, head_pad, rows = qkv.shape
    three = pl.BlockSpec((3, 1, head_pad, rows), lambda h: (0, h, 0, 0))
    return call(
        functools.partial(attend_back_body, scale),
        "attend_back",
        grid=(groups,),
        in_specs=[
            three,
            pl.BlockSpec((1, rows, rows), lambda h: (h, 0, 0)),
            pl.BlockSpec((1, head_pad, rows), lambda h: (h, 0, 0)),
            pl.BlockSpec(memory_space=pl.ANY),
            pl.BlockSpec(memory_space=pl.ANY),
        ],
        out_specs=three,
        out_shape=jax.ShapeDtypeStruct(qkv.shape, low),
    )(qkv, soft, grad, first, other)


def whiten(inputs):
    average = jnp.mean(inputs, axis=-1, keepdims=True)
    centered = inputs - average
    variance = jnp.mean(centered * centered, axis=-1, keepdims=True)
    inverse = lax.rsqrt(variance + norm_eps)
    return centered * inverse, inverse


def whiten_back(grad, gain_row, hat, inverse):
    scaled = grad * gain_row
    mean_one = jnp.mean(scaled, axis=-1, keepdims=True)
    mean_two = jnp.mean(scaled * hat, axis=-1, keepdims=True)
    return inverse * (scaled - mean_one - hat * mean_two)


def gelu_both(inputs):
    squared = inputs * inputs
    curve = jnp.tanh(0.7978845608028654 * (inputs + 0.044715 * inputs * squared))
    value = 0.5 * inputs * (1.0 + curve)
    slope = 0.5 * (1.0 + curve) + 0.5 * inputs * (1.0 - curve * curve) * 0.7978845608028654 * (
        1.0 + 3.0 * 0.044715 * squared
    )
    return value, slope


def product(form, left, right):
    return jnp.einsum(form, left, right, preferred_element_type=f32)


def flip(x, axis, mask):
    count = lax.axis_size(axis)
    return lax.ppermute(x, axis, [(i, i ^ mask) for i in range(count)])


def gather_chunks(piece, first):
    count = lax.axis_size("dp")
    half = count // 2
    me = lax.axis_index("dp")
    pair, core = me >> 1, me & 1
    whole = jnp.zeros((half, 2) + piece.shape, piece.dtype)
    for mask, part in enumerate(exchange(piece, first)):
        whole = lax.dynamic_update_slice(whole, part[None, None], (pair ^ mask, core, 0, 0))
    mine = lax.dynamic_slice_in_dim(whole, core, 1, 1)
    other = flip(mine, "dp", 1)
    whole = lax.dynamic_update_slice_in_dim(whole, other, 1 - core, 1)
    return whole.reshape((count,) + piece.shape)


def scatter_sum(whole, order):
    count, rows, columns = whole.shape
    bits = count.bit_length() - 1
    me = lax.axis_index("dp")
    whole = whole.reshape((2,) * bits + (rows, columns))
    for bit in order:
        at = bits - 1 - bit
        mine = (me >> bit) & 1
        kept = lax.dynamic_slice_in_dim(whole, mine, 1, at)
        sent = lax.dynamic_slice_in_dim(whole, 1 - mine, 1, at)
        got = flip(sent, "dp", 1 << bit)
        whole = (kept.astype(f32) + got.astype(f32)).astype(low)
    return whole.reshape(rows, columns)


def arrivals(piece):
    count = lax.axis_size("seq")
    return [
        lax.ppermute(piece, "seq", [(i, (i + shift) % count) for i in range(count)])
        for shift in range(1, count)
    ]


def gather_seq(piece):
    count = lax.axis_size("seq")
    me = lax.axis_index("seq")
    whole = jnp.zeros((count,) + piece.shape, piece.dtype)
    for shift, part in enumerate([piece] + arrivals(piece)):
        whole = lax.dynamic_update_slice_in_dim(whole, part[None], (me - shift) % count, 0)
    return whole


def total_sum(x):
    for axis in ("dp", "seq"):
        step = 1
        while step < lax.axis_size(axis):
            x = x + flip(x, axis, step)
            step *= 2
    return x


def zero_of(token):
    return jnp.minimum(jnp.abs(token), 0.0)


def after(x, token):
    return x + zero_of(token).astype(x.dtype)


def touch_body(*refs):
    pass


def touch(arrays, *others):
    far = pl.BlockSpec(memory_space=pl.ANY)
    count = len(arrays)
    return call(
        touch_body,
        "touch",
        in_specs=[far] * (count + len(others)),
        out_specs=[far] * count,
        out_shape=[jax.ShapeDtypeStruct(x.shape, x.dtype) for x in arrays],
        input_output_aliases={i: i for i in range(count)},
    )(*arrays, *others)


def relative(me, count):
    place = jnp.arange(count)
    half = count // 2
    return me ^ ((place % half) * 2 + place // half)


def exchange(piece, first=None):
    half = lax.axis_size("dp") // 2
    arrived = [flip(piece, "dp", mask << 1) for mask in range(1, half)]
    return [piece] + ([after(x, first) for x in arrived] if first is not None else arrived)


def gather_relative(pieces, first=None):
    arrived = exchange(jnp.concatenate(pieces, axis=0), first)
    result, at = [], 0
    for piece in pieces:
        rows = piece.shape[0]
        mine = jnp.concatenate([x[at : at + rows] for x in arrived], axis=0)
        result.append(jnp.concatenate([mine, flip(mine, "dp", 1)], axis=0))
        at += rows
    return result


def scatter_relative(whole, order):
    count = lax.axis_size("dp")
    bits = count.bit_length() - 1
    rows, columns = whole.shape[0] // count, whole.shape[1]
    whole = whole.reshape((2,) * bits + (rows, columns))
    for bit in order:
        at = 0 if bit == 0 else bits - bit
        kept = lax.slice_in_dim(whole, 0, 1, axis=at)
        got = flip(lax.slice_in_dim(whole, 1, 2, axis=at), "dp", 1 << bit)
        whole = (kept.astype(f32) + got.astype(f32)).astype(low)
    return whole.reshape(rows, columns)


def local(
    tokens, cotangent, counts, owner_table, owned_weights, owned_moments, vectors, vector_moments
):
    seq_count = lax.axis_size("seq")
    dp_count = lax.axis_size("dp")
    bits = dp_count.bit_length() - 1
    seq_index = lax.axis_index("seq")
    dp_index = lax.axis_index("dp")
    capacity = tokens.shape[1]
    width = tokens.shape[2]
    slots = capacity * seq_count
    head_size = width // HEADS
    head_pad = -(-head_size // 16) * 16
    heads = HEADS // seq_count
    score_scale = 1.0 / math.sqrt(head_size)
    widths = (width, width, width, width, FF, FF)
    cols = width // seq_count
    ff_cols = FF // seq_count
    share = -(-LEN // (16 * seq_count)) * 16
    packed = share * seq_count
    square_rows = heads * head_pad
    square_chunk = -(-square_rows // (8 * dp_count)) * 8
    square_total = square_chunk * dp_count
    wide_chunk = -(-ff_cols // (8 * dp_count)) * 8
    wide_rows = wide_chunk * dp_count
    orders = (tuple(range(bits)), (0,) + tuple(range(bits - 1, 0, -1)))

    rows_in = tokens[0]
    vector_count = vectors.shape[0]
    vector_rows = -(-vector_count // width)
    extra = -(-vector_rows // 16) * 16
    payload = jnp.pad(vectors, (0, extra * width - vector_count)).reshape(extra, width)
    own_ids = jnp.arange(capacity)[:, None]
    own_valid = (own_ids < lax.dynamic_index_in_dim(counts[0], seq_index, 0)).astype(f32)
    cot_own = (cotangent[0] * own_valid).astype(low)
    payload = jnp.concatenate([rows_in.astype(low), payload.astype(low), cot_own], axis=0)
    gathered = lax.all_gather(payload, "seq", axis=0, tiled=False)
    token_slots = gathered[:, : capacity + extra].reshape(seq_count * (capacity + extra), width)
    cot_slots = gathered[:, capacity + extra :].reshape(slots, width)

    counts_row = counts[0]
    starts = jnp.cumsum(counts_row) - counts_row

    def rows_of(per):
        ids = jnp.arange(per * seq_count)
        real = (ids % per) < jnp.repeat(counts_row, per)
        return jnp.where(real, jnp.repeat(starts, per) + ids % per, packed)

    def picks(row):
        return (jnp.arange(packed)[:, None] == row[None, :]).astype(low)

    slot_row = rows_of(capacity)
    token_pick = picks(rows_of(capacity + extra))
    own_row = lax.dynamic_slice_in_dim(slot_row, seq_index * capacity, capacity)
    own_pick = picks(own_row)
    grad_rows = product("rc,cd->rd", picks(slot_row), cot_slots).astype(low)

    slab = jnp.transpose(owned_weights[0], (2, 1, 0))
    moments = jnp.transpose(owned_moments[0], (2, 1, 0))

    def send(x):
        return lax.all_to_all(x, "dp", split_axis=0, concat_axis=0, tiled=True)

    square_own = prep_square(slab, payload, heads, head_size, head_pad)
    near = jnp.stack(exchange(square_own))
    far = flip(near, "dp", 1)
    squares = []
    for m in range(4):
        away = owner_table[m] ^ dp_index
        from_near = lax.dynamic_index_in_dim(near, away >> 1, 0, keepdims=False)
        from_far = lax.dynamic_index_in_dim(far, away >> 1, 0, keepdims=False)
        squares.append(jnp.where((away & 1) == 0, from_near, from_far))
    w_qkv = jnp.concatenate(squares[:3], axis=0)
    w_out_piece = jnp.pad(squares[3], ((0, square_total - square_rows), (0, 0)))
    w_out_piece = lax.dynamic_slice_in_dim(w_out_piece, dp_index * square_chunk, square_chunk)
    w_out_part = gather_seq(w_out_piece).reshape(seq_count * square_chunk, width)
    wide_sent = prep_wide(slab, wide_rows).reshape(dp_count, wide_chunk, width)
    got_wide = send(wide_sent)
    wide_pieces = [lax.dynamic_index_in_dim(got_wide, owner_table[m], 0, keepdims=False) for m in (4, 5)]

    w_up, w_down = gather_relative(wide_pieces)

    vector_full = gathered[:, capacity : capacity + vector_rows].reshape(seq_count, -1)
    vector_full = vector_full[:, :vector_count].reshape(-1).astype(f32)
    row_params = vector_full[: 8 * width].reshape(8, width)
    up_bias = lax.dynamic_slice_in_dim(vector_full, 8 * width + seq_index * ff_cols, ff_cols)
    up_bias = jnp.pad(up_bias, (0, wide_rows - ff_cols)).reshape(dp_count, wide_chunk)
    up_bias = jnp.take(up_bias, relative(dp_index, dp_count), axis=0).reshape(wide_rows)

    def head_bias(row):
        own = lax.dynamic_slice_in_dim(row, seq_index * cols, cols).reshape(heads, head_size)
        return jnp.pad(own, ((0, 0), (0, head_pad - head_size))).reshape(square_rows)

    qkv_bias = jnp.concatenate(
        [head_bias(row_params[2]), jnp.zeros((square_rows,), f32), head_bias(row_params[3])]
    )

    token_rows = product("rc,cd->rd", token_pick, token_slots)
    hat_packed = whiten(token_rows)[0]
    normed = (hat_packed * row_params[0] + row_params[1]).astype(low)
    qkv_bias = after(qkv_bias, w_up[0, 0] + w_down[0, 0] + grad_rows[0, 0] + w_out_part[0, 0])
    qkv = (product("ed,rd->er", w_qkv, normed) + qkv_bias[:, None]).astype(low)
    qkv = qkv.reshape(3, heads, head_pad, packed)
    context_own, soft = attend(qkv, head_size, score_scale)
    token = context_own[0, 0, 0]
    w_out = gather_chunks(w_out_part, token)
    w_out = w_out.reshape(dp_count, seq_count, square_chunk, width).transpose(1, 0, 2, 3)
    w_out = w_out.reshape(seq_count, square_total, width)[:, :square_rows]
    w_out = w_out.reshape(seq_count * heads, head_pad, width)[:, :head_size].reshape(width, width)
    w_out_own = lax.dynamic_slice_in_dim(w_out, seq_index * cols, cols, axis=1)
    w_out_own = jnp.pad(
        w_out_own.reshape(width, heads, head_size), ((0, 0), (0, 0), (0, head_pad - head_size))
    ).reshape(width, square_rows)
    context = lax.all_gather(context_own.reshape(cols, packed), "seq", axis=0, tiled=True)
    middle = token_rows + product("er,oe->ro", context, w_out) + row_params[4]
    hat_two, inverse_two = whiten(middle)
    normed_two = (hat_two * row_params[5] + row_params[6]).astype(low)
    pre_act = product("rd,fd->rf", normed_two, w_up) + up_bias
    hidden_f32, slope = gelu_both(pre_act)
    hidden = hidden_f32.astype(low)

    grad_hidden = product("rd,fd->rf", grad_rows, w_down)
    grad_pre = (slope * grad_hidden).astype(low)
    grad_down = product("rf,rd->fd", hidden, grad_rows).astype(low)
    grad_up = product("rf,rd->fd", grad_pre, normed_two).astype(low)
    grad_normed_two_part = (
        product("rf,fd->rd", grad_pre, w_up) + zero_of(grad_down[0, 0] + grad_up[0, 0]).astype(f32)
    ).astype(low)
    grad_up_bias = jnp.sum(grad_pre.astype(f32), axis=0).reshape(dp_count, wide_chunk)
    back = jnp.arange(dp_count) ^ dp_index
    grad_up_bias = jnp.take(grad_up_bias, (back & 1) * (dp_count // 2) + (back >> 1), axis=0)
    grad_up_bias = grad_up_bias.reshape(wide_rows)[:ff_cols]

    sum_down = scatter_relative(grad_down, orders[0])
    sum_up = scatter_relative(grad_up, orders[1])
    def to_owner(pairs):
        total = 0
        for piece, m in pairs:
            here = (jnp.arange(dp_count) == owner_table[m])[:, None, None]
            total = total + jnp.where(here, piece[None], jnp.zeros((), low))
        return total

    wide_back = to_owner([(sum_up, 4), (sum_down, 5)])
    grad_normed_two = after(
        lax.psum_scatter(grad_normed_two_part, "seq", scatter_dimension=0, tiled=True),
        wide_back[0, 0, 0],
    ).astype(f32)
    back_wide = send(wide_back).reshape(wide_rows, width)
    def own_share(x):
        return lax.dynamic_slice_in_dim(x, seq_index * share, share)

    own_grad = own_share(grad_rows).astype(f32)
    own_hat = own_share(hat_two)
    grad_bias_down = jnp.sum(own_grad, axis=0)
    grad_gain_two = jnp.sum(grad_normed_two * own_hat, axis=0)
    grad_shift_two = jnp.sum(grad_normed_two, axis=0)
    grad_mid_norm = whiten_back(grad_normed_two, row_params[5], own_hat, own_share(inverse_two))
    grad_attn_own = (own_grad + grad_mid_norm).astype(low)
    grad_bias_out = jnp.sum(grad_attn_own.astype(f32), axis=0)
    grad_attn = lax.all_gather(grad_attn_own, "seq", axis=0, tiled=True)
    unpick = (slot_row[:, None] == jnp.arange(packed)[None, :]).astype(low)
    placed_middle = jnp.where(
        (jnp.arange(packed) // share == seq_index)[:, None], middle + row_params[7], 0.0
    )
    out_part = (
        product("rf,fd->rd", hidden, w_down) + placed_middle + zero_of(grad_attn_own[0, 0]).astype(f32)
    ).astype(low)
    out_slots = product("cr,rd->cd", unpick, out_part).astype(low)
    first_moment, top, rest = momentum(moments, back_wide)
    wide_gram = gram_of(top, rest)
    gram_share = lax.psum_scatter(wide_gram, "seq", scatter_dimension=0, tiled=True)
    first_gram = lax.all_gather(gram_share, "seq", axis=0, tiled=True)


    grad_context = product("de,rd->er", w_out_own, grad_attn).astype(low)
    grad_qkv = attend_back(qkv, soft, grad_context.reshape(heads, head_pad, packed), wide_gram, out_slots, score_scale)
    grad_qkv_flat = grad_qkv.reshape(3 * square_rows, packed)
    grad_attn_cols = lax.dynamic_slice_in_dim(grad_attn, seq_index * cols, cols, axis=1)
    grad_w_out = product("rd,er->de", grad_attn_cols, context)
    grad_w_qkv = product("er,rd->ed", grad_qkv_flat, normed)
    grad_qkv_bias = jnp.sum(grad_qkv.astype(f32), axis=3)[:, :, :head_size].reshape(3, cols)

    grad_normed_part = product("er,ed->rd", grad_qkv_flat, w_qkv)
    grad_gain_one = jnp.sum(grad_normed_part * hat_packed, axis=0)
    grad_shift_one = jnp.sum(grad_normed_part, axis=0)
    grad_normed_slots = product("cr,rd->cd", unpick, grad_normed_part.astype(low)).astype(low)

    grad_mid_slots = product("rc,rd->cd", own_pick, grad_attn)

    def square_parts(x):
        x = jnp.pad(x.astype(low), ((0, square_total - square_rows), (0, 0)))
        return x.reshape(dp_count, square_chunk, width)

    late = [square_parts(grad_w_qkv[m * square_rows : (m + 1) * square_rows]) for m in range(3)]
    grad_w_out = jnp.pad(
        grad_w_out.reshape(heads, head_size, width), ((0, 0), (0, head_pad - head_size), (0, 0))
    )
    late.append(square_parts(grad_w_out.reshape(square_rows, width)))
    sum_qk = scatter_sum(jnp.concatenate(late[:2], axis=1), orders[0])
    sum_vo = scatter_sum(jnp.concatenate(late[2:], axis=1), orders[1])
    square_back = to_owner(
        [
            (sum_qk[:square_chunk], 0),
            (sum_qk[square_chunk:], 1),
            (sum_vo[:square_chunk], 2),
            (sum_vo[square_chunk:], 3),
        ]
    )
    back_square = send(after(square_back, gram_share[0, 0])).reshape(square_total, width)[:square_rows]
    back_square = back_square.reshape(heads, head_pad, width)[:, :head_size].reshape(cols, width)
    first_moment, top, rest = momentum_again(
        moments, back_wide[:cols] + back_square, first_moment, top, rest, grad_normed_slots, grad_mid_slots
    )
    def spot(piece):
        return lax.dynamic_update_slice_in_dim(
            jnp.zeros((piece.shape[0] * seq_count,), f32), piece, seq_index * piece.shape[0], 0
        )

    vector_grad = jnp.concatenate(
        [
            grad_gain_one,
            grad_shift_one,
            spot(grad_qkv_bias[0]),
            spot(grad_qkv_bias[2]),
            grad_bias_out,
            grad_gain_two,
            grad_shift_two,
            grad_bias_down,
            spot(grad_up_bias),
        ]
    )
    padded = -(-vector_grad.shape[0] // 1024) * 1024
    vector_grad = jnp.pad(vector_grad, (0, padded - vector_grad.shape[0])).reshape(-1, 128)
    vector_block = total_sum(after(vector_grad, top[0, 0].astype(f32)))
    (direction,) = touch([top[:cols]], first_gram, vector_block)
    direction = lax.all_gather(direction, "seq", axis=0, tiled=True)
    is_square = jnp.any(owner_table[:4] == dp_index).astype(jnp.int32).reshape(1)
    grad_normed_slots, out_slots = touch([grad_normed_slots, out_slots], direction, first_gram)
    update_scale = jnp.zeros((), f32)
    for m in range(6):
        update_scale = jnp.where(
            owner_table[m] == dp_index,
            jnp.float32(matrix_rate * 0.2 * math.sqrt(max(width, widths[m]))),
            update_scale,
        )

    grad_normed = lax.psum_scatter(
        grad_normed_slots, "seq", scatter_dimension=0, tiled=True
    ).astype(f32)
    block_out = lax.psum_scatter(
        out_slots, "seq", scatter_dimension=0, tiled=True
    ).astype(f32)
    hat_one, inverse_one = whiten(rows_in)
    grad_in_norm = whiten_back(grad_normed, row_params[0], hat_one, inverse_one)
    grad_tokens = (grad_mid_slots + grad_in_norm) * own_valid

    vector_total = lax.dynamic_slice_in_dim(
        vector_block.reshape(-1), seq_index * vector_count, vector_count
    )
    updated = iterate(
        is_square, update_scale.reshape(1), first_gram, direction, top, rest, slab, vector_block
    )

    first_new = beta_first * vector_moments[0] + (1.0 - beta_first) * vector_total
    second_new = beta_second * vector_moments[1] + (1.0 - beta_second) * vector_total * vector_total
    first_fix = 1.0 - beta_first**STEP
    second_fix = 1.0 - beta_second**STEP
    vector_new = vectors - vector_rate * (first_new / first_fix) / (
        jnp.sqrt(second_new / second_fix) + adam_eps
    )
    return (
        block_out[None],
        grad_tokens[None],
        jnp.transpose(first_moment, (2, 1, 0))[None],
        jnp.transpose(updated, (2, 1, 0))[None],
        first_new,
        second_new,
        vector_new,
    )


def solution(mesh):
    in_specs = (
        P("dp", "seq", None),
        P("dp", "seq", None),
        P("dp", None),
        P(),
        P("dp", None, "seq", None),
        P("dp", None, "seq", None),
        P("seq"),
        P(None, "seq"),
    )
    out_specs = (
        P("dp", "seq", None),
        P("dp", "seq", None),
        P("dp", None, "seq", None),
        P("dp", None, "seq", None),
        P("seq"),
        P("seq"),
        P("seq"),
    )
    return jax.shard_map(local, mesh=mesh, in_specs=in_specs, out_specs=out_specs, check_vma=False)
```

```python
import functools
import math

import jax
import jax.numpy as jnp
from jax import lax
from jax.experimental import pallas as pl
from jax.experimental.pallas import tpu as pltpu
from jax.sharding import PartitionSpec as P

HEADS = 16
FF = 4304
LEN = 729
NS_ITERS = 5
STEP = 10

norm_eps = 1e-06
coef_a = 3.4445
coef_b = -4.775
coef_c = 2.0315
momentum_decay = 0.95
matrix_rate = 0.15
matrix_decay = 0.1
beta_first = 0.9
beta_second = 0.999
vector_rate = 0.5
adam_eps = 1e-08
low = jnp.bfloat16
f32 = jnp.float32


def call(body, name, **kw):
    vmem = kw.pop("vmem", 48)
    return pl.pallas_call(
        body,
        name=name,
        compiler_params=pltpu.CompilerParams(vmem_limit_bytes=vmem * 1024 * 1024),
        **kw,
    )


def dot(left, right, contract):
    return lax.dot_general(
        left, right, ((tuple(contract[:1]), tuple(contract[1:])), ((), ())), preferred_element_type=f32
    )


def split(x):
    top = x.astype(low)
    return top, (x - top.astype(f32)).astype(low)


def prep_square_body(slab_ref, first_ref, out_ref):
    rows = slab_ref[:, 0, :]
    extra = out_ref.shape[0] - rows.shape[0]
    padded = jnp.concatenate([rows, jnp.zeros((extra, rows.shape[1]), f32)], axis=0)
    out_ref[...] = padded.astype(low)


def prep_square(slab, first, heads, head_size, head_pad):
    width = slab.shape[2]
    return call(
        prep_square_body,
        "prep_square",
        grid=(heads,),
        in_specs=[
            pl.BlockSpec((head_size, 1, width), lambda i: (i, 0, 0)),
            pl.BlockSpec(memory_space=pl.ANY),
        ],
        out_specs=pl.BlockSpec((head_pad, width), lambda i: (i, 0)),
        out_shape=jax.ShapeDtypeStruct((heads * head_pad, width), low),
    )(slab, first)


def prep_wide_body(total, slab_ref, out_ref):
    rows = slab_ref[:, 0, :]
    at = pl.program_id(0) * rows.shape[0] + lax.broadcasted_iota(jnp.int32, rows.shape, 0)
    out_ref[...] = jnp.where(at < total, rows, 0.0).astype(low)


def prep_wide(slab, rows_pad):
    total, _, width = slab.shape
    block = rows_pad // 4
    return call(
        functools.partial(prep_wide_body, total),
        "prep_wide",
        grid=(4,),
        in_specs=[pl.BlockSpec((block, 1, width), lambda i: (i, 0, 0))],
        out_specs=pl.BlockSpec((block, width), lambda i: (i, 0)),
        out_shape=jax.ShapeDtypeStruct((rows_pad, width), low),
    )(slab)


def momentum_body(total, moment_ref, grad_ref, first_ref, top_ref, rest_ref):
    grad = grad_ref[...].astype(f32)
    first = momentum_decay * moment_ref[:, 0, :] + grad
    first_ref[...] = first.reshape(first_ref.shape)
    at = pl.program_id(0) * grad.shape[0] + lax.broadcasted_iota(jnp.int32, grad.shape, 0)
    top, rest = split(jnp.where(at < total, grad + momentum_decay * first, 0.0))
    top_ref[...] = top
    rest_ref[...] = rest


def momentum(moments, grad):
    total, _, width = moments.shape
    rows_pad = grad.shape[0]
    block = rows_pad // 4
    slab_spec = pl.BlockSpec((block, 1, width), lambda i: (i, 0, 0))
    flat_spec = pl.BlockSpec((block, width), lambda i: (i, 0))
    return call(
        functools.partial(momentum_body, total),
        "momentum",
        grid=(4,),
        in_specs=[slab_spec, flat_spec],
        out_specs=[slab_spec, flat_spec, flat_spec],
        out_shape=[
            jax.ShapeDtypeStruct(moments.shape, f32),
            jax.ShapeDtypeStruct((rows_pad, width), low),
            jax.ShapeDtypeStruct((rows_pad, width), low),
        ],
    )(moments, grad)


def momentum_again_body(total, moment_ref, grad_ref, *refs):
    momentum_body(total, moment_ref, grad_ref, *refs[-3:])


def momentum_again(moments, grad, first, top, rest, *others):
    total, _, width = moments.shape
    rows = grad.shape[0]
    slab_spec = pl.BlockSpec((rows, 1, width), lambda i: (i, 0, 0))
    flat_spec = pl.BlockSpec((rows, width), lambda i: (i, 0))
    return call(
        functools.partial(momentum_again_body, total),
        "momentum_again",
        grid=(1,),
        in_specs=[slab_spec, flat_spec] + [pl.BlockSpec(memory_space=pl.ANY)] * (3 + len(others)),
        out_specs=[slab_spec, flat_spec, flat_spec],
        out_shape=[jax.ShapeDtypeStruct(x.shape, x.dtype) for x in (first, top, rest)],
        input_output_aliases={2: 0, 3: 1, 4: 2},
    )(moments, grad, first, top, rest, *others)


def packed_at(column):
    return 128 * (column * (column + 1) // 2)


def upper(width):
    for j in range(0, width, 256):
        for i in range(0, min(j + 256, width), 256):
            yield i, j, pl.ds(i, min(256, width - i)), pl.ds(j, min(256, width - j))


def gram_body(top_ref, rest_ref, out_ref):
    for i, j, rows, columns in upper(top_ref.shape[1]):
        value = (
            dot(top_ref[:, rows], top_ref[:, columns], (0, 0))
            + dot(top_ref[:, rows], rest_ref[:, columns], (0, 0))
            + dot(rest_ref[:, rows], top_ref[:, columns], (0, 0))
        )
        for c in range(j // 128, (j + value.shape[1]) // 128):
            used = min(value.shape[0], 128 * (c + 1) - i)
            lanes = 128 * c - j
            out_ref[pl.ds(packed_at(c) + i, used), :] = value[:used, lanes : lanes + 128]


def gram_of(top, rest):
    count = top.shape[1] // 128
    return call(
        gram_body,
        "gram",
        in_specs=[pl.BlockSpec(memory_space=pltpu.VMEM)] * 2,
        out_specs=pl.BlockSpec(memory_space=pltpu.VMEM),
        out_shape=jax.ShapeDtypeStruct((packed_at(count), 128), f32),
    )(top, rest)


class Iterate:
    def __init__(self, a_top, a_rest, b_top, t_top, t_rest, x_ref):
        self.a = a_top, a_rest
        self.b = b_top
        self.t = t_top, t_rest
        self.x = x_ref
        self.width = a_top.shape[0]
        self.step = x_ref.shape[0] // 4
        self.diagonal = lax.broadcasted_iota(jnp.int32, (128, 128), 0) == lax.broadcasted_iota(
            jnp.int32, (128, 128), 1
        )

    def put(self, i, j, value):
        tall, wide = value.shape
        for x, rows, columns in ((value, pl.ds(i, tall), pl.ds(j, wide)),) + (
            ((value.T, pl.ds(j, wide), pl.ds(i, tall)),) if i != j else ()
        ):
            top, rest = split(x)
            self.a[0][rows, columns] = top
            self.a[1][rows, columns] = rest

    def both(self, pair, rows, columns):
        return pair[0][rows, columns].astype(f32) + pair[1][rows, columns].astype(f32)

    def symmetric(self, left, rights, finish):
        for i, j, rows, columns in upper(self.width):
            value = dot(left[rows, :], rights[0][:, columns], (1, 0))
            for right in rights[1:]:
                value = value + dot(left[rows, :], right[:, columns], (1, 0))
            finish(i, j, rows, columns, value)

    def recenter(self, center):
        total = jnp.zeros((128, 128), f32)
        for c in range(0, self.width, 128):
            at = pl.ds(c, 128)
            total = total + jnp.where(self.diagonal, self.both(self.a, at, at), 0.0)
        mean = jnp.sum(total) / self.width
        for c in range(0, self.width, 128):
            at = pl.ds(c, 128)
            top, rest = split(self.both(self.a, at, at) - jnp.where(self.diagonal, mean, 0.0))
            self.a[0][at, at] = top
            self.a[1][at, at] = rest
        return center + mean

    def mix(self, center):
        def finish(i, j, rows, columns, value):
            value = (coef_b + 2.0 * coef_c * center) * self.both(
                self.a, rows, columns
            ) + coef_c * value
            self.b[rows, columns] = value.astype(low)
            if i != j:
                self.b[columns, rows] = value.T.astype(low)

        self.symmetric(self.a[0], (self.a[0],), finish)
        return coef_a + coef_b * center + coef_c * center * center

    def stepped(self, rows, lead):
        x = self.x[rows, :]
        return lead * x + dot(x.astype(low), self.b[...], (1, 0))

    def propagate(self, center, lead, passes):
        tall = self.width // 3

        @pl.loop(0, 3)
        def _(r):
            rows = pl.ds(r * tall, tall)
            value = lead * self.both(self.a, rows, slice(None)) + center * self.b[rows, :].astype(f32)
            for left in self.a[:passes]:
                value = value + dot(left[rows, :], self.b[...], (1, 0))
            top, rest = split(value)
            self.t[0][rows, :] = top
            self.t[1][rows, :] = rest

        def finish(i, j, rows, columns, value):
            carried = lead * self.both(self.t, rows, columns)
            carried = carried + lead * center * self.b[rows, columns].astype(f32)
            self.put(i, j, carried + value)

        self.symmetric(self.b, self.t[:passes], finish)
        return lead * lead * center

    def sweep(self, center, passes=2):
        center = self.recenter(center)
        lead = self.mix(center)

        @pl.loop(0, 4)
        def _(r):
            rows = pl.ds(r * self.step, self.step)
            self.x[rows, :] = self.stepped(rows, lead)

        return self.propagate(center, lead, passes)


def iterate_body(
    total,
    square_ref,
    rate_ref,
    gram_ref,
    full_hbm,
    top_hbm,
    rest_hbm,
    slab_hbm,
    first_ref,
    out_hbm,
    a_top,
    a_rest,
    b_top,
    t_top,
    t_rest,
    x_ref,
    slab_ref,
    sem,
):
    state = Iterate(a_top, a_rest, b_top, t_top, t_rest, x_ref)
    width, step = state.width, state.step
    rows_pad = x_ref.shape[0]
    fetch_full = pltpu.make_async_copy(full_hbm, t_rest, sem.at[0])
    fetch_top = pltpu.make_async_copy(top_hbm, b_top.at[pl.ds(0, rows_pad)], sem.at[1])
    fetch_rest = pltpu.make_async_copy(rest_hbm, t_top.at[pl.ds(0, rows_pad)], sem.at[2])
    fetch_slab = pltpu.make_async_copy(slab_hbm, slab_ref.at[pl.ds(0, total)], sem.at[3])
    for fetch in (fetch_full, fetch_top, fetch_rest, fetch_slab):
        fetch.start()
    is_square = square_ref[0] == 1
    trace = jnp.zeros((128, 128), f32)
    for c in range(width // 128):
        block = gram_ref[pl.ds(packed_at(c) + 128 * c, 128), :]
        trace = trace + jnp.where(state.diagonal, block, 0.0)
    fetch_full.wait()

    def add_squares(r, sums):
        part = t_rest[pl.ds(r * 128, 128), :].astype(f32)
        return sums + jnp.sum(part * part, axis=0, keepdims=True)

    squares = lax.fori_loop(0, width // 128, add_squares, jnp.zeros((1, width), f32))
    norm = jnp.sqrt(jnp.where(is_square, jnp.sum(squares), jnp.sum(trace)))
    scaling = 1.0 / (norm + 1e-07)
    scale_two = scaling * scaling

    @pl.when(is_square)
    def _():
        for i, j, rows, columns in upper(width):
            state.put(i, j, dot(t_rest[:, rows], t_rest[:, columns], (0, 0)) * scale_two)

    @pl.when(jnp.logical_not(is_square))
    def _():
        for c in range(width // 128):
            for r in range(c + 1):
                block = gram_ref[pl.ds(packed_at(c) + 128 * r, 128), :]
                state.put(128 * r, 128 * c, block * scale_two)

    fetch_top.wait()
    fetch_rest.wait()
    rest_scaling = jnp.where(is_square, 0.0, scaling)

    @pl.loop(0, 4)
    def _(r):
        rows = pl.ds(r * step, step)
        x_ref[rows, :] = b_top[rows, :].astype(f32) * scaling + t_top[rows, :].astype(f32) * rest_scaling

    center = lax.fori_loop(
        0, NS_ITERS - 2, lambda _, center: state.sweep(center), jnp.float32(0.0)
    )
    center = state.sweep(center, 1)
    lead = state.mix(state.recenter(center))
    fetch_slab.wait()
    rate = rate_ref[0]

    @pl.loop(0, 4)
    def _(r):
        rows = pl.ds(r * step, step)
        new = slab_ref[rows, 0, :] * (1.0 - matrix_rate * matrix_decay) - rate * state.stepped(rows, lead)
        slab_ref[rows, :, :] = new.reshape(step, 1, width)

    leave = pltpu.make_async_copy(slab_ref.at[pl.ds(0, total)], out_hbm, sem.at[0])
    leave.start()
    leave.wait()


def iterate(square, rate, gram, full, top, rest, slab, first):
    total, _, width = slab.shape
    rows_pad = top.shape[0]
    vmem, smem = pl.BlockSpec(memory_space=pltpu.VMEM), pl.BlockSpec(memory_space=pltpu.SMEM)
    far = pl.BlockSpec(memory_space=pl.ANY)
    return call(
        functools.partial(iterate_body, total),
        "iterate",
        vmem=56,
        in_specs=[smem, smem, vmem] + [far] * 5,
        out_specs=far,
        out_shape=jax.ShapeDtypeStruct(slab.shape, f32),
        scratch_shapes=[pltpu.VMEM((width, width), low)] * 5
        + [
            pltpu.VMEM((rows_pad, width), f32),
            pltpu.VMEM((rows_pad, 1, width), f32),
            pltpu.SemaphoreType.DMA((4,)),
        ],
        cost_estimate=pl.CostEstimate(
            flops=80_000_000_000, bytes_accessed=20_000_000, transcendentals=0
        ),
    )(square, rate, gram, full, top, rest, slab, first)


def attend_body(scale, qkv_ref, context_ref, soft_ref):
    query, key, value = qkv_ref[0, 0], qkv_ref[1, 0], qkv_ref[2, 0]
    scores = dot(key, query, (0, 0)) * scale
    at = lax.broadcasted_iota(jnp.int32, scores.shape, 0)
    scores = jnp.where(at < LEN, scores, -1e30)
    exponent = jnp.exp(scores - jnp.max(scores, axis=0, keepdims=True))
    soft = (exponent / jnp.sum(exponent, axis=0, keepdims=True)).astype(low)
    soft_ref[0] = soft
    context = dot(value, soft, (1, 0))
    context_ref[0] = context[: context_ref.shape[1]].astype(low)


def attend(qkv, head_size, scale):
    _, groups, head_pad, rows = qkv.shape
    return call(
        functools.partial(attend_body, scale),
        "attend",
        grid=(groups,),
        in_specs=[pl.BlockSpec((3, 1, head_pad, rows), lambda h: (0, h, 0, 0))],
        out_specs=[
            pl.BlockSpec((1, head_size, rows), lambda h: (h, 0, 0)),
            pl.BlockSpec((1, rows, rows), lambda h: (h, 0, 0)),
        ],
        out_shape=[
            jax.ShapeDtypeStruct((groups, head_size, rows), low),
            jax.ShapeDtypeStruct((groups, rows, rows), low),
        ],
    )(qkv)


def attend_back_body(scale, qkv_ref, soft_ref, grad_ref, first_ref, other_ref, out_ref):
    query, key, value = qkv_ref[0, 0], qkv_ref[1, 0], qkv_ref[2, 0]
    grad, soft = grad_ref[0], soft_ref[0]
    grad_soft = dot(value, grad, (0, 0))
    soft_f32 = soft.astype(f32)
    along = jnp.sum(soft_f32 * grad_soft, axis=0, keepdims=True)
    grad_scores = (soft_f32 * (grad_soft - along)).astype(low)
    out_ref[0, 0] = (dot(key, grad_scores, (1, 0)) * scale).astype(low)
    out_ref[1, 0] = (dot(query, grad_scores, (1, 1)) * scale).astype(low)
    out_ref[2, 0] = dot(grad, soft, (1, 1)).astype(low)


def attend_back(qkv, soft, grad, first, other, scale):
    _, groups, head_pad, rows = qkv.shape
    three = pl.BlockSpec((3, 1, head_pad, rows), lambda h: (0, h, 0, 0))
    return call(
        functools.partial(attend_back_body, scale),
        "attend_back",
        grid=(groups,),
        in_specs=[
            three,
            pl.BlockSpec((1, rows, rows), lambda h: (h, 0, 0)),
            pl.BlockSpec((1, head_pad, rows), lambda h: (h, 0, 0)),
            pl.BlockSpec(memory_space=pl.ANY),
            pl.BlockSpec(memory_space=pl.ANY),
        ],
        out_specs=three,
        out_shape=jax.ShapeDtypeStruct(qkv.shape, low),
    )(qkv, soft, grad, first, other)


def whiten(inputs):
    average = jnp.mean(inputs, axis=-1, keepdims=True)
    centered = inputs - average
    variance = jnp.mean(centered * centered, axis=-1, keepdims=True)
    inverse = lax.rsqrt(variance + norm_eps)
    return centered * inverse, inverse


def whiten_back(grad, gain_row, hat, inverse):
    scaled = grad * gain_row
    mean_one = jnp.mean(scaled, axis=-1, keepdims=True)
    mean_two = jnp.mean(scaled * hat, axis=-1, keepdims=True)
    return inverse * (scaled - mean_one - hat * mean_two)


def gelu_both(inputs):
    squared = inputs * inputs
    curve = jnp.tanh(0.7978845608028654 * (inputs + 0.044715 * inputs * squared))
    value = 0.5 * inputs * (1.0 + curve)
    slope = 0.5 * (1.0 + curve) + 0.5 * inputs * (1.0 - curve * curve) * 0.7978845608028654 * (
        1.0 + 3.0 * 0.044715 * squared
    )
    return value, slope


def product(form, left, right):
    return jnp.einsum(form, left, right, preferred_element_type=f32)


def flip(x, axis, mask):
    count = lax.axis_size(axis)
    return lax.ppermute(x, axis, [(i, i ^ mask) for i in range(count)])


def gather_chunks(piece, first):
    count = lax.axis_size("dp")
    half = count // 2
    me = lax.axis_index("dp")
    pair, core = me >> 1, me & 1
    whole = jnp.zeros((half, 2) + piece.shape, piece.dtype)
    for mask, part in enumerate(exchange(piece, first)):
        whole = lax.dynamic_update_slice(whole, part[None, None], (pair ^ mask, core, 0, 0))
    mine = lax.dynamic_slice_in_dim(whole, core, 1, 1)
    other = flip(mine, "dp", 1)
    whole = lax.dynamic_update_slice_in_dim(whole, other, 1 - core, 1)
    return whole.reshape((count,) + piece.shape)


def scatter_sum(whole, order):
    count, rows, columns = whole.shape
    bits = count.bit_length() - 1
    me = lax.axis_index("dp")
    whole = whole.reshape((2,) * bits + (rows, columns))
    for bit in order:
        at = bits - 1 - bit
        mine = (me >> bit) & 1
        kept = lax.dynamic_slice_in_dim(whole, mine, 1, at)
        sent = lax.dynamic_slice_in_dim(whole, 1 - mine, 1, at)
        got = flip(sent, "dp", 1 << bit)
        whole = (kept.astype(f32) + got.astype(f32)).astype(low)
    return whole.reshape(rows, columns)


def arrivals(piece):
    count = lax.axis_size("seq")
    return [
        lax.ppermute(piece, "seq", [(i, (i + shift) % count) for i in range(count)])
        for shift in range(1, count)
    ]


def gather_seq(piece):
    count = lax.axis_size("seq")
    me = lax.axis_index("seq")
    whole = jnp.zeros((count,) + piece.shape, piece.dtype)
    for shift, part in enumerate([piece] + arrivals(piece)):
        whole = lax.dynamic_update_slice_in_dim(whole, part[None], (me - shift) % count, 0)
    return whole


def total_sum(x):
    for axis in ("dp", "seq"):
        step = 1
        while step < lax.axis_size(axis):
            x = x + flip(x, axis, step)
            step *= 2
    return x


def zero_of(token):
    return jnp.minimum(jnp.abs(token), 0.0)


def after(x, token):
    return x + zero_of(token).astype(x.dtype)


def touch_body(*refs):
    pass


def touch(arrays, *others):
    far = pl.BlockSpec(memory_space=pl.ANY)
    count = len(arrays)
    return call(
        touch_body,
        "touch",
        in_specs=[far] * (count + len(others)),
        out_specs=[far] * count,
        out_shape=[jax.ShapeDtypeStruct(x.shape, x.dtype) for x in arrays],
        input_output_aliases={i: i for i in range(count)},
    )(*arrays, *others)


def relative(me, count):
    place = jnp.arange(count)
    half = count // 2
    return me ^ ((place % half) * 2 + place // half)


def exchange(piece, first=None):
    half = lax.axis_size("dp") // 2
    arrived = [flip(piece, "dp", mask << 1) for mask in range(1, half)]
    return [piece] + ([after(x, first) for x in arrived] if first is not None else arrived)


def gather_relative(pieces, first=None):
    arrived = exchange(jnp.concatenate(pieces, axis=0), first)
    result, at = [], 0
    for piece in pieces:
        rows = piece.shape[0]
        mine = jnp.concatenate([x[at : at + rows] for x in arrived], axis=0)
        result.append(jnp.concatenate([mine, flip(mine, "dp", 1)], axis=0))
        at += rows
    return result


def scatter_relative(whole, order):
    count = lax.axis_size("dp")
    bits = count.bit_length() - 1
    rows, columns = whole.shape[0] // count, whole.shape[1]
    whole = whole.reshape((2,) * bits + (rows, columns))
    for bit in order:
        at = 0 if bit == 0 else bits - bit
        kept = lax.slice_in_dim(whole, 0, 1, axis=at)
        got = flip(lax.slice_in_dim(whole, 1, 2, axis=at), "dp", 1 << bit)
        whole = (kept.astype(f32) + got.astype(f32)).astype(low)
    return whole.reshape(rows, columns)


def local(
    tokens, cotangent, counts, owner_table, owned_weights, owned_moments, vectors, vector_moments
):
    seq_count = lax.axis_size("seq")
    dp_count = lax.axis_size("dp")
    bits = dp_count.bit_length() - 1
    seq_index = lax.axis_index("seq")
    dp_index = lax.axis_index("dp")
    capacity = tokens.shape[1]
    width = tokens.shape[2]
    slots = capacity * seq_count
    head_size = width // HEADS
    head_pad = -(-head_size // 16) * 16
    heads = HEADS // seq_count
    score_scale = 1.0 / math.sqrt(head_size)
    widths = (width, width, width, width, FF, FF)
    cols = width // seq_count
    ff_cols = FF // seq_count
    share = -(-LEN // (16 * seq_count)) * 16
    packed = share * seq_count
    square_rows = heads * head_pad
    square_chunk = -(-square_rows // (8 * dp_count)) * 8
    square_total = square_chunk * dp_count
    wide_chunk = -(-ff_cols // (8 * dp_count)) * 8
    wide_rows = wide_chunk * dp_count
    orders = (tuple(range(bits)), (0,) + tuple(range(bits - 1, 0, -1)))

    rows_in = tokens[0]
    vector_count = vectors.shape[0]
    vector_rows = -(-vector_count // width)
    extra = -(-vector_rows // 16) * 16
    payload = jnp.pad(vectors, (0, extra * width - vector_count)).reshape(extra, width)
    own_ids = jnp.arange(capacity)[:, None]
    own_valid = (own_ids < lax.dynamic_index_in_dim(counts[0], seq_index, 0)).astype(f32)
    cot_own = (cotangent[0] * own_valid).astype(low)
    payload = jnp.concatenate([rows_in.astype(low), payload.astype(low), cot_own], axis=0)
    gathered = lax.all_gather(payload, "seq", axis=0, tiled=False)

    counts_row = counts[0]
    starts = jnp.cumsum(counts_row) - counts_row

    def rows_of(per, skip=0):
        ids = jnp.arange(per * seq_count) % per - skip
        real = (ids >= 0) & (ids < jnp.repeat(counts_row, per))
        return jnp.where(real, jnp.repeat(starts, per) + ids, packed)

    def picks(row):
        return (jnp.arange(packed)[:, None] == row[None, :]).astype(low)

    slot_row = rows_of(capacity)
    token_pick = picks(rows_of(payload.shape[0]))
    cot_pick = picks(rows_of(payload.shape[0], capacity + extra))
    own_row = lax.dynamic_slice_in_dim(slot_row, seq_index * capacity, capacity)
    own_pick = picks(own_row)
    slab = jnp.transpose(owned_weights[0], (2, 1, 0))
    moments = jnp.transpose(owned_moments[0], (2, 1, 0))

    def send(x):
        return lax.all_to_all(x, "dp", split_axis=0, concat_axis=0, tiled=True)

    square_own = prep_square(slab, payload, heads, head_size, head_pad)
    near = jnp.stack(exchange(square_own))
    far = flip(near, "dp", 1)
    squares = []
    for m in range(4):
        away = owner_table[m] ^ dp_index
        from_near = lax.dynamic_index_in_dim(near, away >> 1, 0, keepdims=False)
        from_far = lax.dynamic_index_in_dim(far, away >> 1, 0, keepdims=False)
        squares.append(jnp.where((away & 1) == 0, from_near, from_far))
    w_qkv = jnp.concatenate(squares[:3], axis=0)
    w_out_piece = jnp.pad(squares[3], ((0, square_total - square_rows), (0, 0)))
    w_out_piece = lax.dynamic_slice_in_dim(w_out_piece, dp_index * square_chunk, square_chunk)
    w_out_part = gather_seq(w_out_piece).reshape(seq_count * square_chunk, width)
    wide_sent = prep_wide(slab, wide_rows).reshape(dp_count, wide_chunk, width)
    got_wide = send(wide_sent)
    wide_pieces = [lax.dynamic_index_in_dim(got_wide, owner_table[m], 0, keepdims=False) for m in (4, 5)]

    w_up, w_down = gather_relative(wide_pieces)
    (gathered,) = touch([gathered], w_up, w_down, w_out_part)
    gathered_rows = gathered.reshape(seq_count * payload.shape[0], width)
    grad_rows = product("rc,cd->rd", cot_pick, gathered_rows).astype(low)

    vector_full = gathered[:, capacity : capacity + vector_rows].reshape(seq_count, -1)
    vector_full = vector_full[:, :vector_count].reshape(-1).astype(f32)
    row_params = vector_full[: 8 * width].reshape(8, width)
    up_bias = lax.dynamic_slice_in_dim(vector_full, 8 * width + seq_index * ff_cols, ff_cols)
    up_bias = jnp.pad(up_bias, (0, wide_rows - ff_cols)).reshape(dp_count, wide_chunk)
    up_bias = jnp.take(up_bias, relative(dp_index, dp_count), axis=0).reshape(wide_rows)

    def head_bias(row):
        own = lax.dynamic_slice_in_dim(row, seq_index * cols, cols).reshape(heads, head_size)
        return jnp.pad(own, ((0, 0), (0, head_pad - head_size))).reshape(square_rows)

    qkv_bias = jnp.concatenate(
        [head_bias(row_params[2]), jnp.zeros((square_rows,), f32), head_bias(row_params[3])]
    )

    token_rows = product("rc,cd->rd", token_pick, gathered_rows)
    hat_packed = whiten(token_rows)[0]
    normed = (hat_packed * row_params[0] + row_params[1]).astype(low)
    qkv_bias = after(qkv_bias, grad_rows[0, 0])
    qkv = (product("ed,rd->er", w_qkv, normed) + qkv_bias[:, None]).astype(low)
    qkv = qkv.reshape(3, heads, head_pad, packed)
    context_own, soft = attend(qkv, head_size, score_scale)
    token = context_own[0, 0, 0]
    w_out = gather_chunks(w_out_part, token)
    w_out = w_out.reshape(dp_count, seq_count, square_chunk, width).transpose(1, 0, 2, 3)
    w_out = w_out.reshape(seq_count, square_total, width)[:, :square_rows]
    w_out = w_out.reshape(seq_count * heads, head_pad, width)[:, :head_size].reshape(width, width)
    w_out_own = lax.dynamic_slice_in_dim(w_out, seq_index * cols, cols, axis=1)
    w_out_own = jnp.pad(
        w_out_own.reshape(width, heads, head_size), ((0, 0), (0, 0), (0, head_pad - head_size))
    ).reshape(width, square_rows)
    context = lax.all_gather(context_own.reshape(cols, packed), "seq", axis=0, tiled=True)
    middle = token_rows + product("er,oe->ro", context, w_out) + row_params[4]
    hat_two, inverse_two = whiten(middle)
    normed_two = (hat_two * row_params[5] + row_params[6]).astype(low)
    pre_act = product("rd,fd->rf", normed_two, w_up) + up_bias
    hidden_f32, slope = gelu_both(pre_act)
    hidden = hidden_f32.astype(low)

    grad_hidden = product("rd,fd->rf", grad_rows, w_down)
    grad_pre = (slope * grad_hidden).astype(low)
    grad_down = product("rf,rd->fd", hidden, grad_rows).astype(low)
    grad_up = product("rf,rd->fd", grad_pre, normed_two).astype(low)
    grad_normed_two_part = (
        product("rf,fd->rd", grad_pre, w_up) + zero_of(grad_down[0, 0] + grad_up[0, 0]).astype(f32)
    ).astype(low)
    grad_up_bias = jnp.sum(grad_pre.astype(f32), axis=0).reshape(dp_count, wide_chunk)
    back = jnp.arange(dp_count) ^ dp_index
    grad_up_bias = jnp.take(grad_up_bias, (back & 1) * (dp_count // 2) + (back >> 1), axis=0)
    grad_up_bias = grad_up_bias.reshape(wide_rows)[:ff_cols]

    sum_down = scatter_relative(grad_down, orders[0])
    sum_up = scatter_relative(grad_up, orders[1])
    def to_owner(pairs):
        total = 0
        for piece, m in pairs:
            here = (jnp.arange(dp_count) == owner_table[m])[:, None, None]
            total = total + jnp.where(here, piece[None], jnp.zeros((), low))
        return total

    wide_back = to_owner([(sum_up, 4), (sum_down, 5)])
    grad_normed_two = after(
        lax.psum_scatter(grad_normed_two_part, "seq", scatter_dimension=0, tiled=True),
        wide_back[0, 0, 0],
    ).astype(f32)
    back_wide = send(wide_back).reshape(wide_rows, width)
    def own_share(x):
        return lax.dynamic_slice_in_dim(x, seq_index * share, share)

    own_grad = own_share(grad_rows).astype(f32)
    own_hat = own_share(hat_two)
    grad_bias_down = jnp.sum(own_grad, axis=0)
    grad_gain_two = jnp.sum(grad_normed_two * own_hat, axis=0)
    grad_shift_two = jnp.sum(grad_normed_two, axis=0)
    grad_mid_norm = whiten_back(grad_normed_two, row_params[5], own_hat, own_share(inverse_two))
    grad_attn_own = (own_grad + grad_mid_norm).astype(low)
    grad_bias_out = jnp.sum(grad_attn_own.astype(f32), axis=0)
    grad_attn = lax.all_gather(grad_attn_own, "seq", axis=0, tiled=True)
    unpick = (slot_row[:, None] == jnp.arange(packed)[None, :]).astype(low)
    placed_middle = jnp.where(
        (jnp.arange(packed) // share == seq_index)[:, None], middle + row_params[7], 0.0
    )
    out_part = (
        product("rf,fd->rd", hidden, w_down) + placed_middle + zero_of(grad_attn_own[0, 0]).astype(f32)
    ).astype(low)
    out_slots = product("cr,rd->cd", unpick, out_part).astype(low)
    first_moment, top, rest = momentum(moments, back_wide)
    wide_gram = gram_of(top, rest)
    gram_share = lax.psum_scatter(wide_gram, "seq", scatter_dimension=0, tiled=True)
    first_gram = lax.all_gather(gram_share, "seq", axis=0, tiled=True)


    grad_context = product("de,rd->er", w_out_own, grad_attn).astype(low)
    grad_qkv = attend_back(qkv, soft, grad_context.reshape(heads, head_pad, packed), wide_gram, out_slots, score_scale)
    grad_qkv_flat = grad_qkv.reshape(3 * square_rows, packed)
    grad_attn_cols = lax.dynamic_slice_in_dim(grad_attn, seq_index * cols, cols, axis=1)
    grad_w_out = product("rd,er->de", grad_attn_cols, context)
    grad_w_qkv = product("er,rd->ed", grad_qkv_flat, normed)
    grad_qkv_bias = jnp.sum(grad_qkv.astype(f32), axis=3)[:, :, :head_size].reshape(3, cols)

    grad_normed_part = product("er,ed->rd", grad_qkv_flat, w_qkv)
    grad_gain_one = jnp.sum(grad_normed_part * hat_packed, axis=0)
    grad_shift_one = jnp.sum(grad_normed_part, axis=0)
    grad_normed_slots = product("cr,rd->cd", unpick, grad_normed_part.astype(low)).astype(low)

    grad_mid_slots = product("rc,rd->cd", own_pick, grad_attn)

    def square_parts(x):
        x = jnp.pad(x.astype(low), ((0, square_total - square_rows), (0, 0)))
        return x.reshape(dp_count, square_chunk, width)

    late = [square_parts(grad_w_qkv[m * square_rows : (m + 1) * square_rows]) for m in range(3)]
    grad_w_out = jnp.pad(
        grad_w_out.reshape(heads, head_size, width), ((0, 0), (0, head_pad - head_size), (0, 0))
    )
    late.append(square_parts(grad_w_out.reshape(square_rows, width)))
    sum_qk = scatter_sum(jnp.concatenate(late[:2], axis=1), orders[0])
    sum_vo = scatter_sum(jnp.concatenate(late[2:], axis=1), orders[1])
    square_back = to_owner(
        [
            (sum_qk[:square_chunk], 0),
            (sum_qk[square_chunk:], 1),
            (sum_vo[:square_chunk], 2),
            (sum_vo[square_chunk:], 3),
        ]
    )
    back_square = send(after(square_back, gram_share[0, 0])).reshape(square_total, width)[:square_rows]
    back_square = back_square.reshape(heads, head_pad, width)[:, :head_size].reshape(cols, width)
    first_moment, top, rest = momentum_again(
        moments, back_wide[:cols] + back_square, first_moment, top, rest, grad_normed_slots, grad_mid_slots
    )
    def spot(piece):
        return lax.dynamic_update_slice_in_dim(
            jnp.zeros((piece.shape[0] * seq_count,), f32), piece, seq_index * piece.shape[0], 0
        )

    vector_grad = jnp.concatenate(
        [
            grad_gain_one,
            grad_shift_one,
            spot(grad_qkv_bias[0]),
            spot(grad_qkv_bias[2]),
            grad_bias_out,
            grad_gain_two,
            grad_shift_two,
            grad_bias_down,
            spot(grad_up_bias),
        ]
    )
    padded = -(-vector_grad.shape[0] // 1024) * 1024
    vector_grad = jnp.pad(vector_grad, (0, padded - vector_grad.shape[0])).reshape(-1, 128)
    vector_block = total_sum(after(vector_grad, top[0, 0].astype(f32)))
    (direction,) = touch([top[:cols]], first_gram, vector_block)
    direction = lax.all_gather(direction, "seq", axis=0, tiled=True)
    is_square = jnp.any(owner_table[:4] == dp_index).astype(jnp.int32).reshape(1)
    grad_normed_slots, out_slots = touch([grad_normed_slots, out_slots], direction, first_gram)
    update_scale = jnp.zeros((), f32)
    for m in range(6):
        update_scale = jnp.where(
            owner_table[m] == dp_index,
            jnp.float32(matrix_rate * 0.2 * math.sqrt(max(width, widths[m]))),
            update_scale,
        )

    grad_normed = lax.psum_scatter(
        grad_normed_slots, "seq", scatter_dimension=0, tiled=True
    ).astype(f32)
    block_out = lax.psum_scatter(
        out_slots, "seq", scatter_dimension=0, tiled=True
    ).astype(f32)
    hat_one, inverse_one = whiten(rows_in)
    grad_in_norm = whiten_back(grad_normed, row_params[0], hat_one, inverse_one)
    grad_tokens = (grad_mid_slots + grad_in_norm) * own_valid

    vector_total = lax.dynamic_slice_in_dim(
        vector_block.reshape(-1), seq_index * vector_count, vector_count
    )
    updated = iterate(
        is_square, update_scale.reshape(1), first_gram, direction, top, rest, slab, vector_block
    )

    first_new = beta_first * vector_moments[0] + (1.0 - beta_first) * vector_total
    second_new = beta_second * vector_moments[1] + (1.0 - beta_second) * vector_total * vector_total
    first_fix = 1.0 - beta_first**STEP
    second_fix = 1.0 - beta_second**STEP
    vector_new = vectors - vector_rate * (first_new / first_fix) / (
        jnp.sqrt(second_new / second_fix) + adam_eps
    )
    return (
        block_out[None],
        grad_tokens[None],
        jnp.transpose(first_moment, (2, 1, 0))[None],
        jnp.transpose(updated, (2, 1, 0))[None],
        first_new,
        second_new,
        vector_new,
    )


def solution(mesh):
    in_specs = (
        P("dp", "seq", None),
        P("dp", "seq", None),
        P("dp", None),
        P(),
        P("dp", None, "seq", None),
        P("dp", None, "seq", None),
        P("seq"),
        P(None, "seq"),
    )
    out_specs = (
        P("dp", "seq", None),
        P("dp", "seq", None),
        P("dp", None, "seq", None),
        P("dp", None, "seq", None),
        P("seq"),
        P("seq"),
        P("seq"),
    )
    return jax.shard_map(local, mesh=mesh, in_specs=in_specs, out_specs=out_specs, check_vma=False)
```

```python
import functools
import math

import jax
import jax.numpy as jnp
from jax import lax
from jax.experimental import pallas as pl
from jax.experimental.pallas import tpu as pltpu
from jax.sharding import PartitionSpec as P

HEADS = 16
FF = 4304
LEN = 729
NS_ITERS = 5
STEP = 10

norm_eps = 1e-06
coef_a = 3.4445
coef_b = -4.775
coef_c = 2.0315
momentum_decay = 0.95
matrix_rate = 0.15
matrix_decay = 0.1
beta_first = 0.9
beta_second = 0.999
vector_rate = 0.5
adam_eps = 1e-08
low = jnp.bfloat16
f32 = jnp.float32


def call(body, name, **kw):
    vmem = kw.pop("vmem", 48)
    return pl.pallas_call(
        body,
        name=name,
        compiler_params=pltpu.CompilerParams(vmem_limit_bytes=vmem * 1024 * 1024),
        **kw,
    )


def dot(left, right, contract):
    return lax.dot_general(
        left, right, ((tuple(contract[:1]), tuple(contract[1:])), ((), ())), preferred_element_type=f32
    )


def split(x):
    top = x.astype(low)
    return top, (x - top.astype(f32)).astype(low)


def prep_square_body(slab_ref, first_ref, out_ref):
    rows = slab_ref[:, 0, :]
    extra = out_ref.shape[0] - rows.shape[0]
    padded = jnp.concatenate([rows, jnp.zeros((extra, rows.shape[1]), f32)], axis=0)
    out_ref[...] = padded.astype(low)


def prep_square(slab, first, heads, head_size, head_pad):
    width = slab.shape[2]
    return call(
        prep_square_body,
        "prep_square",
        grid=(heads,),
        in_specs=[
            pl.BlockSpec((head_size, 1, width), lambda i: (i, 0, 0)),
            pl.BlockSpec(memory_space=pl.ANY),
        ],
        out_specs=pl.BlockSpec((head_pad, width), lambda i: (i, 0)),
        out_shape=jax.ShapeDtypeStruct((heads * head_pad, width), low),
    )(slab, first)


def prep_wide_body(total, slab_ref, out_ref):
    rows = slab_ref[:, 0, :]
    at = pl.program_id(0) * rows.shape[0] + lax.broadcasted_iota(jnp.int32, rows.shape, 0)
    out_ref[...] = jnp.where(at < total, rows, 0.0).astype(low)


def prep_wide(slab, rows_pad):
    total, _, width = slab.shape
    block = rows_pad // 4
    return call(
        functools.partial(prep_wide_body, total),
        "prep_wide",
        grid=(4,),
        in_specs=[pl.BlockSpec((block, 1, width), lambda i: (i, 0, 0))],
        out_specs=pl.BlockSpec((block, width), lambda i: (i, 0)),
        out_shape=jax.ShapeDtypeStruct((rows_pad, width), low),
    )(slab)


def momentum_body(total, moment_ref, grad_ref, first_ref, top_ref, rest_ref):
    grad = grad_ref[...].astype(f32)
    first = momentum_decay * moment_ref[:, 0, :] + grad
    first_ref[...] = first.reshape(first_ref.shape)
    at = pl.program_id(0) * grad.shape[0] + lax.broadcasted_iota(jnp.int32, grad.shape, 0)
    top, rest = split(jnp.where(at < total, grad + momentum_decay * first, 0.0))
    top_ref[...] = top
    rest_ref[...] = rest


def momentum(moments, grad):
    total, _, width = moments.shape
    rows_pad = grad.shape[0]
    block = rows_pad // 4
    slab_spec = pl.BlockSpec((block, 1, width), lambda i: (i, 0, 0))
    flat_spec = pl.BlockSpec((block, width), lambda i: (i, 0))
    return call(
        functools.partial(momentum_body, total),
        "momentum",
        grid=(4,),
        in_specs=[slab_spec, flat_spec],
        out_specs=[slab_spec, flat_spec, flat_spec],
        out_shape=[
            jax.ShapeDtypeStruct(moments.shape, f32),
            jax.ShapeDtypeStruct((rows_pad, width), low),
            jax.ShapeDtypeStruct((rows_pad, width), low),
        ],
    )(moments, grad)


def momentum_again_body(total, moment_ref, grad_ref, *refs):
    momentum_body(total, moment_ref, grad_ref, *refs[-3:])


def momentum_again(moments, grad, first, top, rest, *others):
    total, _, width = moments.shape
    rows = grad.shape[0]
    slab_spec = pl.BlockSpec((rows, 1, width), lambda i: (i, 0, 0))
    flat_spec = pl.BlockSpec((rows, width), lambda i: (i, 0))
    return call(
        functools.partial(momentum_again_body, total),
        "momentum_again",
        grid=(1,),
        in_specs=[slab_spec, flat_spec] + [pl.BlockSpec(memory_space=pl.ANY)] * (3 + len(others)),
        out_specs=[slab_spec, flat_spec, flat_spec],
        out_shape=[jax.ShapeDtypeStruct(x.shape, x.dtype) for x in (first, top, rest)],
        input_output_aliases={2: 0, 3: 1, 4: 2},
    )(moments, grad, first, top, rest, *others)


def packed_at(column):
    return 128 * (column * (column + 1) // 2)


def upper(width):
    for j in range(0, width, 256):
        for i in range(0, min(j + 256, width), 256):
            yield i, j, pl.ds(i, min(256, width - i)), pl.ds(j, min(256, width - j))


def gram_body(top_ref, rest_ref, out_ref):
    for i, j, rows, columns in upper(top_ref.shape[1]):
        value = (
            dot(top_ref[:, rows], top_ref[:, columns], (0, 0))
            + dot(top_ref[:, rows], rest_ref[:, columns], (0, 0))
            + dot(rest_ref[:, rows], top_ref[:, columns], (0, 0))
        )
        for c in range(j // 128, (j + value.shape[1]) // 128):
            used = min(value.shape[0], 128 * (c + 1) - i)
            lanes = 128 * c - j
            out_ref[pl.ds(packed_at(c) + i, used), :] = value[:used, lanes : lanes + 128]


def gram_of(top, rest):
    count = top.shape[1] // 128
    return call(
        gram_body,
        "gram",
        in_specs=[pl.BlockSpec(memory_space=pltpu.VMEM)] * 2,
        out_specs=pl.BlockSpec(memory_space=pltpu.VMEM),
        out_shape=jax.ShapeDtypeStruct((packed_at(count), 128), f32),
    )(top, rest)


class Iterate:
    def __init__(self, a_top, a_rest, b_top, t_top, t_rest, x_ref):
        self.a = a_top, a_rest
        self.b = b_top
        self.t = t_top, t_rest
        self.x = x_ref
        self.width = a_top.shape[0]
        self.step = x_ref.shape[0] // 4
        self.diagonal = lax.broadcasted_iota(jnp.int32, (128, 128), 0) == lax.broadcasted_iota(
            jnp.int32, (128, 128), 1
        )

    def put(self, i, j, value):
        tall, wide = value.shape
        for x, rows, columns in ((value, pl.ds(i, tall), pl.ds(j, wide)),) + (
            ((value.T, pl.ds(j, wide), pl.ds(i, tall)),) if i != j else ()
        ):
            top, rest = split(x)
            self.a[0][rows, columns] = top
            self.a[1][rows, columns] = rest

    def both(self, pair, rows, columns):
        return pair[0][rows, columns].astype(f32) + pair[1][rows, columns].astype(f32)

    def symmetric(self, left, rights, finish):
        for i, j, rows, columns in upper(self.width):
            value = dot(left[rows, :], rights[0][:, columns], (1, 0))
            for right in rights[1:]:
                value = value + dot(left[rows, :], right[:, columns], (1, 0))
            finish(i, j, rows, columns, value)

    def recenter(self, center):
        total = jnp.zeros((128, 128), f32)
        for c in range(0, self.width, 128):
            at = pl.ds(c, 128)
            total = total + jnp.where(self.diagonal, self.both(self.a, at, at), 0.0)
        mean = jnp.sum(total) / self.width
        for c in range(0, self.width, 128):
            at = pl.ds(c, 128)
            top, rest = split(self.both(self.a, at, at) - jnp.where(self.diagonal, mean, 0.0))
            self.a[0][at, at] = top
            self.a[1][at, at] = rest
        return center + mean

    def mix(self, center):
        def finish(i, j, rows, columns, value):
            value = (coef_b + 2.0 * coef_c * center) * self.both(
                self.a, rows, columns
            ) + coef_c * value
            self.b[rows, columns] = value.astype(low)
            if i != j:
                self.b[columns, rows] = value.T.astype(low)

        self.symmetric(self.a[0], (self.a[0],), finish)
        return coef_a + coef_b * center + coef_c * center * center

    def stepped(self, rows, lead):
        x = self.x[rows, :]
        return lead * x + dot(x.astype(low), self.b[...], (1, 0))

    def propagate(self, center, lead, passes):
        tall = self.width // 3

        @pl.loop(0, 3)
        def _(r):
            rows = pl.ds(r * tall, tall)
            value = lead * self.both(self.a, rows, slice(None)) + center * self.b[rows, :].astype(f32)
            for left in self.a[:passes]:
                value = value + dot(left[rows, :], self.b[...], (1, 0))
            top, rest = split(value)
            self.t[0][rows, :] = top
            self.t[1][rows, :] = rest

        def finish(i, j, rows, columns, value):
            carried = lead * self.both(self.t, rows, columns)
            carried = carried + lead * center * self.b[rows, columns].astype(f32)
            self.put(i, j, carried + value)

        self.symmetric(self.b, self.t[:passes], finish)
        return lead * lead * center

    def sweep(self, center, passes=2):
        center = self.recenter(center)
        lead = self.mix(center)

        @pl.loop(0, 4)
        def _(r):
            rows = pl.ds(r * self.step, self.step)
            self.x[rows, :] = self.stepped(rows, lead)

        return self.propagate(center, lead, passes)


def iterate_body(
    total,
    square_ref,
    rate_ref,
    gram_ref,
    full_hbm,
    top_hbm,
    rest_hbm,
    slab_hbm,
    first_ref,
    out_hbm,
    a_top,
    a_rest,
    b_top,
    t_top,
    t_rest,
    x_ref,
    slab_ref,
    sem,
):
    state = Iterate(a_top, a_rest, b_top, t_top, t_rest, x_ref)
    width, step = state.width, state.step
    rows_pad = x_ref.shape[0]
    fetch_full = pltpu.make_async_copy(full_hbm, t_rest, sem.at[0])
    fetch_top = pltpu.make_async_copy(top_hbm, b_top.at[pl.ds(0, rows_pad)], sem.at[1])
    fetch_rest = pltpu.make_async_copy(rest_hbm, t_top.at[pl.ds(0, rows_pad)], sem.at[2])
    fetch_slab = pltpu.make_async_copy(slab_hbm, slab_ref.at[pl.ds(0, total)], sem.at[3])
    for fetch in (fetch_full, fetch_top, fetch_rest, fetch_slab):
        fetch.start()
    is_square = square_ref[0] == 1
    trace = jnp.zeros((128, 128), f32)
    for c in range(width // 128):
        block = gram_ref[pl.ds(packed_at(c) + 128 * c, 128), :]
        trace = trace + jnp.where(state.diagonal, block, 0.0)
    fetch_full.wait()

    def add_squares(r, sums):
        part = t_rest[pl.ds(r * 128, 128), :].astype(f32)
        return sums + jnp.sum(part * part, axis=0, keepdims=True)

    squares = lax.fori_loop(0, width // 128, add_squares, jnp.zeros((1, width), f32))
    norm = jnp.sqrt(jnp.where(is_square, jnp.sum(squares), jnp.sum(trace)))
    scaling = 1.0 / (norm + 1e-07)
    scale_two = scaling * scaling

    @pl.when(is_square)
    def _():
        for i, j, rows, columns in upper(width):
            state.put(i, j, dot(t_rest[:, rows], t_rest[:, columns], (0, 0)) * scale_two)

    @pl.when(jnp.logical_not(is_square))
    def _():
        for c in range(width // 128):
            for r in range(c + 1):
                block = gram_ref[pl.ds(packed_at(c) + 128 * r, 128), :]
                state.put(128 * r, 128 * c, block * scale_two)

    fetch_top.wait()
    fetch_rest.wait()
    rest_scaling = jnp.where(is_square, 0.0, scaling)

    @pl.loop(0, 4)
    def _(r):
        rows = pl.ds(r * step, step)
        x_ref[rows, :] = b_top[rows, :].astype(f32) * scaling + t_top[rows, :].astype(f32) * rest_scaling

    center = lax.fori_loop(
        0, NS_ITERS - 2, lambda _, center: state.sweep(center), jnp.float32(0.0)
    )
    center = state.sweep(center, 1)
    lead = state.mix(state.recenter(center))
    fetch_slab.wait()
    rate = rate_ref[0]

    @pl.loop(0, 4)
    def _(r):
        rows = pl.ds(r * step, step)
        new = slab_ref[rows, 0, :] * (1.0 - matrix_rate * matrix_decay) - rate * state.stepped(rows, lead)
        slab_ref[rows, :, :] = new.reshape(step, 1, width)

    leave = pltpu.make_async_copy(slab_ref.at[pl.ds(0, total)], out_hbm, sem.at[0])
    leave.start()
    leave.wait()


def iterate(square, rate, gram, full, top, rest, slab, first):
    total, _, width = slab.shape
    rows_pad = top.shape[0]
    vmem, smem = pl.BlockSpec(memory_space=pltpu.VMEM), pl.BlockSpec(memory_space=pltpu.SMEM)
    far = pl.BlockSpec(memory_space=pl.ANY)
    return call(
        functools.partial(iterate_body, total),
        "iterate",
        vmem=56,
        in_specs=[smem, smem, vmem] + [far] * 5,
        out_specs=far,
        out_shape=jax.ShapeDtypeStruct(slab.shape, f32),
        scratch_shapes=[pltpu.VMEM((width, width), low)] * 5
        + [
            pltpu.VMEM((rows_pad, width), f32),
            pltpu.VMEM((rows_pad, 1, width), f32),
            pltpu.SemaphoreType.DMA((4,)),
        ],
        cost_estimate=pl.CostEstimate(
            flops=80_000_000_000, bytes_accessed=20_000_000, transcendentals=0
        ),
    )(square, rate, gram, full, top, rest, slab, first)


def attend_body(scale, qkv_ref, context_ref, soft_ref):
    query, key, value = qkv_ref[0, 0], qkv_ref[1, 0], qkv_ref[2, 0]
    scores = dot(key, query, (0, 0)) * scale
    at = lax.broadcasted_iota(jnp.int32, scores.shape, 0)
    scores = jnp.where(at < LEN, scores, -1e30)
    exponent = jnp.exp(scores - jnp.max(scores, axis=0, keepdims=True))
    soft = (exponent / jnp.sum(exponent, axis=0, keepdims=True)).astype(low)
    soft_ref[0] = soft
    context = dot(value, soft, (1, 0))
    context_ref[0] = context[: context_ref.shape[1]].astype(low)


def attend(qkv, head_size, scale):
    _, groups, head_pad, rows = qkv.shape
    return call(
        functools.partial(attend_body, scale),
        "attend",
        grid=(groups,),
        in_specs=[pl.BlockSpec((3, 1, head_pad, rows), lambda h: (0, h, 0, 0))],
        out_specs=[
            pl.BlockSpec((1, head_size, rows), lambda h: (h, 0, 0)),
            pl.BlockSpec((1, rows, rows), lambda h: (h, 0, 0)),
        ],
        out_shape=[
            jax.ShapeDtypeStruct((groups, head_size, rows), low),
            jax.ShapeDtypeStruct((groups, rows, rows), low),
        ],
    )(qkv)


def attend_back_body(scale, qkv_ref, soft_ref, grad_ref, first_ref, other_ref, out_ref):
    query, key, value = qkv_ref[0, 0], qkv_ref[1, 0], qkv_ref[2, 0]
    grad, soft = grad_ref[0], soft_ref[0]
    grad_soft = dot(value, grad, (0, 0))
    soft_f32 = soft.astype(f32)
    along = jnp.sum(soft_f32 * grad_soft, axis=0, keepdims=True)
    grad_scores = (soft_f32 * (grad_soft - along)).astype(low)
    out_ref[0, 0] = (dot(key, grad_scores, (1, 0)) * scale).astype(low)
    out_ref[1, 0] = (dot(query, grad_scores, (1, 1)) * scale).astype(low)
    out_ref[2, 0] = dot(grad, soft, (1, 1)).astype(low)


def attend_back(qkv, soft, grad, first, other, scale):
    _, groups, head_pad, rows = qkv.shape
    three = pl.BlockSpec((3, 1, head_pad, rows), lambda h: (0, h, 0, 0))
    return call(
        functools.partial(attend_back_body, scale),
        "attend_back",
        grid=(groups,),
        in_specs=[
            three,
            pl.BlockSpec((1, rows, rows), lambda h: (h, 0, 0)),
            pl.BlockSpec((1, head_pad, rows), lambda h: (h, 0, 0)),
            pl.BlockSpec(memory_space=pl.ANY),
            pl.BlockSpec(memory_space=pl.ANY),
        ],
        out_specs=three,
        out_shape=jax.ShapeDtypeStruct(qkv.shape, low),
    )(qkv, soft, grad, first, other)


def whiten(inputs):
    average = jnp.mean(inputs, axis=-1, keepdims=True)
    centered = inputs - average
    variance = jnp.mean(centered * centered, axis=-1, keepdims=True)
    inverse = lax.rsqrt(variance + norm_eps)
    return centered * inverse, inverse


def whiten_back(grad, gain_row, hat, inverse):
    scaled = grad * gain_row
    mean_one = jnp.mean(scaled, axis=-1, keepdims=True)
    mean_two = jnp.mean(scaled * hat, axis=-1, keepdims=True)
    return inverse * (scaled - mean_one - hat * mean_two)


def gelu_both(inputs):
    squared = inputs * inputs
    curve = jnp.tanh(0.7978845608028654 * (inputs + 0.044715 * inputs * squared))
    value = 0.5 * inputs * (1.0 + curve)
    slope = 0.5 * (1.0 + curve) + 0.5 * inputs * (1.0 - curve * curve) * 0.7978845608028654 * (
        1.0 + 3.0 * 0.044715 * squared
    )
    return value, slope


def product(form, left, right):
    return jnp.einsum(form, left, right, preferred_element_type=f32)


def flip(x, axis, mask):
    count = lax.axis_size(axis)
    return lax.ppermute(x, axis, [(i, i ^ mask) for i in range(count)])


def gather_chunks(piece, first):
    count = lax.axis_size("dp")
    half = count // 2
    me = lax.axis_index("dp")
    pair, core = me >> 1, me & 1
    whole = jnp.zeros((half, 2) + piece.shape, piece.dtype)
    for mask, part in enumerate(exchange(piece, first)):
        whole = lax.dynamic_update_slice(whole, part[None, None], (pair ^ mask, core, 0, 0))
    mine = lax.dynamic_slice_in_dim(whole, core, 1, 1)
    other = flip(mine, "dp", 1)
    whole = lax.dynamic_update_slice_in_dim(whole, other, 1 - core, 1)
    return whole.reshape((count,) + piece.shape)


def scatter_sum(whole, order):
    count, rows, columns = whole.shape
    bits = count.bit_length() - 1
    me = lax.axis_index("dp")
    whole = whole.reshape((2,) * bits + (rows, columns))
    for bit in order:
        at = bits - 1 - bit
        mine = (me >> bit) & 1
        kept = lax.dynamic_slice_in_dim(whole, mine, 1, at)
        sent = lax.dynamic_slice_in_dim(whole, 1 - mine, 1, at)
        got = flip(sent, "dp", 1 << bit)
        whole = (kept.astype(f32) + got.astype(f32)).astype(low)
    return whole.reshape(rows, columns)


def arrivals(piece):
    count = lax.axis_size("seq")
    return [
        lax.ppermute(piece, "seq", [(i, (i + shift) % count) for i in range(count)])
        for shift in range(1, count)
    ]


def gather_seq(piece):
    count = lax.axis_size("seq")
    me = lax.axis_index("seq")
    whole = jnp.zeros((count,) + piece.shape, piece.dtype)
    for shift, part in enumerate([piece] + arrivals(piece)):
        whole = lax.dynamic_update_slice_in_dim(whole, part[None], (me - shift) % count, 0)
    return whole


def total_sum(x):
    for axis in ("dp", "seq"):
        step = 1
        while step < lax.axis_size(axis):
            x = x + flip(x, axis, step)
            step *= 2
    return x


def zero_of(token):
    return jnp.minimum(jnp.abs(token), 0.0)


def after(x, token):
    return x + zero_of(token).astype(x.dtype)


def touch_body(*refs):
    pass


def touch(arrays, *others):
    far = pl.BlockSpec(memory_space=pl.ANY)
    count = len(arrays)
    return call(
        touch_body,
        "touch",
        in_specs=[far] * (count + len(others)),
        out_specs=[far] * count,
        out_shape=[jax.ShapeDtypeStruct(x.shape, x.dtype) for x in arrays],
        input_output_aliases={i: i for i in range(count)},
    )(*arrays, *others)


def relative(me, count):
    place = jnp.arange(count)
    half = count // 2
    return me ^ ((place % half) * 2 + place // half)


def exchange(piece, first=None):
    half = lax.axis_size("dp") // 2
    arrived = [flip(piece, "dp", mask << 1) for mask in range(1, half)]
    return [piece] + ([after(x, first) for x in arrived] if first is not None else arrived)


def gather_relative(pieces, first=None):
    arrived = exchange(jnp.concatenate(pieces, axis=0), first)
    result, at = [], 0
    for piece in pieces:
        rows = piece.shape[0]
        mine = jnp.concatenate([x[at : at + rows] for x in arrived], axis=0)
        result.append(jnp.concatenate([mine, flip(mine, "dp", 1)], axis=0))
        at += rows
    return result


def scatter_relative(whole, order):
    count = lax.axis_size("dp")
    bits = count.bit_length() - 1
    rows, columns = whole.shape[0] // count, whole.shape[1]
    whole = whole.reshape((2,) * bits + (rows, columns))
    for bit in order:
        at = 0 if bit == 0 else bits - bit
        kept = lax.slice_in_dim(whole, 0, 1, axis=at)
        got = flip(lax.slice_in_dim(whole, 1, 2, axis=at), "dp", 1 << bit)
        whole = (kept.astype(f32) + got.astype(f32)).astype(low)
    return whole.reshape(rows, columns)


def local(
    tokens, cotangent, counts, owner_table, owned_weights, owned_moments, vectors, vector_moments
):
    seq_count = lax.axis_size("seq")
    dp_count = lax.axis_size("dp")
    bits = dp_count.bit_length() - 1
    seq_index = lax.axis_index("seq")
    dp_index = lax.axis_index("dp")
    capacity = tokens.shape[1]
    width = tokens.shape[2]
    slots = capacity * seq_count
    head_size = width // HEADS
    head_pad = -(-head_size // 16) * 16
    heads = HEADS // seq_count
    score_scale = 1.0 / math.sqrt(head_size)
    widths = (width, width, width, width, FF, FF)
    cols = width // seq_count
    ff_cols = FF // seq_count
    share = -(-LEN // (16 * seq_count)) * 16
    packed = share * seq_count
    square_rows = heads * head_pad
    square_chunk = -(-square_rows // (8 * dp_count)) * 8
    square_total = square_chunk * dp_count
    wide_chunk = -(-ff_cols // (8 * dp_count)) * 8
    wide_rows = wide_chunk * dp_count
    orders = (tuple(range(bits)), (0,) + tuple(range(bits - 1, 0, -1)))

    rows_in = tokens[0]
    vector_count = vectors.shape[0]
    vector_rows = -(-vector_count // width)
    extra = -(-vector_rows // 16) * 16
    payload = jnp.pad(vectors, (0, extra * width - vector_count)).reshape(extra, width)
    own_ids = jnp.arange(capacity)[:, None]
    own_valid = (own_ids < lax.dynamic_index_in_dim(counts[0], seq_index, 0)).astype(f32)
    cot_own = (cotangent[0] * own_valid).astype(low)
    payload = jnp.concatenate([rows_in.astype(low), payload.astype(low), cot_own], axis=0)
    gathered = lax.all_gather(payload, "seq", axis=0, tiled=False)

    counts_row = counts[0]
    starts = jnp.cumsum(counts_row) - counts_row

    def rows_of(per, skip=0):
        ids = jnp.arange(per * seq_count) % per - skip
        real = (ids >= 0) & (ids < jnp.repeat(counts_row, per))
        return jnp.where(real, jnp.repeat(starts, per) + ids, packed)

    def picks(row):
        return (jnp.arange(packed)[:, None] == row[None, :]).astype(low)

    slot_row = rows_of(capacity)
    token_pick = picks(rows_of(payload.shape[0]))
    cot_pick = picks(rows_of(payload.shape[0], capacity + extra))
    own_row = lax.dynamic_slice_in_dim(slot_row, seq_index * capacity, capacity)
    own_pick = picks(own_row)
    slab = jnp.transpose(owned_weights[0], (2, 1, 0))
    moments = jnp.transpose(owned_moments[0], (2, 1, 0))

    def send(x):
        return lax.all_to_all(x, "dp", split_axis=0, concat_axis=0, tiled=True)

    square_own = prep_square(slab, payload, heads, head_size, head_pad)
    near = jnp.stack(exchange(square_own))
    far = flip(near, "dp", 1)
    squares = []
    for m in range(4):
        away = owner_table[m] ^ dp_index
        from_near = lax.dynamic_index_in_dim(near, away >> 1, 0, keepdims=False)
        from_far = lax.dynamic_index_in_dim(far, away >> 1, 0, keepdims=False)
        squares.append(jnp.where((away & 1) == 0, from_near, from_far))
    w_qkv = jnp.concatenate(squares[:3], axis=0)
    w_out_piece = jnp.pad(squares[3], ((0, square_total - square_rows), (0, 0)))
    w_out_piece = lax.dynamic_slice_in_dim(w_out_piece, dp_index * square_chunk, square_chunk)
    w_out_part = gather_seq(w_out_piece).reshape(seq_count * square_chunk, width)
    wide_sent = prep_wide(slab, wide_rows).reshape(dp_count, wide_chunk, width)
    got_wide = send(wide_sent)
    wide_pieces = [lax.dynamic_index_in_dim(got_wide, owner_table[m], 0, keepdims=False) for m in (4, 5)]

    w_up, w_down = gather_relative(wide_pieces)
    (gathered,) = touch([gathered], w_up, w_down, w_out_part)
    gathered_rows = gathered.reshape(seq_count * payload.shape[0], width)
    grad_rows = product("rc,cd->rd", cot_pick, gathered_rows).astype(low)

    vector_full = gathered[:, capacity : capacity + vector_rows].reshape(seq_count, -1)
    vector_full = vector_full[:, :vector_count].reshape(-1).astype(f32)
    row_params = vector_full[: 8 * width].reshape(8, width)
    up_bias = lax.dynamic_slice_in_dim(vector_full, 8 * width + seq_index * ff_cols, ff_cols)
    up_bias = jnp.pad(up_bias, (0, wide_rows - ff_cols)).reshape(dp_count, wide_chunk)
    up_bias = jnp.take(up_bias, relative(dp_index, dp_count), axis=0).reshape(wide_rows)

    def head_bias(row):
        own = lax.dynamic_slice_in_dim(row, seq_index * cols, cols).reshape(heads, head_size)
        return jnp.pad(own, ((0, 0), (0, head_pad - head_size))).reshape(square_rows)

    qkv_bias = jnp.concatenate(
        [head_bias(row_params[2]), jnp.zeros((square_rows,), f32), head_bias(row_params[3])]
    )

    token_rows = product("rc,cd->rd", token_pick, gathered_rows)
    hat_packed = whiten(token_rows)[0]
    normed = (hat_packed * row_params[0] + row_params[1]).astype(low)
    qkv_bias = after(qkv_bias, grad_rows[0, 0])
    qkv = (product("ed,rd->er", w_qkv, normed) + qkv_bias[:, None]).astype(low)
    qkv = qkv.reshape(3, heads, head_pad, packed)
    context_own, soft = attend(qkv, head_size, score_scale)
    token = context_own[0, 0, 0]
    w_out = gather_chunks(w_out_part, token)
    w_out = w_out.reshape(dp_count, seq_count, square_chunk, width).transpose(1, 0, 2, 3)
    w_out = w_out.reshape(seq_count, square_total, width)[:, :square_rows]
    w_out = w_out.reshape(seq_count * heads, head_pad, width)[:, :head_size].reshape(width, width)
    w_out_own = lax.dynamic_slice_in_dim(w_out, seq_index * cols, cols, axis=1)
    w_out_own = jnp.pad(
        w_out_own.reshape(width, heads, head_size), ((0, 0), (0, 0), (0, head_pad - head_size))
    ).reshape(width, square_rows)
    context = lax.all_gather(context_own.reshape(cols, packed), "seq", axis=0, tiled=True)
    middle = token_rows + product("er,oe->ro", context, w_out) + row_params[4]
    hat_two, inverse_two = whiten(middle)
    normed_two = (hat_two * row_params[5] + row_params[6]).astype(low)
    pre_act = product("rd,fd->rf", normed_two, w_up) + up_bias
    hidden_f32, slope = gelu_both(pre_act)
    hidden = hidden_f32.astype(low)

    grad_hidden = product("rd,fd->rf", grad_rows, w_down)
    grad_pre = (slope * grad_hidden).astype(low)
    grad_down = product("rf,rd->fd", hidden, grad_rows).astype(low)
    grad_up = product("rf,rd->fd", grad_pre, normed_two).astype(low)
    grad_normed_two_part = (
        product("rf,fd->rd", grad_pre, w_up) + zero_of(grad_down[0, 0] + grad_up[0, 0]).astype(f32)
    ).astype(low)
    grad_up_bias = jnp.sum(grad_pre.astype(f32), axis=0).reshape(dp_count, wide_chunk)
    back = jnp.arange(dp_count) ^ dp_index
    grad_up_bias = jnp.take(grad_up_bias, (back & 1) * (dp_count // 2) + (back >> 1), axis=0)
    grad_up_bias = grad_up_bias.reshape(wide_rows)[:ff_cols]

    sum_down = scatter_relative(grad_down, orders[0])
    sum_up = scatter_relative(grad_up, orders[1])
    def to_owner(pairs):
        total = 0
        for piece, m in pairs:
            here = (jnp.arange(dp_count) == owner_table[m])[:, None, None]
            total = total + jnp.where(here, piece[None], jnp.zeros((), low))
        return total

    wide_back = to_owner([(sum_up, 4), (sum_down, 5)])
    grad_normed_two = after(
        lax.psum_scatter(grad_normed_two_part, "seq", scatter_dimension=0, tiled=True),
        wide_back[0, 0, 0],
    ).astype(f32)

    def own_share(x):
        return lax.dynamic_slice_in_dim(x, seq_index * share, share)

    own_grad = own_share(grad_rows).astype(f32)
    own_hat = own_share(hat_two)
    grad_bias_down = jnp.sum(own_grad, axis=0)
    grad_gain_two = jnp.sum(grad_normed_two * own_hat, axis=0)
    grad_shift_two = jnp.sum(grad_normed_two, axis=0)
    grad_mid_norm = whiten_back(grad_normed_two, row_params[5], own_hat, own_share(inverse_two))
    grad_attn_own = (own_grad + grad_mid_norm).astype(low)
    grad_bias_out = jnp.sum(grad_attn_own.astype(f32), axis=0)
    grad_attn = lax.all_gather(grad_attn_own, "seq", axis=0, tiled=True)
    (wide_back,) = touch([wide_back], grad_attn_own)
    back_wide = send(wide_back).reshape(wide_rows, width)
    unpick = (slot_row[:, None] == jnp.arange(packed)[None, :]).astype(low)
    placed_middle = jnp.where(
        (jnp.arange(packed) // share == seq_index)[:, None], middle + row_params[7], 0.0
    )
    out_part = (
        product("rf,fd->rd", hidden, w_down) + placed_middle + zero_of(grad_attn_own[0, 0]).astype(f32)
    ).astype(low)
    out_slots = product("cr,rd->cd", unpick, out_part).astype(low)
    first_moment, top, rest = momentum(moments, back_wide)
    wide_gram = gram_of(top, rest)
    gram_parts = send(wide_gram.reshape(dp_count, -1, 128))
    gram_two = jnp.concatenate(
        [lax.dynamic_index_in_dim(gram_parts, owner_table[m], 0, keepdims=False) for m in (4, 5)],
        axis=0,
    )


    grad_context = product("de,rd->er", w_out_own, grad_attn).astype(low)
    grad_qkv = attend_back(qkv, soft, grad_context.reshape(heads, head_pad, packed), wide_gram, out_slots, score_scale)
    (gram_two,) = touch([gram_two], grad_qkv)
    gram_sums = lax.psum(gram_two, "seq")
    grad_qkv_flat = grad_qkv.reshape(3 * square_rows, packed)
    grad_attn_cols = lax.dynamic_slice_in_dim(grad_attn, seq_index * cols, cols, axis=1)
    grad_w_out = product("rd,er->de", grad_attn_cols, context)
    grad_w_qkv = product("er,rd->ed", grad_qkv_flat, normed)
    grad_qkv_bias = jnp.sum(grad_qkv.astype(f32), axis=3)[:, :, :head_size].reshape(3, cols)

    grad_normed_part = product("er,ed->rd", grad_qkv_flat, w_qkv)
    grad_gain_one = jnp.sum(grad_normed_part * hat_packed, axis=0)
    grad_shift_one = jnp.sum(grad_normed_part, axis=0)
    grad_normed_slots = product("cr,rd->cd", unpick, grad_normed_part.astype(low)).astype(low)

    grad_mid_slots = product("rc,rd->cd", own_pick, grad_attn)

    def square_parts(x):
        x = jnp.pad(x.astype(low), ((0, square_total - square_rows), (0, 0)))
        return x.reshape(dp_count, square_chunk, width)

    late = [square_parts(grad_w_qkv[m * square_rows : (m + 1) * square_rows]) for m in range(3)]
    grad_w_out = jnp.pad(
        grad_w_out.reshape(heads, head_size, width), ((0, 0), (0, head_pad - head_size), (0, 0))
    )
    late.append(square_parts(grad_w_out.reshape(square_rows, width)))
    token = gram_two[0, 0].astype(low)
    sum_qk = scatter_sum(after(jnp.concatenate(late[:2], axis=1), token), orders[0])
    sum_vo = scatter_sum(jnp.concatenate(late[2:], axis=1), orders[1])
    square_back = to_owner(
        [
            (sum_qk[:square_chunk], 0),
            (sum_qk[square_chunk:], 1),
            (sum_vo[:square_chunk], 2),
            (sum_vo[square_chunk:], 3),
        ]
    )
    def spot(piece):
        return lax.dynamic_update_slice_in_dim(
            jnp.zeros((piece.shape[0] * seq_count,), f32), piece, seq_index * piece.shape[0], 0
        )

    vector_grad = jnp.concatenate(
        [
            grad_gain_one,
            grad_shift_one,
            spot(grad_qkv_bias[0]),
            spot(grad_qkv_bias[2]),
            grad_bias_out,
            grad_gain_two,
            grad_shift_two,
            grad_bias_down,
            spot(grad_up_bias),
        ]
    )
    padded = -(-vector_grad.shape[0] // 1024) * 1024
    vector_grad = jnp.pad(vector_grad, (0, padded - vector_grad.shape[0])).reshape(-1, 128)
    vector_block = total_sum(vector_grad)
    back_square = send(after(square_back, gram_sums[0, 0] + vector_block[0, 0])).reshape(square_total, width)[:square_rows]
    back_square = back_square.reshape(heads, head_pad, width)[:, :head_size].reshape(cols, width)
    first_moment, top, rest = momentum_again(
        moments, back_wide[:cols] + back_square, first_moment, top, rest, grad_normed_slots, grad_mid_slots
    )
    direction = lax.all_gather(top[:cols], "seq", axis=0, tiled=True)
    chunk_rows = gram_sums.shape[0] // 2
    (gram_sums,) = touch([gram_sums], vector_block)
    gram_back = jnp.zeros((), f32)
    for k, m in enumerate((4, 5)):
        here = (jnp.arange(dp_count) == owner_table[m])[:, None, None]
        gram_back = gram_back + jnp.where(here, gram_sums[k * chunk_rows : (k + 1) * chunk_rows][None], 0.0)
    first_gram = send(gram_back).reshape(wide_gram.shape)
    is_square = jnp.any(owner_table[:4] == dp_index).astype(jnp.int32).reshape(1)
    grad_normed_slots, out_slots = touch([grad_normed_slots, out_slots], direction, first_gram)
    update_scale = jnp.zeros((), f32)
    for m in range(6):
        update_scale = jnp.where(
            owner_table[m] == dp_index,
            jnp.float32(matrix_rate * 0.2 * math.sqrt(max(width, widths[m]))),
            update_scale,
        )

    grad_normed = lax.psum_scatter(
        grad_normed_slots, "seq", scatter_dimension=0, tiled=True
    ).astype(f32)
    block_out = lax.psum_scatter(
        out_slots, "seq", scatter_dimension=0, tiled=True
    ).astype(f32)
    hat_one, inverse_one = whiten(rows_in)
    grad_in_norm = whiten_back(grad_normed, row_params[0], hat_one, inverse_one)
    grad_tokens = (grad_mid_slots + grad_in_norm) * own_valid

    vector_total = lax.dynamic_slice_in_dim(
        vector_block.reshape(-1), seq_index * vector_count, vector_count
    )
    updated = iterate(
        is_square, update_scale.reshape(1), first_gram, direction, top, rest, slab, vector_block
    )

    first_new = beta_first * vector_moments[0] + (1.0 - beta_first) * vector_total
    second_new = beta_second * vector_moments[1] + (1.0 - beta_second) * vector_total * vector_total
    first_fix = 1.0 - beta_first**STEP
    second_fix = 1.0 - beta_second**STEP
    vector_new = vectors - vector_rate * (first_new / first_fix) / (
        jnp.sqrt(second_new / second_fix) + adam_eps
    )
    return (
        block_out[None],
        grad_tokens[None],
        jnp.transpose(first_moment, (2, 1, 0))[None],
        jnp.transpose(updated, (2, 1, 0))[None],
        first_new,
        second_new,
        vector_new,
    )


def solution(mesh):
    in_specs = (
        P("dp", "seq", None),
        P("dp", "seq", None),
        P("dp", None),
        P(),
        P("dp", None, "seq", None),
        P("dp", None, "seq", None),
        P("seq"),
        P(None, "seq"),
    )
    out_specs = (
        P("dp", "seq", None),
        P("dp", "seq", None),
        P("dp", None, "seq", None),
        P("dp", None, "seq", None),
        P("seq"),
        P("seq"),
        P("seq"),
    )
    return jax.shard_map(local, mesh=mesh, in_specs=in_specs, out_specs=out_specs, check_vma=False)
```
